256 devices in a mesh: seq: 32 (over z, x), ch: 8 (over y, core).
Axes of the slice: x: 4, y: 4, z: 8, core: 2. Of those that a mesh axis runs over, the one named last changes fastest.
Arguments:
- grad_out: bfloat16 [16384, 4096], P('seq', 'ch'), may hold values from -6 to 6
- out_weight: bfloat16 [4096, 4096], P('seq', 'ch'), may hold values from -0.09375 to 0.09375
- gate_in: bfloat16 [4096, 16384], P('ch', 'seq'), may hold values from -6 to 6
- gate_out: bfloat16 [4096, 16384], P('ch', 'seq'), may hold values from -6 to 6
- values: bfloat16 [4096, 16384], P('ch', 'seq'), may hold values from -6 to 6
- conv_out: bfloat16 [4096, 16384], P('ch', 'seq'), may hold values from -6 to 6
- filters: float32 [4096, 16384], P('ch', 'seq'), may hold values from -1 to 1
- skip_scale: float32 [4096], P('ch'), may hold values from -4 to 4
Outputs:
- grad_gate_in: bfloat16 [4096, 16384], P('ch', 'seq')
- grad_values: bfloat16 [4096, 16384], P('ch', 'seq')
- grad_gate_out: bfloat16 [4096, 16384], P('ch', 'seq')
- grad_filters: float32 [4096, 16384], P('ch', 'seq')
The draws below stay inside these ranges and needn't reach their ends.
All inputs are finite; a program needn't handle non-finite values.
Results may differ from the reference program's by a relative error of at most 0.0057.
Values may be sent and summed in bfloat16 or wider, within the bound.
A program may use at most 128 MiB of HBM per device.

```python
import math
import jax
import jax.numpy as jnp
from jax import lax

D = 4096
SEQ = 16384


def draw_filters(key, part):
    key = jax.random.fold_in(key, 7)
    rate_key = jax.random.fold_in(key, 1)
    noise_key = jax.random.fold_in(key, 2)
    rates = jnp.exp(jax.random.uniform(rate_key, (D, 1), minval=math.log(0.5), maxval=math.log(8.0)))
    lags = jnp.arange(SEQ).astype(jnp.float32)[None, :] / SEQ
    envelope = jnp.exp(-rates * lags) * jnp.sqrt(2.0 * rates / SEQ)
    noise = jax.random.truncated_normal(noise_key, -4.0, 4.0, (D, SEQ))
    return (noise * envelope).astype(jnp.float32)


def level_of(stream_key, shape, split, low, top_value):
    def one(axis_at, blocks):
        draws = jax.random.uniform(jax.random.fold_in(jax.random.fold_in(stream_key, 6), axis_at), (blocks,), jnp.float32, low / len(split), top_value / len(split))
        return jnp.repeat(jnp.exp(draws), shape[axis_at] // blocks).reshape((-1,) + (1,) * (len(shape) - axis_at - 1))

    level = one(*split[0])
    for cut in split[1:]:
        level = level * one(*cut)
    return level


def bell_draw(rng, extent, deviation, most, cuts=(), held_as=jnp.bfloat16):
    values = deviation * jax.random.normal(rng, extent, jnp.float32)
    if cuts:
        values = values * level_of(rng, extent, cuts, -0.22, 0.18)
    return jnp.clip(values, -most, most).astype(held_as)


def setup_inputs(seed: int = 0) -> dict:
    seeds = jax.random.split(jax.random.key(seed), 9)
    return {
        "grad_out": bell_draw(seeds[0], (SEQ, D), 1.0, 6.0, ((0, 32), (1, 8))),
        "out_weight": bell_draw(seeds[1], (D, D), D ** -0.5, 0.09375, ((0, 32), (1, 8))),
        "gate_in": bell_draw(seeds[2], (D, SEQ), 1.0, 6.0, ((0, 8), (1, 32))),
        "gate_out": bell_draw(seeds[3], (D, SEQ), 1.0, 6.0, ((0, 8), (1, 32))),
        "values": bell_draw(seeds[4], (D, SEQ), 1.0, 6.0, ((0, 8), (1, 32))),
        "conv_out": bell_draw(seeds[5], (D, SEQ), 1.0, 6.0, ((0, 8), (1, 32))),
        "filters": draw_filters(jax.random.fold_in(seeds[8], 71), 0),
        "skip_scale": bell_draw(seeds[7], (D,), 1.0, 4.0, ((0, 8),), jnp.float32),
    }


def correlate(block):
    grad_block, product_block, filter_block, scale_block = block
    total = 2 * SEQ
    grad_spec = jnp.fft.rfft(grad_block.astype(jnp.float32), n=total, axis=1)
    filter_spec = jnp.fft.rfft(filter_block, n=total, axis=1)
    product_spec = jnp.fft.rfft(product_block.astype(jnp.float32), n=total, axis=1)
    mixed = jnp.fft.irfft(grad_spec * jnp.conj(filter_spec), n=total, axis=1)[:, :SEQ]
    mixed = mixed + scale_block[:, None] * grad_block.astype(jnp.float32)
    grad_filt = jnp.fft.irfft(grad_spec * jnp.conj(product_spec), n=total, axis=1)[:, :SEQ]
    return mixed.astype(jnp.bfloat16), grad_filt.astype(jnp.float32)


def reference(grad_out, out_weight, gate_in, gate_out, values, conv_out, filters, skip_scale):
    back = jnp.dot(out_weight, grad_out.T, preferred_element_type=jnp.float32)
    grad_gate_out = (back * conv_out.astype(jnp.float32)).astype(jnp.bfloat16)
    gated = (back * gate_out.astype(jnp.float32)).astype(jnp.bfloat16)
    product = (gate_in.astype(jnp.float32) * values.astype(jnp.float32)).astype(jnp.bfloat16)
    groups = D // 256
    mixed, grad_filters = lax.map(correlate, (gated.reshape(groups, 256, SEQ), product.reshape(groups, 256, SEQ), filters.reshape(groups, 256, SEQ), skip_scale.reshape(groups, 256)))
    mixed = mixed.reshape(D, SEQ)
    grad_filters = grad_filters.reshape(D, SEQ)
    grad_gate_in = (mixed.astype(jnp.float32) * values.astype(jnp.float32)).astype(jnp.bfloat16)
    grad_values = (mixed.astype(jnp.float32) * gate_in.astype(jnp.float32)).astype(jnp.bfloat16)
    return grad_gate_in, grad_values, grad_gate_out, grad_filters
```

```python
import functools
import math

import jax
import jax.numpy as jnp
import ml_dtypes
import numpy as np
from jax import lax
from jax.experimental import pallas as pl
from jax.experimental.pallas import tpu as pltpu
from jax.sharding import PartitionSpec as P

OUTER = 64
CHUNK = 256


def split_pair(table):
    high = table.astype(np.float32).astype(ml_dtypes.bfloat16)
    low = (table - high.astype(np.float64)).astype(np.float32).astype(ml_dtypes.bfloat16)
    return high, low


def make_tables(blocks, width, inner):
    total = OUTER * inner
    half = OUTER // 2 + 1
    k = np.arange(half)
    a = np.arange(blocks)
    b = np.arange(inner)
    first = 2.0 * np.pi * (np.outer(k, a) % OUTER) / OUTER
    eye = np.eye(width)
    k_cos = np.kron(np.cos(first), eye)
    k_sin = np.kron(np.sin(first), eye)
    into = np.concatenate([k_cos, -k_sin], 0)
    weight = np.full((half, 1), 2.0)
    weight[0] = 1.0
    weight[-1] = 1.0
    weight = weight / total
    back_cos = np.kron((weight * np.cos(first)).T, eye)
    back_sin = np.kron((weight * np.sin(first)).T, eye)
    out_of = np.concatenate([back_cos, back_sin], 1)
    turn = 2.0 * np.pi * (np.outer(k, b) % total) / total
    turn = np.repeat(turn, width, axis=0)
    second = 2.0 * np.pi * (np.outer(b, b) % inner) / inner
    c, s = np.cos(second), np.sin(second)
    across = np.concatenate([np.concatenate([c, -s], 1), np.concatenate([s, c], 1)], 0)
    return (
        split_pair(into),
        split_pair(out_of),
        np.cos(turn).astype(np.float32),
        np.sin(turn).astype(np.float32),
        split_pair(across),
    )


def dot(left, right):
    return jnp.dot(left, right, preferred_element_type=jnp.float32)


def turned(real, imag, cos, sin):
    return real * cos + imag * sin, imag * cos - real * sin


def spread(x_ref, into, twist, z_ref):
    rows = z_ref.shape[0]
    inner = x_ref.shape[1]

    @pl.loop(0, inner // CHUNK)
    def _(i):
        at = pl.ds(pl.multiple_of(i * CHUNK, CHUNK), CHUNK)
        block = x_ref[:, at]
        y = dot(into[0][...], block) + dot(into[1][...], block)
        real, imag = turned(y[:rows], y[rows:], twist[0][:, at], twist[1][:, at])
        z_ref[:, at] = real.astype(jnp.bfloat16)
        z_ref[:, pl.ds(pl.multiple_of(inner + i * CHUNK, CHUNK), CHUNK)] = imag.astype(jnp.bfloat16)


def across_columns(z_ref, across, out_ref):
    @pl.loop(0, z_ref.shape[1] // CHUNK)
    def _(i):
        at = pl.ds(pl.multiple_of(i * CHUNK, CHUNK), CHUNK)
        z = z_ref[...]
        out_ref[:, at] = dot(z, across[0][:, at]) + dot(z, across[1][:, at])


def combine(grad_ref, other_ref, z_ref, inner):
    @pl.loop(0, inner // CHUNK)
    def _(i):
        at = pl.ds(pl.multiple_of(i * CHUNK, CHUNK), CHUNK)
        far = pl.ds(pl.multiple_of(inner + i * CHUNK, CHUNK), CHUNK)
        g_re, g_im = grad_ref[:, at], grad_ref[:, far]
        o_re, o_im = other_ref[:, at], other_ref[:, far]
        z_ref[:, at] = (g_re * o_re + g_im * o_im).astype(jnp.bfloat16)
        z_ref[:, far] = (g_re * o_im - g_im * o_re).astype(jnp.bfloat16)


def gather_up(spec_ref, out_of, twist, u_ref, inner, store):
    rows = spec_ref.shape[0]

    @pl.loop(0, inner // CHUNK)
    def _(i):
        at = pl.ds(pl.multiple_of(i * CHUNK, CHUNK), CHUNK)
        far = pl.ds(pl.multiple_of(inner + i * CHUNK, CHUNK), CHUNK)
        real, imag = turned(spec_ref[:, at], spec_ref[:, far], twist[0][:, at], twist[1][:, at])
        u_ref[:rows, :] = real.astype(jnp.bfloat16)
        u_ref[rows:, :] = imag.astype(jnp.bfloat16)
        u = u_ref[...]
        store(at, dot(out_of[0][...], u) + dot(out_of[1][...], u))


def forward_kernel(x_ref, in_hi, in_lo, cos, sin, ac_hi, ac_lo, out_ref, z_ref):
    for i in range(2):
        spread(x_ref.at[i], (in_hi, in_lo), (cos, sin), z_ref)
        across_columns(z_ref, (ac_hi, ac_lo), out_ref.at[i])


def inverse_kernel(
    g_ref, other_ref, skip_ref, in_hi, in_lo, of_hi, of_lo, cos, sin, ac_hi, ac_lo, out_ref,
    z_ref, grad_ref, spec_ref, u_ref,
):
    inner = g_ref.shape[1]
    across = (ac_hi, ac_lo)
    spread(g_ref, (in_hi, in_lo), (cos, sin), z_ref)
    across_columns(z_ref, across, grad_ref)
    for i in range(2):
        combine(grad_ref, other_ref.at[i], z_ref, inner)
        across_columns(z_ref, across, spec_ref)

        def store(at, value):
            if i == 1:
                value = value + skip_ref[...] * g_ref[:, at].astype(jnp.float32)
            out_ref[i, :, at] = value.astype(jnp.bfloat16)

        gather_up(spec_ref, (of_hi, of_lo), (cos, sin), u_ref, inner, store)


VMEM = pl.BlockSpec(memory_space=pltpu.VMEM)


def shards(grad_out, out_weight, gate_in, gate_out, values, conv_out, filters, skip_scale):
    blocks = lax.axis_size("seq")
    rows, inner = gate_in.shape
    width = rows // blocks
    into, out_of, cos, sin, across = make_tables(blocks, width, inner)
    spec_rows = cos.shape[0]
    params = pltpu.CompilerParams(vmem_limit_bytes=50 * 1024 * 1024)

    product = (gate_in.astype(jnp.float32) * values.astype(jnp.float32)).astype(jnp.bfloat16)
    sent = jnp.stack(
        [product.reshape(blocks, width, inner), filters.astype(jnp.bfloat16).reshape(blocks, width, inner)], 1
    )
    landed = lax.all_to_all(sent, "seq", split_axis=0, concat_axis=0, tiled=True)
    landed = landed.transpose(1, 0, 2, 3).reshape(2, rows, inner)
    weight_rows = lax.all_gather(out_weight, "seq", axis=0, tiled=True)
    others = pl.pallas_call(
        forward_kernel,
        out_shape=jax.ShapeDtypeStruct((2, spec_rows, 2 * inner), jnp.float32),
        in_specs=[VMEM] * 7,
        out_specs=VMEM,
        scratch_shapes=[pltpu.VMEM((spec_rows, 2 * inner), jnp.bfloat16)],
        compiler_params=params,
        cost_estimate=pl.CostEstimate(flops=7 * 10**9, bytes_accessed=16 * 10**6, transcendentals=0),
    )(landed, *into, cos, sin, *across)

    back = lax.psum_scatter(
        lax.dot_general(
            weight_rows, grad_out, (((1,), (1,)), ((), ())), preferred_element_type=jnp.float32
        ),
        "ch",
        scatter_dimension=0,
        tiled=True,
    )
    grad_gate_out = (back * conv_out.astype(jnp.float32)).astype(jnp.bfloat16)
    gated = (back * gate_out.astype(jnp.float32)).astype(jnp.bfloat16)
    gated = lax.all_to_all(
        gated.reshape(blocks, width, inner), "seq", split_axis=0, concat_axis=0, tiled=True
    ).reshape(rows, inner)
    scale = lax.dynamic_slice_in_dim(skip_scale, lax.axis_index("seq") * width, width, 0)
    scale = jnp.tile(scale, blocks)[:, None]
    both = pl.pallas_call(
        inverse_kernel,
        out_shape=jax.ShapeDtypeStruct((2, rows, inner), jnp.bfloat16),
        in_specs=[VMEM] * 11,
        out_specs=VMEM,
        scratch_shapes=[
            pltpu.VMEM((spec_rows, 2 * inner), jnp.bfloat16),
            pltpu.VMEM((spec_rows, 2 * inner), jnp.float32),
            pltpu.VMEM((spec_rows, 2 * inner), jnp.float32),
            pltpu.VMEM((2 * spec_rows, CHUNK), jnp.bfloat16),
        ],
        compiler_params=params,
        cost_estimate=pl.CostEstimate(flops=10 * 10**9, bytes_accessed=20 * 10**6, transcendentals=0),
    )(gated, others, scale, *into, *out_of, cos, sin, *across)
    mixed = lax.all_to_all(
        both[1].reshape(blocks, width, inner), "seq", split_axis=0, concat_axis=0, tiled=True
    ).reshape(rows, inner)
    grad_filters = lax.all_to_all(
        both[0].reshape(blocks, width, inner), "seq", split_axis=0, concat_axis=0, tiled=True
    ).reshape(rows, inner)
    mixed_wide = mixed.astype(jnp.float32)
    grad_gate_in = (mixed_wide * values.astype(jnp.float32)).astype(jnp.bfloat16)
    grad_values = (mixed_wide * gate_in.astype(jnp.float32)).astype(jnp.bfloat16)
    return (grad_gate_in, grad_values, grad_gate_out, grad_filters.astype(jnp.float32))


def solution(mesh):
    placed = (
        P("seq", "ch"),
        P("seq", "ch"),
        P("ch", "seq"),
        P("ch", "seq"),
        P("ch", "seq"),
        P("ch", "seq"),
        P("ch", "seq"),
        P("ch"),
    )
    return jax.shard_map(
        shards,
        mesh=mesh,
        in_specs=placed,
        out_specs=(P("ch", "seq"), P("ch", "seq"), P("ch", "seq"), P("ch", "seq")),
        check_vma=False,
    )
```

```python
import functools
import math

import jax
import jax.numpy as jnp
import ml_dtypes
import numpy as np
from jax import lax
from jax.experimental import pallas as pl
from jax.experimental.pallas import tpu as pltpu
from jax.sharding import PartitionSpec as P

OUTER = 64
CHUNK = 256


def split_pair(table):
    high = table.astype(np.float32).astype(ml_dtypes.bfloat16)
    low = (table - high.astype(np.float64)).astype(np.float32).astype(ml_dtypes.bfloat16)
    return high, low


def make_tables(blocks, width, inner):
    total = OUTER * inner
    half = OUTER // 2 + 1
    k = np.arange(half)
    a = np.arange(blocks)
    b = np.arange(inner)
    first = 2.0 * np.pi * (np.outer(k, a) % OUTER) / OUTER
    eye = np.eye(width)
    k_cos = np.kron(np.cos(first), eye)
    k_sin = np.kron(np.sin(first), eye)
    into = np.concatenate([k_cos, -k_sin], 0)
    weight = np.full((half, 1), 2.0)
    weight[0] = 1.0
    weight[-1] = 1.0
    weight = weight / total
    back_cos = np.kron((weight * np.cos(first)).T, eye)
    back_sin = np.kron((weight * np.sin(first)).T, eye)
    out_of = np.concatenate([back_cos, back_sin], 1)
    turn = 2.0 * np.pi * (np.outer(k, b) % total) / total
    turn = np.repeat(turn, width, axis=0)
    second = 2.0 * np.pi * (np.outer(b, b) % inner) / inner
    c, s = np.cos(second), np.sin(second)
    across = np.concatenate([np.concatenate([c, -s], 1), np.concatenate([s, c], 1)], 0)
    return (
        split_pair(into),
        split_pair(out_of),
        np.cos(turn).astype(np.float32),
        np.sin(turn).astype(np.float32),
        split_pair(across),
    )


def dot(left, right):
    return jnp.dot(left, right, preferred_element_type=jnp.float32)


def turned(real, imag, cos, sin):
    return real * cos + imag * sin, imag * cos - real * sin


def spread(x_ref, into, twist, z_ref):
    rows = z_ref.shape[0]
    inner = x_ref.shape[1]

    @pl.loop(0, inner // CHUNK)
    def _(i):
        at = pl.ds(pl.multiple_of(i * CHUNK, CHUNK), CHUNK)
        block = x_ref[:, at]
        y = dot(into[0][...], block) + dot(into[1][...], block)
        real, imag = turned(y[:rows], y[rows:], twist[0][:, at], twist[1][:, at])
        z_ref[:, at] = real.astype(jnp.bfloat16)
        z_ref[:, pl.ds(pl.multiple_of(inner + i * CHUNK, CHUNK), CHUNK)] = imag.astype(jnp.bfloat16)


def across_columns(z_ref, across, out_ref):
    @pl.loop(0, z_ref.shape[1] // CHUNK)
    def _(i):
        at = pl.ds(pl.multiple_of(i * CHUNK, CHUNK), CHUNK)
        z = z_ref[...]
        out_ref[:, at] = dot(z, across[0][:, at]) + dot(z, across[1][:, at])


def combine(grad_ref, other_ref, z_ref, inner):
    @pl.loop(0, inner // CHUNK)
    def _(i):
        at = pl.ds(pl.multiple_of(i * CHUNK, CHUNK), CHUNK)
        far = pl.ds(pl.multiple_of(inner + i * CHUNK, CHUNK), CHUNK)
        g_re, g_im = grad_ref[:, at], grad_ref[:, far]
        o_re, o_im = other_ref[:, at], other_ref[:, far]
        z_ref[:, at] = (g_re * o_re + g_im * o_im).astype(jnp.bfloat16)
        z_ref[:, far] = (g_re * o_im - g_im * o_re).astype(jnp.bfloat16)


def gather_up(spec_ref, out_of, twist, u_ref, inner, store):
    rows = spec_ref.shape[0]

    @pl.loop(0, inner // CHUNK)
    def _(i):
        at = pl.ds(pl.multiple_of(i * CHUNK, CHUNK), CHUNK)
        far = pl.ds(pl.multiple_of(inner + i * CHUNK, CHUNK), CHUNK)
        real, imag = turned(spec_ref[:, at], spec_ref[:, far], twist[0][:, at], twist[1][:, at])
        u_ref[:rows, :] = real.astype(jnp.bfloat16)
        u_ref[rows:, :] = imag.astype(jnp.bfloat16)
        u = u_ref[...]
        store(at, dot(out_of[0][...], u) + dot(out_of[1][...], u))


def forward_kernel(x_ref, in_hi, in_lo, cos, sin, ac_hi, ac_lo, out_ref, z_ref):
    for i in range(2):
        spread(x_ref.at[i], (in_hi, in_lo), (cos, sin), z_ref)
        across_columns(z_ref, (ac_hi, ac_lo), out_ref.at[i])


def inverse_kernel(
    g_ref, other_ref, skip_ref, in_hi, in_lo, of_hi, of_lo, cos, sin, ac_hi, ac_lo, out_ref,
    z_ref, grad_ref, spec_ref, u_ref,
):
    inner = g_ref.shape[1]
    across = (ac_hi, ac_lo)
    spread(g_ref, (in_hi, in_lo), (cos, sin), z_ref)
    across_columns(z_ref, across, grad_ref)
    for i in range(2):
        combine(grad_ref, other_ref.at[i], z_ref, inner)
        across_columns(z_ref, across, spec_ref)

        def store(at, value):
            if i == 1:
                value = value + skip_ref[...] * g_ref[:, at].astype(jnp.float32)
            out_ref[i, :, at] = value.astype(jnp.bfloat16)

        gather_up(spec_ref, (of_hi, of_lo), (cos, sin), u_ref, inner, store)


VMEM = pl.BlockSpec(memory_space=pltpu.VMEM)


ZS, XS, YS = 8, 4, 4
MESH = pl.DeviceIdType.MESH


def project_kernel(
    w_ref, g_ref, gate_in_ref, values_ref, gate_out_ref, filters_ref,
    gated_out, pair_out, home_out,
    w_ring, w_mine, w_other, g_ring, g_other, own, part, sums, near_gate, back_bf, gated, stage, crossed,
    send_sems, recv_sems,
):
    s, h = lax.axis_index("seq"), lax.axis_index("ch")
    z, x = s // XS, s % XS
    y, core = h // 2, h % 2

    def at_z(d):
        return (lax.rem(z + d + ZS, ZS) * XS + x, h)

    def at_x(d):
        return (z * XS + lax.rem(x + d + XS, XS), h)

    def at_y(d):
        return (s, lax.rem(y + d, YS) * 2 + core)

    sibling = (s, y * 2 + 1 - core)
    peers = [at_z(d) for d in range(1, ZS)] + [at_x(d) for d in range(1, XS)]
    peers += [at_y(d) for d in range(1, YS)] + [sibling]

    barrier = pltpu.get_barrier_semaphore()
    for peer in peers:
        pl.semaphore_signal(barrier, inc=1, device_id=peer, device_id_type=MESH)
    pl.semaphore_wait(barrier, len(peers))

    copies = []

    def send(src, dst, device):
        k = len(copies)
        copy = pltpu.make_async_remote_copy(
            src_ref=src, dst_ref=dst, send_sem=send_sems.at[k], recv_sem=recv_sems.at[k],
            device_id=device, device_id_type=MESH,
        )
        copy.start()
        copies.append(copy)
        return copy

    def zmod(d):
        return lax.rem(z + d + ZS, ZS)

    def xmod(d):
        return lax.rem(x + d + XS, XS)

    half_w = w_ref.shape[0] // 2
    half_g = g_ref.shape[0] // 2
    top, low = pl.ds(0, half_g), pl.ds(half_g, half_g)

    up = send(w_ref, w_ring.at[z], at_z(1))
    down = send(w_ref, w_ring.at[z], at_z(-1))
    right_top = send(g_ref.at[top], g_ring.at[x, top], at_x(1))
    left_low = send(g_ref.at[low], g_ring.at[x, low], at_x(-1))
    right_low = send(g_ref.at[low], g_ring.at[x, low], at_x(1))
    left_top = send(g_ref.at[top], g_ring.at[x, top], at_x(-1))
    shared = [send(g_ref, g_other.at[0], sibling)]
    w_ring[z] = w_ref[...]
    for i in range(XS):
        product = gate_in_ref[i].astype(jnp.float32) * values_ref[i].astype(jnp.float32)
        stage[0, i] = product.astype(jnp.bfloat16)
        stage[1, i] = filters_ref[i].astype(jnp.bfloat16)

    up.wait_recv()
    up = send(w_ring.at[zmod(-1)], w_ring.at[zmod(-1)], at_z(1))
    down.wait_recv()
    down = send(w_ring.at[zmod(1)], w_ring.at[zmod(1)], at_z(-1))
    right_top.wait_recv()
    far_top = send(g_ring.at[xmod(-1), top], g_ring.at[xmod(-1), top], at_x(1))
    left_low.wait_recv()
    far_low = send(g_ring.at[xmod(1), low], g_ring.at[xmod(1), low], at_x(-1))
    gates = [send(gate_out_ref.at[xmod(d)], near_gate.at[d], at_x(d)) for d in range(1, XS)]
    near_gate[0] = gate_out_ref[x]
    up.wait_recv()
    up = send(w_ring.at[zmod(-2)], w_ring.at[zmod(-2)], at_z(1))
    down.wait_recv()
    down = send(w_ring.at[zmod(2)], w_ring.at[zmod(2)], at_z(-1))
    up.wait_recv()
    first, second = pl.ds(0, half_w), pl.ds(half_w, half_w)
    up = send(w_ring.at[zmod(-3), first], w_ring.at[zmod(-3), first], at_z(1))
    down.wait_recv()
    down = send(w_ring.at[zmod(3), second], w_ring.at[zmod(3), second], at_z(-1))
    pairs = [
        send(stage.at[:, :, zmod(d)], crossed.at[:, z], at_z(d)) for d in range(1, ZS)
    ]
    crossed[:, z] = stage[:, :, z]
    up.wait_recv()
    down.wait_recv()

    def rows_for(d, of_core):
        return lax.rem(y + d, YS) * 2 + of_core

    w_shared = [
        send(w_ring.at[rows_for(d, 1 - core)], w_other.at[d], sibling) for d in range(YS)
    ]
    for d in range(YS):
        w_mine[d] = w_ring[rows_for(d, core)]
    right_low.wait_recv()
    shared.append(send(g_ring.at[xmod(-1)], g_other.at[1], sibling))
    left_top.wait_recv()
    shared.append(send(g_ring.at[xmod(1)], g_other.at[2], sibling))
    for copy in w_shared:
        copy.wait_recv()

    offsets = (0, -1, 1, 2)
    parts = []
    wide = (YS * w_ref.shape[0], w_ref.shape[1])
    tile = 256
    for n, off in enumerate(offsets):
        if n == 3:
            far_top.wait_recv()
            far_low.wait_recv()
            shared.append(send(g_ring.at[xmod(2)], g_other.at[3], sibling))
        shared[n].wait_recv()

        @pl.loop(0, g_ref.shape[0] // tile)
        def _(i, n=n, off=off):
            at = pl.ds(pl.multiple_of(i * tile, tile), tile)
            near = g_ref[at, :] if n == 0 else g_ring[xmod(off), at, :]
            form = (((1,), (1,)), ((), ()))
            total = lax.dot_general(
                w_mine[...].reshape(wide), near, form, preferred_element_type=jnp.float32
            ) + lax.dot_general(
                w_other[...].reshape(wide), g_other[n, at, :], form, preferred_element_type=jnp.float32
            )
            total = total.reshape(YS, w_ref.shape[0], tile)
            own[n, :, at] = total[0]
            part[n, :, :, at] = total[1:].astype(jnp.bfloat16)

        parts.append([send(part.at[n, d - 1], sums.at[n, d - 1], at_y(d)) for d in range(1, YS)])

    for copy in pairs:
        copy.wait_recv()
    tails = [
        send(crossed.at[:, :, xmod(d)], pair_out.at[:, :, x], at_x(d)) for d in range(1, XS)
    ]
    pair_out[:, :, x] = crossed[:, :, x]

    arrivals = []
    for n, off in enumerate(offsets):
        for copy in parts[n]:
            copy.wait_recv()
        back = own[n]
        for d in range(1, YS):
            back = back + sums[n, d - 1].astype(jnp.float32)
        result = back * near_gate_value(near_gate, gates, off)
        gated[n] = result.astype(jnp.bfloat16).reshape(gated.shape[1:])
        for d in range(1, ZS):
            arrivals.append(send(gated.at[n, zmod(d)], gated_out.at[z, xmod(off)], at_z(d)))
        gated_out[z, xmod(off)] = gated[n, z]
        back_bf[n] = back.astype(jnp.bfloat16)
        if n == 0:
            home_out[x] = back_bf[n]
        else:
            arrivals.append(send(back_bf.at[n], home_out.at[x], at_x(off)))

    for copy in tails + arrivals:
        copy.wait_recv()
    for copy in copies:
        copy.wait_send()


def near_gate_value(near_gate, gates, off):
    d = -off % XS
    if d:
        gates[d - 1].wait_recv()
    return near_gate[d].astype(jnp.float32)


def project(grad_out, out_weight, gate_in, gate_out, values, filters):
    rows, inner = gate_in.shape
    deep, wide = out_weight.shape
    width = rows // (ZS * XS)
    bf = jnp.bfloat16
    split = (XS, ZS, width, inner)
    count = 2 + 4 + 1 + 2 + 2 + 3 + 2 + 2 + 7 + 4 + 3 + 12 + 3 + 28 + 3
    return pl.pallas_call(
        project_kernel,
        out_shape=[
            jax.ShapeDtypeStruct((ZS, XS, width, inner), bf),
            jax.ShapeDtypeStruct((2, ZS, XS, width, inner), bf),
            jax.ShapeDtypeStruct((XS, deep, inner), bf),
        ],
        in_specs=[VMEM] * 6,
        out_specs=[VMEM] * 3,
        scratch_shapes=[
            pltpu.VMEM((ZS, deep, wide), bf),
            pltpu.VMEM((YS, deep, wide), bf),
            pltpu.VMEM((YS, deep, wide), bf),
            pltpu.VMEM((XS,) + grad_out.shape, bf),
            pltpu.VMEM((XS,) + grad_out.shape, bf),
            pltpu.VMEM((XS, deep, inner), jnp.float32),
            pltpu.VMEM((XS, YS - 1, deep, inner), bf),
            pltpu.VMEM((XS, YS - 1, deep, inner), bf),
            pltpu.VMEM((XS, deep, inner), bf),
            pltpu.VMEM((XS, deep, inner), bf),
            pltpu.VMEM((XS, ZS, width, inner), bf),
            pltpu.VMEM((2,) + split, bf),
            pltpu.VMEM((2, ZS, XS, width, inner), bf),
            pltpu.SemaphoreType.DMA((count,)),
            pltpu.SemaphoreType.DMA((count,)),
        ],
        compiler_params=pltpu.CompilerParams(
            collective_id=0, has_side_effects=True, vmem_limit_bytes=50 * 1024 * 1024
        ),
        cost_estimate=pl.CostEstimate(flops=3 * 10**9, bytes_accessed=6 * 10**6, transcendentals=0),
    )(
        out_weight,
        grad_out,
        gate_in.reshape(split),
        values.reshape(split),
        gate_out.reshape(XS, deep, inner),
        filters.reshape(split),
    )


def shards(grad_out, out_weight, gate_in, gate_out, values, conv_out, filters, skip_scale):
    rows, inner = gate_in.shape
    blocks = ZS * XS
    width = rows // blocks
    into, out_of, cos, sin, across = make_tables(blocks, width, inner)
    spec_rows = cos.shape[0]
    params = pltpu.CompilerParams(vmem_limit_bytes=50 * 1024 * 1024)

    gated, pair, home = project(grad_out, out_weight, gate_in, gate_out, values, filters)
    grad_gate_out = (
        home.reshape(rows, inner).astype(jnp.float32) * conv_out.astype(jnp.float32)
    ).astype(jnp.bfloat16)
    others = pl.pallas_call(
        forward_kernel,
        out_shape=jax.ShapeDtypeStruct((2, spec_rows, 2 * inner), jnp.float32),
        in_specs=[VMEM] * 7,
        out_specs=VMEM,
        scratch_shapes=[pltpu.VMEM((spec_rows, 2 * inner), jnp.bfloat16)],
        compiler_params=params,
        cost_estimate=pl.CostEstimate(flops=7 * 10**9, bytes_accessed=16 * 10**6, transcendentals=0),
    )(pair.reshape(2, rows, inner), *into, cos, sin, *across)
    place = lax.axis_index("seq")
    start = (place % XS) * (rows // XS) + (place // XS) * width
    scale = lax.dynamic_slice_in_dim(skip_scale, start, width, 0)
    scale = jnp.tile(scale, blocks)[:, None]
    both = pl.pallas_call(
        inverse_kernel,
        out_shape=jax.ShapeDtypeStruct((2, rows, inner), jnp.bfloat16),
        in_specs=[VMEM] * 11,
        out_specs=VMEM,
        scratch_shapes=[
            pltpu.VMEM((spec_rows, 2 * inner), jnp.bfloat16),
            pltpu.VMEM((spec_rows, 2 * inner), jnp.float32),
            pltpu.VMEM((spec_rows, 2 * inner), jnp.float32),
            pltpu.VMEM((2 * spec_rows, CHUNK), jnp.bfloat16),
        ],
        compiler_params=params,
        cost_estimate=pl.CostEstimate(flops=10 * 10**9, bytes_accessed=20 * 10**6, transcendentals=0),
    )(gated.reshape(rows, inner), others, scale, *into, *out_of, cos, sin, *across)
    landed = [
        lax.all_to_all(
            both[i].reshape(blocks, width, inner), "seq", split_axis=0, concat_axis=0, tiled=True
        ).reshape(ZS, XS, width, inner).transpose(1, 0, 2, 3).reshape(rows, inner)
        for i in (1, 0)
    ]
    mixed_wide = landed[0].astype(jnp.float32)
    grad_gate_in = (mixed_wide * values.astype(jnp.float32)).astype(jnp.bfloat16)
    grad_values = (mixed_wide * gate_in.astype(jnp.float32)).astype(jnp.bfloat16)
    return (grad_gate_in, grad_values, grad_gate_out, landed[1].astype(jnp.float32))


def solution(mesh):
    placed = (
        P("seq", "ch"),
        P("seq", "ch"),
        P("ch", "seq"),
        P("ch", "seq"),
        P("ch", "seq"),
        P("ch", "seq"),
        P("ch", "seq"),
        P("ch"),
    )
    return jax.shard_map(
        shards,
        mesh=mesh,
        in_specs=placed,
        out_specs=(P("ch", "seq"), P("ch", "seq"), P("ch", "seq"), P("ch", "seq")),
        check_vma=False,
    )
```

```python
import jax
import jax.numpy as jnp
import ml_dtypes
import numpy as np
from jax import lax
from jax.experimental import pallas as pl
from jax.experimental.pallas import tpu as pltpu
from jax.sharding import PartitionSpec as P

OUTER = 64
CHUNK = 256


def split_pair(table):
    high = table.astype(np.float32).astype(ml_dtypes.bfloat16)
    low = (table - high.astype(np.float64)).astype(np.float32).astype(ml_dtypes.bfloat16)
    return high, low


def make_tables(blocks, width, inner):
    total = OUTER * inner
    half = OUTER // 2 + 1
    k = np.arange(half)
    a = np.arange(blocks)
    b = np.arange(inner)
    first = 2.0 * np.pi * (np.outer(k, a) % OUTER) / OUTER
    eye = np.eye(width)
    k_cos = np.kron(np.cos(first), eye)
    k_sin = np.kron(np.sin(first), eye)
    into = np.concatenate([k_cos, -k_sin], 0)
    weight = np.full((half, 1), 2.0)
    weight[0] = 1.0
    weight[-1] = 1.0
    weight = weight / total
    back_cos = np.kron((weight * np.cos(first)).T, eye)
    back_sin = np.kron((weight * np.sin(first)).T, eye)
    out_of = np.concatenate([back_cos, back_sin], 1)
    turn = 2.0 * np.pi * (np.outer(k, b) % total) / total
    turn = np.repeat(turn, width, axis=0)
    second = 2.0 * np.pi * (np.outer(b, b) % inner) / inner
    c, s = np.cos(second), np.sin(second)
    across = np.concatenate([np.concatenate([c, -s], 1), np.concatenate([s, c], 1)], 0)
    return (
        split_pair(into),
        split_pair(out_of),
        np.cos(turn).astype(np.float32),
        np.sin(turn).astype(np.float32),
        split_pair(across),
    )


def dot(left, right):
    return jnp.dot(left, right, preferred_element_type=jnp.float32)


def turned(real, imag, cos, sin):
    return real * cos + imag * sin, imag * cos - real * sin


ZS, XS, YS = 8, 4, 4
VMEM = pl.BlockSpec(memory_space=pltpu.VMEM)
MESH = pl.DeviceIdType.MESH
BF = jnp.bfloat16


def spread(block_of, into, twist, z_ref, inner):
    rows = z_ref.shape[0]

    @pl.loop(0, inner // CHUNK)
    def _(i):
        at = pl.ds(pl.multiple_of(i * CHUNK, CHUNK), CHUNK)
        block = block_of(at)
        y = dot(into[0][...], block) + dot(into[1][...], block)
        real, imag = turned(y[:rows], y[rows:], twist[0][:, at], twist[1][:, at])
        z_ref[:, at] = real.astype(BF)
        z_ref[:, pl.ds(pl.multiple_of(inner + i * CHUNK, CHUNK), CHUNK)] = imag.astype(BF)


def across_columns(z_ref, across, out_ref):
    @pl.loop(0, z_ref.shape[1] // CHUNK)
    def _(i):
        at = pl.ds(pl.multiple_of(i * CHUNK, CHUNK), CHUNK)
        z = z_ref[...]
        out_ref[:, at] = dot(z, across[0][:, at]) + dot(z, across[1][:, at])


def combine(grad_ref, other_ref, z_ref, inner):
    @pl.loop(0, inner // CHUNK)
    def _(i):
        at = pl.ds(pl.multiple_of(i * CHUNK, CHUNK), CHUNK)
        far = pl.ds(pl.multiple_of(inner + i * CHUNK, CHUNK), CHUNK)
        g_re, g_im = grad_ref[:, at], grad_ref[:, far]
        o_re, o_im = other_ref[:, at], other_ref[:, far]
        z_ref[:, at] = (g_re * o_re + g_im * o_im).astype(BF)
        z_ref[:, far] = (g_re * o_im - g_im * o_re).astype(BF)


def layer_kernel(
    w_hbm, g_hbm, gate_in_hbm, values_hbm, gate_out_hbm, filters_hbm, skip_ref,
    in_hi_h, in_lo_h, of_hi_h, of_lo_h, cos_h, sin_h, ac_hi_h, ac_lo_h,
    home_out, result_out,
    gate_in, values, filters, in_hi, in_lo, of_hi, of_lo, cos, sin, ac_hi, ac_lo,
    w_ring, w_mine, w_other, g_ring, g_other, own, hold, part, inbox, relay, final,
    near_gate, back_bf, gated, gated_in, stage, crossed, pair_in,
    z_ref, u_ref, spec_g, spec_p, spec_f, leaving, landed,
    send_sems, recv_sems, local_sems,
):
    s, h = lax.axis_index("seq"), lax.axis_index("ch")
    z, x = s // XS, s % XS
    y, core = h // 2, h % 2

    def zmod(d):
        return lax.rem(z + d + ZS, ZS)

    def xmod(d):
        return lax.rem(x + d + XS, XS)

    def at_z(d):
        return (zmod(d) * XS + x, h)

    def at_x(d):
        return (z * XS + xmod(d), h)

    def at_y(d):
        return (s, lax.rem(y + d + YS, YS) * 2 + core)

    sibling = (s, y * 2 + 1 - core)
    peers = [at_z(d) for d in range(1, ZS)] + [at_x(d) for d in range(1, XS)]
    peers += [at_y(d) for d in (1, -1)] + [sibling]

    barrier = pltpu.get_barrier_semaphore()
    for peer in peers:
        pl.semaphore_signal(barrier, inc=1, device_id=peer, device_id_type=MESH)

    loads = []

    def load(src, dst):
        copy = pltpu.make_async_copy(src, dst, local_sems.at[len(loads)])
        copy.start()
        loads.append(copy)
        return copy

    w_load = load(w_hbm, w_ring.at[z])
    g_load = load(g_hbm, g_ring.at[x])
    pair_loads = [load(gate_in_hbm, gate_in), load(values_hbm, values), load(filters_hbm, filters)]
    gate_load = load(gate_out_hbm.at[x], near_gate.at[0])
    table_loads = [
        load(src, dst)
        for src, dst in (
            (in_hi_h, in_hi), (in_lo_h, in_lo), (ac_hi_h, ac_hi), (ac_lo_h, ac_lo),
            (cos_h, cos), (sin_h, sin), (of_hi_h, of_hi), (of_lo_h, of_lo),
        )
    ]
    pl.semaphore_wait(barrier, len(peers))

    copies = []

    def send(src, dst, device):
        k = len(copies)
        copy = pltpu.make_async_remote_copy(
            src_ref=src, dst_ref=dst, send_sem=send_sems.at[k], recv_sem=recv_sems.at[k],
            device_id=device, device_id_type=MESH,
        )
        copy.start()
        copies.append(copy)
        return copy

    half_w = w_ring.shape[1] // 2
    half_g = g_ring.shape[1] // 2
    first, second = pl.ds(0, half_w), pl.ds(half_w, half_w)
    top, low = pl.ds(0, half_g), pl.ds(half_g, half_g)

    up = send(w_hbm, w_ring.at[z], at_z(1))
    down = send(w_hbm, w_ring.at[z], at_z(-1))
    right_top = send(g_hbm.at[top], g_ring.at[x, top], at_x(1))
    left_low = send(g_hbm.at[low], g_ring.at[x, low], at_x(-1))
    right_low = send(g_hbm.at[low], g_ring.at[x, low], at_x(1))
    left_top = send(g_hbm.at[top], g_ring.at[x, top], at_x(-1))
    shared = [send(g_hbm, g_other.at[0], sibling)]
    for copy in pair_loads:
        copy.wait()
    for i in range(XS):
        product = gate_in[i].astype(jnp.float32) * values[i].astype(jnp.float32)
        stage[0, i] = product.astype(BF)
        stage[1, i] = filters[i].astype(BF)

    up.wait_recv()
    up = send(w_ring.at[zmod(-1)], w_ring.at[zmod(-1)], at_z(1))
    down.wait_recv()
    down = send(w_ring.at[zmod(1)], w_ring.at[zmod(1)], at_z(-1))
    right_top.wait_recv()
    far_top = send(g_ring.at[xmod(-1), top], g_ring.at[xmod(-1), top], at_x(1))
    left_low.wait_recv()
    far_low = send(g_ring.at[xmod(1), low], g_ring.at[xmod(1), low], at_x(-1))
    gates = [send(gate_out_hbm.at[xmod(d)], near_gate.at[d], at_x(d)) for d in range(1, XS)]
    up.wait_recv()
    up = send(w_ring.at[zmod(-2)], w_ring.at[zmod(-2)], at_z(1))
    down.wait_recv()
    down = send(w_ring.at[zmod(2)], w_ring.at[zmod(2)], at_z(-1))
    up.wait_recv()
    up = send(w_ring.at[zmod(-3), first], w_ring.at[zmod(-3), first], at_z(1))
    down.wait_recv()
    down = send(w_ring.at[zmod(3), second], w_ring.at[zmod(3), second], at_z(-1))
    pairs = [
        send(stage.at[:, :, zmod(d)], crossed.at[:, z], at_z(d)) for d in range(1, ZS)
    ]
    crossed[:, z] = stage[:, :, z]
    w_load.wait()
    g_load.wait()
    up.wait_recv()
    down.wait_recv()

    def rows_for(d, of_core):
        return lax.rem(y + d, YS) * 2 + of_core

    w_shared = [
        send(w_ring.at[rows_for(d, 1 - core)], w_other.at[d], sibling) for d in range(YS)
    ]
    for d in range(YS):
        w_mine[d] = w_ring[rows_for(d, core)]
    right_low.wait_recv()
    shared.append(send(g_ring.at[xmod(-1)], g_other.at[1], sibling))
    left_top.wait_recv()
    shared.append(send(g_ring.at[xmod(1)], g_other.at[2], sibling))
    for copy in w_shared:
        copy.wait_recv()

    offsets = (0, -1, 1, 2)
    parts = []
    passed = []
    deep = w_ring.shape[1]
    wide = (YS * deep, w_ring.shape[2])

    def pass_on(n):
        for side in range(2):
            parts[n][side].wait_recv()
            relay[n, side] = (hold[n, side] + inbox[n, side, 0].astype(jnp.float32)).astype(BF)
            passed.append(send(relay.at[n, side], final.at[n, side], at_y(1 - 2 * side)))

    for n, off in enumerate(offsets):
        if n == 3:
            far_top.wait_recv()
            far_low.wait_recv()
            shared.append(send(g_ring.at[xmod(2)], g_other.at[3], sibling))
        shared[n].wait_recv()

        @pl.loop(0, g_ring.shape[1] // CHUNK)
        def _(i, n=n, off=off):
            at = pl.ds(pl.multiple_of(i * CHUNK, CHUNK), CHUNK)
            form = (((1,), (1,)), ((), ()))
            total = lax.dot_general(
                w_mine[...].reshape(wide), g_ring[xmod(off), at, :], form,
                preferred_element_type=jnp.float32,
            ) + lax.dot_general(
                w_other[...].reshape(wide), g_other[n, at, :], form,
                preferred_element_type=jnp.float32,
            )
            total = total.reshape(YS, deep, CHUNK)
            own[n, :, at] = total[0]
            hold[n, 0, :, at] = total[1, :half_w]
            hold[n, 1, :, at] = total[3, half_w:]
            part[n, 0, 0, :, at] = total[2, :half_w].astype(BF)
            part[n, 0, 1, :, at] = total[1, half_w:].astype(BF)
            part[n, 1, 0, :, at] = total[2, half_w:].astype(BF)
            part[n, 1, 1, :, at] = total[3, :half_w].astype(BF)

        parts.append([send(part.at[n, side], inbox.at[n, side], at_y(1 - 2 * side)) for side in range(2)])
        if n:
            pass_on(n - 1)

    for copy in pairs:
        copy.wait_recv()
    tails = [
        send(crossed.at[:, :, xmod(d)], pair_in.at[:, :, x], at_x(d)) for d in range(1, XS)
    ]
    pair_in[:, :, x] = crossed[:, :, x]
    pass_on(len(offsets) - 1)

    gate_load.wait()
    arrivals = []
    homes = []
    for n, off in enumerate(offsets):
        for copy in passed[2 * n : 2 * n + 2]:
            copy.wait_recv()
        d = -off % XS
        if d:
            gates[d - 1].wait_recv()
        upper = own[n, :half_w] + final[n, 0].astype(jnp.float32) + inbox[n, 1, 1].astype(jnp.float32)
        lower = own[n, half_w:] + final[n, 1].astype(jnp.float32) + inbox[n, 0, 1].astype(jnp.float32)
        back = jnp.concatenate([upper, lower], 0)
        result = back * near_gate[d].astype(jnp.float32)
        gated[n] = result.astype(BF).reshape(gated.shape[1:])
        for d in range(1, ZS):
            arrivals.append(send(gated.at[n, zmod(d)], gated_in.at[z, xmod(off)], at_z(d)))
        gated_in[z, xmod(off)] = gated[n, z]
        back_bf[n] = back.astype(BF)
        if n == 0:
            home_out[x] = back_bf[n]
        else:
            homes.append(send(back_bf.at[n], home_out.at[x], at_x(off)))

    inner = g_ring.shape[2]
    rows = g_ring.shape[1]
    into, twist, across = (in_hi, in_lo), (cos, sin), (ac_hi, ac_lo)
    for copy in table_loads:
        copy.wait()
    for copy in tails:
        copy.wait_recv()
    for i, spec in ((1, spec_f), (0, spec_p)):
        spread(lambda at, i=i: pair_in[i, :, :, :, at].reshape(rows, CHUNK), into, twist, z_ref, inner)
        across_columns(z_ref, across, spec)
    for copy in arrivals:
        copy.wait_recv()
    spread(lambda at: gated_in[:, :, :, at].reshape(rows, CHUNK), into, twist, z_ref, inner)
    across_columns(z_ref, across, spec_g)

    width = gated_in.shape[2]
    lanes = skip_ref.shape[1]
    pick = lax.broadcasted_iota(jnp.int32, (width, lanes), 1) == z * width + lax.broadcasted_iota(
        jnp.int32, (width, lanes), 0
    )
    scale = jnp.sum(jnp.where(pick, skip_ref[pl.ds(x, 1), :], 0.0), axis=1, keepdims=True)
    spec_rows = z_ref.shape[0]
    gone = []
    turns = []

    def turn_x(k):
        for copy in gone[k]:
            copy.wait_recv()
        turns.extend(
            send(landed.at[k, :, xmod(d)], result_out.at[k, x], at_x(d)) for d in range(1, XS)
        )
        result_out[k, x] = landed[k, :, x]

    for k in range(4):
        which, c = divmod(k, 2)
        if c == 0:
            combine(spec_g, (spec_p, spec_f)[which], z_ref, inner)
        at, far = pl.ds(c * CHUNK, CHUNK), pl.ds(inner + c * CHUNK, CHUNK)
        values_z = z_ref[...]
        real = dot(values_z, ac_hi[:, at]) + dot(values_z, ac_lo[:, at])
        imag = dot(values_z, ac_hi[:, far]) + dot(values_z, ac_lo[:, far])
        real, imag = turned(real, imag, cos[:, at], sin[:, at])
        u_ref[:spec_rows, :] = real.astype(BF)
        u_ref[spec_rows:, :] = imag.astype(BF)
        u = u_ref[...]
        out = (dot(of_hi[...], u) + dot(of_lo[...], u)).reshape(leaving.shape[1:])
        if which == 1:
            out = out + scale * gated_in[:, :, :, at].astype(jnp.float32)
        leaving[k] = out.astype(BF)
        gone.append(
            [send(leaving.at[k, zmod(d)], landed.at[k, z], at_z(d)) for d in range(1, ZS)]
        )
        landed[k, z] = leaving[k, z]
        if k >= 2:
            turn_x(k - 2)
    turn_x(2)
    turn_x(3)
    for copy in homes + turns:
        copy.wait_recv()
    for copy in copies:
        copy.wait_send()


def layer(grad_out, out_weight, gate_in, gate_out, values, filters, skip_scale):
    rows, inner = gate_in.shape
    deep, wide = out_weight.shape
    width = rows // (ZS * XS)
    into, out_of, cos, sin, across = make_tables(ZS * XS, width, inner)
    tables = (*into, *out_of, cos, sin, *across)
    spec_rows = cos.shape[0]
    split = (XS, ZS, width, inner)
    parts = inner // CHUNK
    count = 122

    def vmem(shape, dtype=BF):
        return pltpu.VMEM(shape, dtype)

    spec = vmem((spec_rows, 2 * inner), jnp.float32)
    return pl.pallas_call(
        layer_kernel,
        out_shape=[
            jax.ShapeDtypeStruct((XS, deep, inner), BF),
            jax.ShapeDtypeStruct((2 * parts, XS, ZS, width, CHUNK), BF),
        ],
        in_specs=[pl.BlockSpec(memory_space=pl.ANY)] * 6
        + [VMEM]
        + [pl.BlockSpec(memory_space=pl.ANY)] * len(tables),
        out_specs=[VMEM] * 2,
        scratch_shapes=[
            vmem(split),
            vmem(split),
            vmem(split, jnp.float32),
            *[vmem(t.shape, t.dtype) for t in tables],
            vmem((ZS, deep, wide)),
            vmem((YS, deep, wide)),
            vmem((YS, deep, wide)),
            vmem((XS,) + grad_out.shape),
            vmem((XS,) + grad_out.shape),
            vmem((XS, deep, inner), jnp.float32),
            vmem((XS, 2, deep // 2, inner), jnp.float32),
            vmem((XS, 2, 2, deep // 2, inner)),
            vmem((XS, 2, 2, deep // 2, inner)),
            vmem((XS, 2, deep // 2, inner)),
            vmem((XS, 2, deep // 2, inner)),
            vmem((XS, deep, inner)),
            vmem((XS, deep, inner)),
            vmem((XS, ZS, width, inner)),
            vmem((ZS, XS, width, inner)),
            vmem((2,) + split),
            vmem((2, ZS, XS, width, inner)),
            vmem((2, ZS, XS, width, inner)),
            vmem((spec_rows, 2 * inner)),
            vmem((2 * spec_rows, CHUNK)),
            spec,
            spec,
            spec,
            vmem((2 * parts, ZS, XS, width, CHUNK)),
            vmem((2 * parts, ZS, XS, width, CHUNK)),
            pltpu.SemaphoreType.DMA((count,)),
            pltpu.SemaphoreType.DMA((count,)),
            pltpu.SemaphoreType.DMA((14,)),
        ],
        compiler_params=pltpu.CompilerParams(
            collective_id=0, has_side_effects=True, vmem_limit_bytes=58 * 1024 * 1024
        ),
        cost_estimate=pl.CostEstimate(flops=20 * 10**9, bytes_accessed=20 * 10**6, transcendentals=0),
    )(
        out_weight,
        grad_out,
        gate_in.reshape(split),
        values.reshape(split),
        gate_out.reshape(XS, deep, inner),
        filters.reshape(split),
        skip_scale.reshape(XS, deep),
        *tables,
    )


def shards(grad_out, out_weight, gate_in, gate_out, values, conv_out, filters, skip_scale):
    rows, inner = gate_in.shape
    home, result = layer(grad_out, out_weight, gate_in, gate_out, values, filters, skip_scale)
    back = home.reshape(rows, inner).astype(jnp.float32)
    grad_gate_out = (back * conv_out.astype(jnp.float32)).astype(BF)
    result = result.reshape(2, inner // CHUNK, rows, CHUNK).transpose(0, 2, 1, 3)
    result = result.reshape(2, rows, inner).astype(jnp.float32)
    grad_gate_in = (result[1] * values.astype(jnp.float32)).astype(BF)
    grad_values = (result[1] * gate_in.astype(jnp.float32)).astype(BF)
    return (grad_gate_in, grad_values, grad_gate_out, result[0])


def solution(mesh):
    placed = (
        P("seq", "ch"),
        P("seq", "ch"),
        P("ch", "seq"),
        P("ch", "seq"),
        P("ch", "seq"),
        P("ch", "seq"),
        P("ch", "seq"),
        P("ch"),
    )
    return jax.shard_map(
        shards,
        mesh=mesh,
        in_specs=placed,
        out_specs=(P("ch", "seq"), P("ch", "seq"), P("ch", "seq"), P("ch", "seq")),
        check_vma=False,
    )
```

```python
import functools

import jax
import jax.numpy as jnp
import ml_dtypes
import numpy as np
from jax import lax
from jax.experimental import pallas as pl
from jax.experimental.pallas import tpu as pltpu
from jax.sharding import PartitionSpec as P

OUTER = 64
CHUNK = 256


def split_pair(table):
    high = table.astype(np.float32).astype(ml_dtypes.bfloat16)
    low = (table - high.astype(np.float64)).astype(np.float32).astype(ml_dtypes.bfloat16)
    return high, low


def make_tables(blocks, width, inner):
    total = OUTER * inner
    half = OUTER // 2 + 1
    k = np.arange(half)
    a = np.arange(blocks)
    b = np.arange(inner)
    first = 2.0 * np.pi * (np.outer(k, a) % OUTER) / OUTER
    eye = np.eye(width)
    k_cos = np.kron(np.cos(first), eye)
    k_sin = np.kron(np.sin(first), eye)
    into = np.concatenate([k_cos, -k_sin], 0)
    weight = np.full((half, 1), 2.0)
    weight[0] = 1.0
    weight[-1] = 1.0
    weight = weight / total
    back_cos = np.kron((weight * np.cos(first)).T, eye)
    back_sin = np.kron((weight * np.sin(first)).T, eye)
    out_of = np.concatenate([back_cos, back_sin], 1)
    turn = 2.0 * np.pi * (np.outer(k, b) % total) / total
    turn = np.repeat(turn, width, axis=0)
    second = 2.0 * np.pi * (np.outer(b, b) % inner) / inner
    c, s = np.cos(second), np.sin(second)
    across = np.concatenate([np.concatenate([c, -s], 1), np.concatenate([s, c], 1)], 0)
    return (
        split_pair(into),
        split_pair(out_of),
        np.cos(turn).astype(np.float32),
        np.sin(turn).astype(np.float32),
        split_pair(across),
    )


def dot(left, right):
    return jnp.dot(left, right, preferred_element_type=jnp.float32)


def turned(real, imag, cos, sin):
    return real * cos + imag * sin, imag * cos - real * sin


ZS, XS, YS = 8, 4, 4
VMEM = pl.BlockSpec(memory_space=pltpu.VMEM)
MESH = pl.DeviceIdType.MESH
BF = jnp.bfloat16


def forward_pieces(block_of, into, twist, across, z_ref, out_ref):
    rows = z_ref.shape[0]
    inner = z_ref.shape[1] // 2

    def spread(c):
        at = pl.ds(c * CHUNK, CHUNK)
        block = block_of(at)
        y = sum(dot(table[...], block) for table in into)
        real, imag = turned(y[:rows], y[rows:], twist[0][:, at], twist[1][:, at])
        z_ref[:, at] = real.astype(BF)
        z_ref[:, pl.ds(inner + c * CHUNK, CHUNK)] = imag.astype(BF)

    def columns(c):
        at = pl.ds(c * CHUNK, CHUNK)
        z = z_ref[...]
        out_ref[:, at] = sum(dot(z, table[:, at]) for table in across)

    pieces = [functools.partial(spread, c) for c in range(inner // CHUNK)]
    pieces += [functools.partial(columns, c) for c in range(2 * inner // CHUNK)]
    return pieces


def combine(grad_ref, other_ref, z_ref, inner):
    @pl.loop(0, inner // CHUNK)
    def _(i):
        at = pl.ds(pl.multiple_of(i * CHUNK, CHUNK), CHUNK)
        far = pl.ds(pl.multiple_of(inner + i * CHUNK, CHUNK), CHUNK)
        g_re, g_im = grad_ref[:, at], grad_ref[:, far]
        o_re, o_im = other_ref[:, at], other_ref[:, far]
        z_ref[:, at] = (g_re * o_re + g_im * o_im).astype(BF)
        z_ref[:, far] = (g_re * o_im - g_im * o_re).astype(BF)


def layer_kernel(
    w_hbm, g_hbm, gate_in_hbm, values_hbm, gate_out_hbm, filters_hbm, skip_ref,
    in_hi_h, in_lo_h, of_hi_h, of_lo_h, cos_h, sin_h, ac_hi_h, ac_lo_h,
    home_out, filters_out, mixed_out,
    gate_in, values, filters, in_hi, in_lo, of_hi, of_lo, cos, sin, ac_hi, ac_lo,
    w_ring, w_mine, w_other, g_ring, g_other, own, hold, part, inbox, relay, final,
    near_gate, back_bf, gated, gated_in, stage, crossed, pair_in,
    z_ref, u_ref, spec_g, spec_p, spec_f, leaving, landed,
    send_sems, recv_sems, local_sems,
):
    s, h = lax.axis_index("seq"), lax.axis_index("ch")
    z, x = s // XS, s % XS
    y, core = h // 2, h % 2

    def zmod(d):
        return lax.rem(z + d + ZS, ZS)

    def xmod(d):
        return lax.rem(x + d + XS, XS)

    def at_z(d):
        return (zmod(d) * XS + x, h)

    def at_x(d):
        return (z * XS + xmod(d), h)

    def at_y(d):
        return (s, lax.rem(y + d + YS, YS) * 2 + core)

    sibling = (s, y * 2 + 1 - core)
    peers = [at_z(d) for d in range(1, ZS)] + [at_x(d) for d in range(1, XS)]
    peers += [at_y(d) for d in (1, -1)] + [sibling]

    barrier = pltpu.get_barrier_semaphore()
    for peer in peers:
        pl.semaphore_signal(barrier, inc=1, device_id=peer, device_id_type=MESH)

    loads = []

    def load(src, dst):
        copy = pltpu.make_async_copy(src, dst, local_sems.at[len(loads)])
        copy.start()
        loads.append(copy)
        return copy

    w_load = load(w_hbm, w_ring.at[z])
    g_load = load(g_hbm, g_ring.at[x])
    pair_loads = [load(gate_in_hbm, gate_in), load(values_hbm, values), load(filters_hbm, filters)]
    gate_load = load(gate_out_hbm.at[x], near_gate.at[0])
    table_loads = [
        load(src, dst)
        for src, dst in (
            (in_hi_h, in_hi), (in_lo_h, in_lo), (ac_hi_h, ac_hi), (ac_lo_h, ac_lo),
            (cos_h, cos), (sin_h, sin), (of_hi_h, of_hi), (of_lo_h, of_lo),
        )
    ]
    pl.semaphore_wait(barrier, len(peers))

    copies = []

    def send(src, dst, device):
        k = len(copies)
        copy = pltpu.make_async_remote_copy(
            src_ref=src, dst_ref=dst, send_sem=send_sems.at[k], recv_sem=recv_sems.at[k],
            device_id=device, device_id_type=MESH,
        )
        copy.start()
        copies.append(copy)
        return copy

    half_w = w_ring.shape[1] // 2
    half_g = g_ring.shape[1] // 2
    first, second = pl.ds(0, half_w), pl.ds(half_w, half_w)
    top, low = pl.ds(0, half_g), pl.ds(half_g, half_g)

    up = send(w_hbm, w_ring.at[z], at_z(1))
    down = send(w_hbm, w_ring.at[z], at_z(-1))
    right_top = send(g_hbm.at[top], g_ring.at[x, top], at_x(1))
    left_low = send(g_hbm.at[low], g_ring.at[x, low], at_x(-1))
    right_low = send(g_hbm.at[low], g_ring.at[x, low], at_x(1))
    left_top = send(g_hbm.at[top], g_ring.at[x, top], at_x(-1))
    shared = [send(g_hbm, g_other.at[0], sibling)]
    for copy in pair_loads:
        copy.wait()
    for i in range(XS):
        product = gate_in[i].astype(jnp.float32) * values[i].astype(jnp.float32)
        stage[0, i] = product.astype(BF)
        stage[1, i] = filters[i].astype(BF)

    up.wait_recv()
    up = send(w_ring.at[zmod(-1)], w_ring.at[zmod(-1)], at_z(1))
    down.wait_recv()
    down = send(w_ring.at[zmod(1)], w_ring.at[zmod(1)], at_z(-1))
    right_top.wait_recv()
    far_top = send(g_ring.at[xmod(-1), top], g_ring.at[xmod(-1), top], at_x(1))
    left_low.wait_recv()
    far_low = send(g_ring.at[xmod(1), low], g_ring.at[xmod(1), low], at_x(-1))
    gates = [send(gate_out_hbm.at[xmod(d)], near_gate.at[d], at_x(d)) for d in range(1, XS)]
    up.wait_recv()
    up = send(w_ring.at[zmod(-2)], w_ring.at[zmod(-2)], at_z(1))
    down.wait_recv()
    down = send(w_ring.at[zmod(2)], w_ring.at[zmod(2)], at_z(-1))
    over_z = {}
    over_x = {}

    def pair_z(i):
        over_z[i] = [
            send(stage.at[i, :, zmod(d)], crossed.at[i, z], at_z(d)) for d in range(1, ZS)
        ]
        crossed[i, z] = stage[i, :, z]

    def pair_x(i):
        for copy in over_z[i]:
            copy.wait_recv()
        over_x[i] = [
            send(crossed.at[i, :, xmod(d)], pair_in.at[i, :, x], at_x(d)) for d in range(1, XS)
        ]
        pair_in[i, :, x] = crossed[i, :, x]

    pair_z(1)
    up.wait_recv()
    up = send(w_ring.at[zmod(-3), first], w_ring.at[zmod(-3), first], at_z(1))
    down.wait_recv()
    down = send(w_ring.at[zmod(3), second], w_ring.at[zmod(3), second], at_z(-1))
    w_load.wait()
    g_load.wait()
    up.wait_recv()
    down.wait_recv()
    pair_z(0)

    def rows_for(d, of_core):
        return lax.rem(y + d, YS) * 2 + of_core

    w_shared = [
        send(w_ring.at[rows_for(d, 1 - core)], w_other.at[d], sibling) for d in range(YS)
    ]
    for d in range(YS):
        w_mine[d] = w_ring[rows_for(d, core)]
    right_low.wait_recv()
    shared.append(send(g_ring.at[xmod(-1)], g_other.at[1], sibling))
    left_top.wait_recv()
    shared.append(send(g_ring.at[xmod(1)], g_other.at[2], sibling))
    for copy in w_shared:
        copy.wait_recv()

    offsets = (0, -1, 1, 2)
    parts = []
    passed = []
    deep = w_ring.shape[1]
    wide = (YS * deep, w_ring.shape[2])

    def pass_on(n):
        for side in range(2):
            parts[n][side].wait_recv()
            relay[n, side] = (hold[n, side] + inbox[n, side, 0].astype(jnp.float32)).astype(BF)
            passed.append(send(relay.at[n, side], final.at[n, side], at_y(1 - 2 * side)))

    for n, off in enumerate(offsets):
        if n == 3:
            far_top.wait_recv()
            far_low.wait_recv()
            shared.append(send(g_ring.at[xmod(2)], g_other.at[3], sibling))
        shared[n].wait_recv()

        @pl.loop(0, g_ring.shape[1] // CHUNK)
        def _(i, n=n, off=off):
            at = pl.ds(pl.multiple_of(i * CHUNK, CHUNK), CHUNK)
            form = (((1,), (1,)), ((), ()))
            total = lax.dot_general(
                w_mine[...].reshape(wide), g_ring[xmod(off), at, :], form,
                preferred_element_type=jnp.float32,
            ) + lax.dot_general(
                w_other[...].reshape(wide), g_other[n, at, :], form,
                preferred_element_type=jnp.float32,
            )
            total = total.reshape(YS, deep, CHUNK)
            own[n, :, at] = total[0]
            hold[n, 0, :, at] = total[1, :half_w]
            hold[n, 1, :, at] = total[3, half_w:]
            part[n, 0, 0, :, at] = total[2, :half_w].astype(BF)
            part[n, 0, 1, :, at] = total[1, half_w:].astype(BF)
            part[n, 1, 0, :, at] = total[2, half_w:].astype(BF)
            part[n, 1, 1, :, at] = total[3, :half_w].astype(BF)

        parts.append([send(part.at[n, side], inbox.at[n, side], at_y(1 - 2 * side)) for side in range(2)])

    arrivals = []
    homes = []

    def total_up(n):
        off = offsets[n]
        for copy in passed[2 * n : 2 * n + 2]:
            copy.wait_recv()
        d = -off % XS
        if d:
            gates[d - 1].wait_recv()
        else:
            gate_load.wait()
        upper = own[n, :half_w] + final[n, 0].astype(jnp.float32) + inbox[n, 1, 1].astype(jnp.float32)
        lower = own[n, half_w:] + final[n, 1].astype(jnp.float32) + inbox[n, 0, 1].astype(jnp.float32)
        back = jnp.concatenate([upper, lower], 0)
        result = back * near_gate[d].astype(jnp.float32)
        gated[n] = result.astype(BF).reshape(gated.shape[1:])
        for d in range(1, ZS):
            arrivals.append(send(gated.at[n, zmod(d)], gated_in.at[z, xmod(off)], at_z(d)))
        gated_in[z, xmod(off)] = gated[n, z]
        back_bf[n] = back.astype(BF)

    inner = g_ring.shape[2]
    rows = g_ring.shape[1]
    into, twist, across = (in_hi, in_lo), (cos, sin), (ac_hi, ac_lo)

    def pair_block(i):
        return lambda at: pair_in[i, :, :, :, at].reshape(rows, CHUNK)

    pass_on(0)
    pass_on(1)
    pair_x(1)
    pass_on(2)
    total_up(0)
    pass_on(3)
    total_up(1)
    for copy in table_loads:
        copy.wait()
    for copy in over_x[1]:
        copy.wait_recv()
    pieces = forward_pieces(pair_block(1), into, twist, across, z_ref, spec_f)
    for piece in pieces[:2]:
        piece()
    total_up(2)
    pieces[2]()
    total_up(3)
    pair_x(0)
    for piece in pieces[3:]:
        piece()
    for copy in over_x[0]:
        copy.wait_recv()
    for piece in forward_pieces(pair_block(0), into, twist, across, z_ref, spec_p):
        piece()
    home_out[x] = back_bf[0]
    for n, off in enumerate(offsets):
        if n:
            homes.append(send(back_bf.at[n], home_out.at[x], at_x(off)))
    for copy in arrivals:
        copy.wait_recv()
    for piece in forward_pieces(
        lambda at: gated_in[:, :, :, at].reshape(rows, CHUNK), into, twist, across[:1], z_ref, spec_g
    ):
        piece()

    width = gated_in.shape[2]
    lanes = skip_ref.shape[1]
    pick = lax.broadcasted_iota(jnp.int32, (width, lanes), 1) == z * width + lax.broadcasted_iota(
        jnp.int32, (width, lanes), 0
    )
    scale = jnp.sum(jnp.where(pick, skip_ref[pl.ds(x, 1), :], 0.0), axis=1, keepdims=True)
    spec_rows = z_ref.shape[0]
    gone = []
    turns = []

    def turn_x(k):
        for copy in gone[k]:
            copy.wait_recv()
        which, c = divmod(k, 2)
        result = (filters_out, mixed_out)[which]
        at = pl.ds(c * CHUNK, CHUNK)
        turns.extend(
            send(landed.at[k, :, xmod(d)], result.at[x, :, :, at], at_x(d))
            for d in range(1, XS)
        )
        result[x, :, :, at] = landed[k, :, x]

    for k in range(4):
        which, c = divmod(k, 2)
        if c == 0:
            combine(spec_g, (spec_p, spec_f)[which], z_ref, inner)
        at, far = pl.ds(c * CHUNK, CHUNK), pl.ds(inner + c * CHUNK, CHUNK)
        values_z = z_ref[...]
        real = dot(values_z, ac_hi[:, at]) + dot(values_z, ac_lo[:, at])
        imag = dot(values_z, ac_hi[:, far]) + dot(values_z, ac_lo[:, far])
        real, imag = turned(real, imag, cos[:, at], sin[:, at])
        u_ref[:spec_rows, :] = real.astype(BF)
        u_ref[spec_rows:, :] = imag.astype(BF)
        u = u_ref[...]
        out = (dot(of_hi[...], u) + dot(of_lo[...], u)).reshape(leaving.shape[1:])
        if which == 1:
            out = out + scale * gated_in[:, :, :, at].astype(jnp.float32)
        leaving[k] = out.astype(BF)
        gone.append(
            [send(leaving.at[k, zmod(d)], landed.at[k, z], at_z(d)) for d in range(1, ZS)]
        )
        landed[k, z] = leaving[k, z]
        if k >= 2:
            turn_x(k - 2)
    turn_x(2)
    turn_x(3)
    for copy in homes + turns:
        copy.wait_recv()
    for copy in copies:
        copy.wait_send()


def layer(grad_out, out_weight, gate_in, gate_out, values, filters, skip_scale):
    rows, inner = gate_in.shape
    deep, wide = out_weight.shape
    width = rows // (ZS * XS)
    into, out_of, cos, sin, across = make_tables(ZS * XS, width, inner)
    tables = (*into, *out_of, cos, sin, *across)
    spec_rows = cos.shape[0]
    split = (XS, ZS, width, inner)
    parts = inner // CHUNK
    count = 132

    def vmem(shape, dtype=BF):
        return pltpu.VMEM(shape, dtype)

    spec = vmem((spec_rows, 2 * inner), jnp.float32)
    return pl.pallas_call(
        layer_kernel,
        out_shape=[
            jax.ShapeDtypeStruct((XS, deep, inner), BF),
            jax.ShapeDtypeStruct(split, BF),
            jax.ShapeDtypeStruct(split, BF),
        ],
        in_specs=[pl.BlockSpec(memory_space=pl.ANY)] * 6
        + [VMEM]
        + [pl.BlockSpec(memory_space=pl.ANY)] * len(tables),
        out_specs=[VMEM] * 3,
        scratch_shapes=[
            vmem(split),
            vmem(split),
            vmem(split, jnp.float32),
            *[vmem(t.shape, t.dtype) for t in tables],
            vmem((ZS, deep, wide)),
            vmem((YS, deep, wide)),
            vmem((YS, deep, wide)),
            vmem((XS,) + grad_out.shape),
            vmem((XS,) + grad_out.shape),
            vmem((XS, deep, inner), jnp.float32),
            vmem((XS, 2, deep // 2, inner), jnp.float32),
            vmem((XS, 2, 2, deep // 2, inner)),
            vmem((XS, 2, 2, deep // 2, inner)),
            vmem((XS, 2, deep // 2, inner)),
            vmem((XS, 2, deep // 2, inner)),
            vmem((XS, deep, inner)),
            vmem((XS, deep, inner)),
            vmem((XS, ZS, width, inner)),
            vmem((ZS, XS, width, inner)),
            vmem((2,) + split),
            vmem((2, ZS, XS, width, inner)),
            vmem((2, ZS, XS, width, inner)),
            vmem((spec_rows, 2 * inner)),
            vmem((2 * spec_rows, CHUNK)),
            spec,
            spec,
            spec,
            vmem((2 * parts, ZS, XS, width, CHUNK)),
            vmem((2 * parts, ZS, XS, width, CHUNK)),
            pltpu.SemaphoreType.DMA((count,)),
            pltpu.SemaphoreType.DMA((count,)),
            pltpu.SemaphoreType.DMA((14,)),
        ],
        compiler_params=pltpu.CompilerParams(
            collective_id=0, has_side_effects=True, vmem_limit_bytes=58 * 1024 * 1024
        ),
        cost_estimate=pl.CostEstimate(flops=20 * 10**9, bytes_accessed=20 * 10**6, transcendentals=0),
    )(
        out_weight,
        grad_out,
        gate_in.reshape(split),
        values.reshape(split),
        gate_out.reshape(XS, deep, inner),
        filters.reshape(split),
        skip_scale.reshape(XS, deep),
        *tables,
    )


def shards(grad_out, out_weight, gate_in, gate_out, values, conv_out, filters, skip_scale):
    rows, inner = gate_in.shape
    home, grad_filters, mixed = layer(
        grad_out, out_weight, gate_in, gate_out, values, filters, skip_scale
    )

    def wide(block):
        return block.reshape(rows, inner).astype(jnp.float32)

    grad_gate_out = (wide(home) * wide(conv_out)).astype(BF)
    grad_gate_in = (wide(mixed) * wide(values)).astype(BF)
    grad_values = (wide(mixed) * wide(gate_in)).astype(BF)
    return (grad_gate_in, grad_values, grad_gate_out, wide(grad_filters))


def solution(mesh):
    placed = (
        P("seq", "ch"),
        P("seq", "ch"),
        P("ch", "seq"),
        P("ch", "seq"),
        P("ch", "seq"),
        P("ch", "seq"),
        P("ch", "seq"),
        P("ch"),
    )
    return jax.shard_map(
        shards,
        mesh=mesh,
        in_specs=placed,
        out_specs=(P("ch", "seq"), P("ch", "seq"), P("ch", "seq"), P("ch", "seq")),
        check_vma=False,
    )
```

```python
import functools

import jax
import jax.numpy as jnp
import ml_dtypes
import numpy as np
from jax import lax
from jax.experimental import pallas as pl
from jax.experimental.pallas import tpu as pltpu
from jax.sharding import PartitionSpec as P

OUTER = 64
CHUNK = 256


def split_pair(table):
    high = table.astype(np.float32).astype(ml_dtypes.bfloat16)
    low = (table - high.astype(np.float64)).astype(np.float32).astype(ml_dtypes.bfloat16)
    return high, low


def make_tables(blocks, width, inner):
    total = OUTER * inner
    half = OUTER // 2 + 1
    k = np.arange(half)
    a = np.arange(blocks)
    b = np.arange(inner)
    first = 2.0 * np.pi * (np.outer(k, a) % OUTER) / OUTER
    eye = np.eye(width)
    k_cos = np.kron(np.cos(first), eye)
    k_sin = np.kron(np.sin(first), eye)
    into = np.concatenate([k_cos, -k_sin], 0)
    weight = np.full((half, 1), 2.0)
    weight[0] = 1.0
    weight[-1] = 1.0
    weight = weight / total
    back_cos = np.kron((weight * np.cos(first)).T, eye)
    back_sin = np.kron((weight * np.sin(first)).T, eye)
    out_of = np.concatenate([back_cos, back_sin], 1)
    turn = 2.0 * np.pi * (np.outer(k, b) % total) / total
    turn = np.repeat(turn, width, axis=0)
    second = 2.0 * np.pi * (np.outer(b, b) % inner) / inner
    c, s = np.cos(second), np.sin(second)
    across = np.concatenate([np.concatenate([c, -s], 1), np.concatenate([s, c], 1)], 0)
    return (
        split_pair(into),
        split_pair(out_of),
        np.cos(turn).astype(np.float32),
        np.sin(turn).astype(np.float32),
        split_pair(across),
    )


def dot(left, right):
    return jnp.dot(left, right, preferred_element_type=jnp.float32)


def turned(real, imag, cos, sin):
    return real * cos + imag * sin, imag * cos - real * sin


ZS, XS, YS = 8, 4, 4
VMEM = pl.BlockSpec(memory_space=pltpu.VMEM)
MESH = pl.DeviceIdType.MESH
BF = jnp.bfloat16


def forward_pieces(block_of, into, twist, across, z_ref, out_ref):
    rows = z_ref.shape[0]
    inner = z_ref.shape[1] // 2

    def spread(c):
        at = pl.ds(c * CHUNK, CHUNK)
        block = block_of(at)
        y = sum(dot(table[...], block) for table in into)
        real, imag = turned(y[:rows], y[rows:], twist[0][:, at], twist[1][:, at])
        z_ref[:, at] = real.astype(BF)
        z_ref[:, pl.ds(inner + c * CHUNK, CHUNK)] = imag.astype(BF)

    def columns(c):
        at = pl.ds(c * CHUNK, CHUNK)
        z = z_ref[...]
        out_ref[:, at] = sum(dot(z, table[:, at]) for table in across)

    pieces = [functools.partial(spread, c) for c in range(inner // CHUNK)]
    pieces += [functools.partial(columns, c) for c in range(2 * inner // CHUNK)]
    return pieces


def combine(grad_ref, other_ref, z_ref, inner):
    @pl.loop(0, inner // CHUNK)
    def _(i):
        at = pl.ds(pl.multiple_of(i * CHUNK, CHUNK), CHUNK)
        far = pl.ds(pl.multiple_of(inner + i * CHUNK, CHUNK), CHUNK)
        g_re, g_im = grad_ref[:, at], grad_ref[:, far]
        o_re, o_im = other_ref[:, at], other_ref[:, far]
        z_ref[:, at] = (g_re * o_re + g_im * o_im).astype(BF)
        z_ref[:, far] = (g_re * o_im - g_im * o_re).astype(BF)


def layer_kernel(
    w_hbm, g_hbm, gate_in_hbm, values_hbm, gate_out_hbm, filters_hbm, skip_ref,
    in_hi_h, in_lo_h, of_hi_h, of_lo_h, cos_h, sin_h, ac_hi_h, ac_lo_h,
    home_out, filters_out, mixed_out,
    gate_in, values, filters, in_hi, in_lo, of_hi, of_lo, cos, sin, ac_hi, ac_lo,
    w_ring, w_mine, w_other, g_ring, g_other, own, hold, part, inbox, relay, final,
    near_gate, back_bf, gated, gated_in, stage, crossed, pair_in,
    z_ref, u_ref, spec_g, spec_p, spec_f, leaving, landed,
    send_sems, recv_sems, local_sems,
):
    s, h = lax.axis_index("seq"), lax.axis_index("ch")
    z, x = s // XS, s % XS
    y, core = h // 2, h % 2

    def zmod(d):
        return lax.rem(z + d + ZS, ZS)

    def xmod(d):
        return lax.rem(x + d + XS, XS)

    def at_z(d):
        return (zmod(d) * XS + x, h)

    def at_x(d):
        return (z * XS + xmod(d), h)

    def at_y(d):
        return (s, lax.rem(y + d + YS, YS) * 2 + core)

    sibling = (s, y * 2 + 1 - core)
    peers = [at_z(d) for d in range(1, ZS)] + [at_x(d) for d in range(1, XS)]
    peers += [at_y(d) for d in (1, -1)] + [sibling]

    barrier = pltpu.get_barrier_semaphore()
    for peer in peers:
        pl.semaphore_signal(barrier, inc=1, device_id=peer, device_id_type=MESH)

    loads = []

    def load(src, dst):
        copy = pltpu.make_async_copy(src, dst, local_sems.at[len(loads)])
        copy.start()
        loads.append(copy)
        return copy

    w_load = load(w_hbm, w_ring.at[z])
    g_load = load(g_hbm, g_ring.at[x])
    pair_loads = [load(gate_in_hbm, gate_in), load(values_hbm, values), load(filters_hbm, filters)]
    gate_load = load(gate_out_hbm.at[x], near_gate.at[0])
    table_loads = [
        load(src, dst)
        for src, dst in (
            (in_hi_h, in_hi), (in_lo_h, in_lo), (ac_hi_h, ac_hi), (ac_lo_h, ac_lo),
            (cos_h, cos), (sin_h, sin), (of_hi_h, of_hi), (of_lo_h, of_lo),
        )
    ]
    pl.semaphore_wait(barrier, len(peers))

    copies = []

    def send(src, dst, device):
        k = len(copies)
        copy = pltpu.make_async_remote_copy(
            src_ref=src, dst_ref=dst, send_sem=send_sems.at[k], recv_sem=recv_sems.at[k],
            device_id=device, device_id_type=MESH,
        )
        copy.start()
        copies.append(copy)
        return copy

    half_w = w_ring.shape[1] // 2
    half_g = g_ring.shape[1] // 2
    first, second = pl.ds(0, half_w), pl.ds(half_w, half_w)
    top, low = pl.ds(0, half_g), pl.ds(half_g, half_g)

    up = send(w_hbm, w_ring.at[z], at_z(1))
    down = send(w_hbm, w_ring.at[z], at_z(-1))
    right_top = send(g_hbm.at[top], g_ring.at[x, top], at_x(1))
    left_low = send(g_hbm.at[low], g_ring.at[x, low], at_x(-1))
    right_low = send(g_hbm.at[low], g_ring.at[x, low], at_x(1))
    left_top = send(g_hbm.at[top], g_ring.at[x, top], at_x(-1))
    shared = [send(g_hbm, g_other.at[0], sibling)]
    for copy in pair_loads:
        copy.wait()
    for i in range(XS):
        product = gate_in[i].astype(jnp.float32) * values[i].astype(jnp.float32)
        stage[0, i] = product.astype(BF)
        stage[1, i] = filters[i].astype(BF)

    up.wait_recv()
    up = send(w_ring.at[zmod(-1)], w_ring.at[zmod(-1)], at_z(1))
    down.wait_recv()
    down = send(w_ring.at[zmod(1)], w_ring.at[zmod(1)], at_z(-1))
    right_top.wait_recv()
    far_top = send(g_ring.at[xmod(-1), top], g_ring.at[xmod(-1), top], at_x(1))
    left_low.wait_recv()
    far_low = send(g_ring.at[xmod(1), low], g_ring.at[xmod(1), low], at_x(-1))
    gates = [send(gate_out_hbm.at[xmod(d)], near_gate.at[d], at_x(d)) for d in range(1, XS)]
    up.wait_recv()
    up = send(w_ring.at[zmod(-2)], w_ring.at[zmod(-2)], at_z(1))
    down.wait_recv()
    down = send(w_ring.at[zmod(2)], w_ring.at[zmod(2)], at_z(-1))
    over_z = {}
    over_x = {}

    def pair_z(i, start, size):
        at = pl.ds(start, size)
        over_z.setdefault(i, []).extend(
            send(stage.at[i, at, zmod(d)], crossed.at[i, z, at], at_z(d)) for d in range(1, ZS)
        )
        crossed[i, z, at] = stage[i, at, z]

    def pair_x(i):
        for copy in over_z[i]:
            copy.wait_recv()
        over_x[i] = [
            send(crossed.at[i, :, xmod(d)], pair_in.at[i, :, x], at_x(d)) for d in range(1, XS)
        ]
        pair_in[i, :, x] = crossed[i, :, x]

    pair_z(1, 0, XS)
    up.wait_recv()
    up = send(w_ring.at[zmod(-3), first], w_ring.at[zmod(-3), first], at_z(1))
    down.wait_recv()
    down = send(w_ring.at[zmod(3), second], w_ring.at[zmod(3), second], at_z(-1))
    w_load.wait()
    g_load.wait()
    up.wait_recv()
    down.wait_recv()
    pair_z(0, 0, XS // 2)

    def rows_for(d, of_core):
        return lax.rem(y + d, YS) * 2 + of_core

    w_shared = [
        send(w_ring.at[rows_for(d, 1 - core)], w_other.at[d], sibling) for d in range(YS)
    ]
    for d in range(YS):
        w_mine[d] = w_ring[rows_for(d, core)]
    right_low.wait_recv()
    shared.append(send(g_ring.at[xmod(-1)], g_other.at[1], sibling))
    left_top.wait_recv()
    shared.append(send(g_ring.at[xmod(1)], g_other.at[2], sibling))
    for copy in w_shared:
        copy.wait_recv()

    offsets = (0, -1, 1, 2)
    parts = []
    passed = []
    deep = w_ring.shape[1]
    wide = (YS * deep, w_ring.shape[2])

    def pass_on(n):
        for side in range(2):
            parts[n][side].wait_recv()
            relay[n, side] = (hold[n, side] + inbox[n, side, 0].astype(jnp.float32)).astype(BF)
            passed.append(send(relay.at[n, side], final.at[n, side], at_y(1 - 2 * side)))

    for n, off in enumerate(offsets):
        if n == 3:
            far_top.wait_recv()
            far_low.wait_recv()
            shared.append(send(g_ring.at[xmod(2)], g_other.at[3], sibling))
        shared[n].wait_recv()

        @pl.loop(0, g_ring.shape[1] // CHUNK)
        def _(i, n=n, off=off):
            at = pl.ds(pl.multiple_of(i * CHUNK, CHUNK), CHUNK)
            form = (((1,), (1,)), ((), ()))
            total = lax.dot_general(
                w_mine[...].reshape(wide), g_ring[xmod(off), at, :], form,
                preferred_element_type=jnp.float32,
            ) + lax.dot_general(
                w_other[...].reshape(wide), g_other[n, at, :], form,
                preferred_element_type=jnp.float32,
            )
            total = total.reshape(YS, deep, CHUNK)
            own[n, :, at] = total[0]
            hold[n, 0, :, at] = total[1, :half_w]
            hold[n, 1, :, at] = total[3, half_w:]
            part[n, 0, 0, :, at] = total[2, :half_w].astype(BF)
            part[n, 0, 1, :, at] = total[1, half_w:].astype(BF)
            part[n, 1, 0, :, at] = total[2, half_w:].astype(BF)
            part[n, 1, 1, :, at] = total[3, :half_w].astype(BF)

        parts.append([send(part.at[n, side], inbox.at[n, side], at_y(1 - 2 * side)) for side in range(2)])

    arrivals = []
    homes = []

    def total_up(n):
        off = offsets[n]
        for copy in passed[2 * n : 2 * n + 2]:
            copy.wait_recv()
        d = -off % XS
        if d:
            gates[d - 1].wait_recv()
        else:
            gate_load.wait()
        upper = own[n, :half_w] + final[n, 0].astype(jnp.float32) + inbox[n, 1, 1].astype(jnp.float32)
        lower = own[n, half_w:] + final[n, 1].astype(jnp.float32) + inbox[n, 0, 1].astype(jnp.float32)
        back = jnp.concatenate([upper, lower], 0)
        result = back * near_gate[d].astype(jnp.float32)
        gated[n] = result.astype(BF).reshape(gated.shape[1:])
        for d in range(1, ZS):
            arrivals.append(send(gated.at[n, zmod(d)], gated_in.at[z, xmod(off)], at_z(d)))
        gated_in[z, xmod(off)] = gated[n, z]
        back_bf[n] = back.astype(BF)

    inner = g_ring.shape[2]
    rows = g_ring.shape[1]
    into, twist, across = (in_hi, in_lo), (cos, sin), (ac_hi, ac_lo)

    def pair_block(i):
        return lambda at: pair_in[i, :, :, :, at].reshape(rows, CHUNK)

    pass_on(0)
    pass_on(1)
    pair_x(1)
    pass_on(2)
    total_up(0)
    pass_on(3)
    total_up(1)
    for copy in table_loads:
        copy.wait()
    for copy in over_x[1]:
        copy.wait_recv()
    pieces = forward_pieces(pair_block(1), into, twist, across, z_ref, spec_f)
    for piece in pieces[:2]:
        piece()
    total_up(2)
    pieces[2]()
    total_up(3)
    pair_z(0, XS // 2, XS // 2)
    for piece in pieces[3:]:
        piece()
    home_out[x] = back_bf[0]
    for copy in arrivals:
        copy.wait_recv()
    for piece in forward_pieces(
        lambda at: gated_in[:, :, :, at].reshape(rows, CHUNK), into, twist, across[:1], z_ref, spec_g
    ):
        piece()

    width = gated_in.shape[2]
    lanes = skip_ref.shape[1]
    pick = lax.broadcasted_iota(jnp.int32, (width, lanes), 1) == z * width + lax.broadcasted_iota(
        jnp.int32, (width, lanes), 0
    )
    scale = jnp.sum(jnp.where(pick, skip_ref[pl.ds(x, 1), :], 0.0), axis=1, keepdims=True)
    spec_rows = z_ref.shape[0]
    gone = []
    turns = []

    def turn_x(k):
        for copy in gone[k]:
            copy.wait_recv()
        which, c = divmod(k, 2)
        result = (mixed_out, filters_out)[which]
        at = pl.ds(c * CHUNK, CHUNK)
        turns.extend(
            send(landed.at[k, :, xmod(d)], result.at[x, :, :, at], at_x(d))
            for d in range(1, XS)
        )
        result[x, :, :, at] = landed[k, :, x]

    def leave(k):
        which, c = divmod(k, 2)
        if c == 0:
            combine(spec_g, (spec_f, spec_p)[which], z_ref, inner)
        at, far = pl.ds(c * CHUNK, CHUNK), pl.ds(inner + c * CHUNK, CHUNK)
        values_z = z_ref[...]
        real = dot(values_z, ac_hi[:, at]) + dot(values_z, ac_lo[:, at])
        imag = dot(values_z, ac_hi[:, far]) + dot(values_z, ac_lo[:, far])
        real, imag = turned(real, imag, cos[:, at], sin[:, at])
        u_ref[:spec_rows, :] = real.astype(BF)
        u_ref[spec_rows:, :] = imag.astype(BF)
        u = u_ref[...]
        out = (dot(of_hi[...], u) + dot(of_lo[...], u)).reshape(leaving.shape[1:])
        if which == 0:
            out = out + scale * gated_in[:, :, :, at].astype(jnp.float32)
        leaving[k] = out.astype(BF)
        gone.append(
            [send(leaving.at[k, zmod(d)], landed.at[k, z], at_z(d)) for d in range(1, ZS)]
        )
        landed[k, z] = leaving[k, z]

    leave(0)
    pair_x(0)
    leave(1)
    for n, off in enumerate(offsets):
        if n:
            homes.append(send(back_bf.at[n], home_out.at[x], at_x(off)))
    for copy in over_x[0]:
        copy.wait_recv()
    for piece in forward_pieces(pair_block(0), into, twist, across, z_ref, spec_p):
        piece()
    leave(2)
    turn_x(0)
    leave(3)
    turn_x(1)
    turn_x(2)
    turn_x(3)
    for copy in homes + turns:
        copy.wait_recv()
    for copy in copies:
        copy.wait_send()


def layer(grad_out, out_weight, gate_in, gate_out, values, filters, skip_scale):
    rows, inner = gate_in.shape
    deep, wide = out_weight.shape
    width = rows // (ZS * XS)
    into, out_of, cos, sin, across = make_tables(ZS * XS, width, inner)
    tables = (*into, *out_of, cos, sin, *across)
    spec_rows = cos.shape[0]
    split = (XS, ZS, width, inner)
    parts = inner // CHUNK
    count = 139

    def vmem(shape, dtype=BF):
        return pltpu.VMEM(shape, dtype)

    spec = vmem((spec_rows, 2 * inner), jnp.float32)
    return pl.pallas_call(
        layer_kernel,
        out_shape=[
            jax.ShapeDtypeStruct((XS, deep, inner), BF),
            jax.ShapeDtypeStruct(split, BF),
            jax.ShapeDtypeStruct(split, BF),
        ],
        in_specs=[pl.BlockSpec(memory_space=pl.ANY)] * 6
        + [VMEM]
        + [pl.BlockSpec(memory_space=pl.ANY)] * len(tables),
        out_specs=[VMEM] * 3,
        scratch_shapes=[
            vmem(split),
            vmem(split),
            vmem(split, jnp.float32),
            *[vmem(t.shape, t.dtype) for t in tables],
            vmem((ZS, deep, wide)),
            vmem((YS, deep, wide)),
            vmem((YS, deep, wide)),
            vmem((XS,) + grad_out.shape),
            vmem((XS,) + grad_out.shape),
            vmem((XS, deep, inner), jnp.float32),
            vmem((XS, 2, deep // 2, inner), jnp.float32),
            vmem((XS, 2, 2, deep // 2, inner)),
            vmem((XS, 2, 2, deep // 2, inner)),
            vmem((XS, 2, deep // 2, inner)),
            vmem((XS, 2, deep // 2, inner)),
            vmem((XS, deep, inner)),
            vmem((XS, deep, inner)),
            vmem((XS, ZS, width, inner)),
            vmem((ZS, XS, width, inner)),
            vmem((2,) + split),
            vmem((2, ZS, XS, width, inner)),
            vmem((2, ZS, XS, width, inner)),
            vmem((spec_rows, 2 * inner)),
            vmem((2 * spec_rows, CHUNK)),
            spec,
            spec,
            spec,
            vmem((2 * parts, ZS, XS, width, CHUNK)),
            vmem((2 * parts, ZS, XS, width, CHUNK)),
            pltpu.SemaphoreType.DMA((count,)),
            pltpu.SemaphoreType.DMA((count,)),
            pltpu.SemaphoreType.DMA((14,)),
        ],
        compiler_params=pltpu.CompilerParams(
            collective_id=0, has_side_effects=True, vmem_limit_bytes=58 * 1024 * 1024
        ),
        cost_estimate=pl.CostEstimate(flops=20 * 10**9, bytes_accessed=20 * 10**6, transcendentals=0),
    )(
        out_weight,
        grad_out,
        gate_in.reshape(split),
        values.reshape(split),
        gate_out.reshape(XS, deep, inner),
        filters.reshape(split),
        skip_scale.reshape(XS, deep),
        *tables,
    )


def shards(grad_out, out_weight, gate_in, gate_out, values, conv_out, filters, skip_scale):
    rows, inner = gate_in.shape
    home, grad_filters, mixed = layer(
        grad_out, out_weight, gate_in, gate_out, values, filters, skip_scale
    )

    def wide(block):
        return block.reshape(rows, inner).astype(jnp.float32)

    grad_gate_out = (wide(home) * wide(conv_out)).astype(BF)
    grad_gate_in = (wide(mixed) * wide(values)).astype(BF)
    grad_values = (wide(mixed) * wide(gate_in)).astype(BF)
    return (grad_gate_in, grad_values, grad_gate_out, wide(grad_filters))


def solution(mesh):
    placed = (
        P("seq", "ch"),
        P("seq", "ch"),
        P("ch", "seq"),
        P("ch", "seq"),
        P("ch", "seq"),
        P("ch", "seq"),
        P("ch", "seq"),
        P("ch"),
    )
    return jax.shard_map(
        shards,
        mesh=mesh,
        in_specs=placed,
        out_specs=(P("ch", "seq"), P("ch", "seq"), P("ch", "seq"), P("ch", "seq")),
        check_vma=False,
    )
```

```python
import functools

import jax
import jax.numpy as jnp
import ml_dtypes
import numpy as np
from jax import lax
from jax.experimental import pallas as pl
from jax.experimental.pallas import tpu as pltpu
from jax.sharding import PartitionSpec as P

OUTER = 64
CHUNK = 256


def split_pair(table):
    high = table.astype(np.float32).astype(ml_dtypes.bfloat16)
    low = (table - high.astype(np.float64)).astype(np.float32).astype(ml_dtypes.bfloat16)
    return high, low


def make_tables(blocks, width, inner):
    total = OUTER * inner
    half = OUTER // 2 + 1
    k = np.arange(half)
    a = np.arange(blocks)
    b = np.arange(inner)
    first = 2.0 * np.pi * (np.outer(k, a) % OUTER) / OUTER
    eye = np.eye(width)
    k_cos = np.kron(np.cos(first), eye)
    k_sin = np.kron(np.sin(first), eye)
    into = np.concatenate([k_cos, -k_sin], 0)
    weight = np.full((half, 1), 2.0)
    weight[0] = 1.0
    weight[-1] = 1.0
    weight = weight / total
    back_cos = np.kron((weight * np.cos(first)).T, eye)
    back_sin = np.kron((weight * np.sin(first)).T, eye)
    out_of = np.concatenate([back_cos, back_sin], 1)
    turn = 2.0 * np.pi * (np.outer(k, b) % total) / total
    turn = np.repeat(turn, width, axis=0)
    second = 2.0 * np.pi * (np.outer(b, b) % inner) / inner
    c, s = np.cos(second), np.sin(second)
    across = np.concatenate([np.concatenate([c, -s], 1), np.concatenate([s, c], 1)], 0)
    return (
        split_pair(into),
        split_pair(out_of),
        np.cos(turn).astype(np.float32),
        np.sin(turn).astype(np.float32),
        split_pair(across),
    )


def dot(left, right):
    return jnp.dot(left, right, preferred_element_type=jnp.float32)


def turned(real, imag, cos, sin):
    return real * cos + imag * sin, imag * cos - real * sin


ZS, XS, YS = 8, 4, 4
VMEM = pl.BlockSpec(memory_space=pltpu.VMEM)
MESH = pl.DeviceIdType.MESH
BF = jnp.bfloat16


def forward_pieces(block_of, into, twist, across, z_ref, out_ref):
    rows = z_ref.shape[0]
    inner = z_ref.shape[1] // 2

    def spread(c):
        at = pl.ds(c * CHUNK, CHUNK)
        block = block_of(at)
        y = sum(dot(table[...], block) for table in into)
        real, imag = turned(y[:rows], y[rows:], twist[0][:, at], twist[1][:, at])
        z_ref[:, at] = real.astype(BF)
        z_ref[:, pl.ds(inner + c * CHUNK, CHUNK)] = imag.astype(BF)

    def columns(c):
        at = pl.ds(c * CHUNK, CHUNK)
        z = z_ref[...]
        out_ref[:, at] = sum(dot(z, table[:, at]) for table in across)

    pieces = [functools.partial(spread, c) for c in range(inner // CHUNK)]
    pieces += [functools.partial(columns, c) for c in range(2 * inner // CHUNK)]
    return pieces


def combine(grad_ref, other_ref, z_ref, inner):
    @pl.loop(0, inner // CHUNK)
    def _(i):
        at = pl.ds(pl.multiple_of(i * CHUNK, CHUNK), CHUNK)
        far = pl.ds(pl.multiple_of(inner + i * CHUNK, CHUNK), CHUNK)
        g_re, g_im = grad_ref[:, at], grad_ref[:, far]
        o_re, o_im = other_ref[:, at], other_ref[:, far]
        z_ref[:, at] = (g_re * o_re + g_im * o_im).astype(BF)
        z_ref[:, far] = (g_re * o_im - g_im * o_re).astype(BF)


def layer_kernel(
    w_hbm, g_hbm, gate_in_hbm, values_hbm, gate_out_hbm, filters_hbm, skip_ref,
    in_hi_h, in_lo_h, of_hi_h, of_lo_h, cos_h, sin_h, ac_hi_h, ac_lo_h,
    home_out, filters_out, mixed_out,
    gate_in, values, filters, in_hi, in_lo, of_hi, of_lo, cos, sin, ac_hi, ac_lo,
    w_ring, w_mine, w_other, g_ring, g_other, own, hold, part, inbox, relay, final,
    near_gate, back_bf, gated, gated_in, stage, crossed, pair_in,
    z_ref, u_ref, spec_g, spec_p, spec_f, leaving, landed,
    send_sems, recv_sems, local_sems,
):
    s, h = lax.axis_index("seq"), lax.axis_index("ch")
    z, x = s // XS, s % XS
    y, core = h // 2, h % 2

    def zmod(d):
        return lax.rem(z + d + ZS, ZS)

    def xmod(d):
        return lax.rem(x + d + XS, XS)

    def at_z(d):
        return (zmod(d) * XS + x, h)

    def at_x(d):
        return (z * XS + xmod(d), h)

    def at_y(d):
        return (s, lax.rem(y + d + YS, YS) * 2 + core)

    sibling = (s, y * 2 + 1 - core)
    peers = [at_z(d) for d in range(1, ZS)] + [at_x(d) for d in range(1, XS)]
    peers += [at_y(d) for d in (1, -1)] + [sibling]

    barrier = pltpu.get_barrier_semaphore()
    for peer in peers:
        pl.semaphore_signal(barrier, inc=1, device_id=peer, device_id_type=MESH)

    loads = []

    def load(src, dst):
        copy = pltpu.make_async_copy(src, dst, local_sems.at[len(loads)])
        copy.start()
        loads.append(copy)
        return copy

    w_load = load(w_hbm, w_ring.at[z])
    g_load = load(g_hbm, g_ring.at[x])
    pair_loads = [load(gate_in_hbm, gate_in), load(values_hbm, values), load(filters_hbm, filters)]
    gate_load = load(gate_out_hbm.at[x], near_gate.at[0])
    table_loads = [
        load(src, dst)
        for src, dst in (
            (in_hi_h, in_hi), (in_lo_h, in_lo), (ac_hi_h, ac_hi), (ac_lo_h, ac_lo),
            (cos_h, cos), (sin_h, sin), (of_hi_h, of_hi), (of_lo_h, of_lo),
        )
    ]
    pl.semaphore_wait(barrier, len(peers))

    copies = []

    def send(src, dst, device):
        k = len(copies)
        copy = pltpu.make_async_remote_copy(
            src_ref=src, dst_ref=dst, send_sem=send_sems.at[k], recv_sem=recv_sems.at[k],
            device_id=device, device_id_type=MESH,
        )
        copy.start()
        copies.append(copy)
        return copy

    half_w = w_ring.shape[1] // 2
    half_g = g_ring.shape[1] // 2
    first, second = pl.ds(0, half_w), pl.ds(half_w, half_w)
    top, low = pl.ds(0, half_g), pl.ds(half_g, half_g)

    up = send(w_hbm, w_ring.at[z], at_z(1))
    down = send(w_hbm, w_ring.at[z], at_z(-1))
    right_top = send(g_hbm.at[top], g_ring.at[x, top], at_x(1))
    left_low = send(g_hbm.at[low], g_ring.at[x, low], at_x(-1))
    right_low = send(g_hbm.at[low], g_ring.at[x, low], at_x(1))
    left_top = send(g_hbm.at[top], g_ring.at[x, top], at_x(-1))
    shared = [send(g_hbm, g_other.at[0], sibling)]
    for copy in pair_loads:
        copy.wait()
    for i in range(XS):
        product = gate_in[i].astype(jnp.float32) * values[i].astype(jnp.float32)
        stage[0, i] = product.astype(BF)
        stage[1, i] = filters[i].astype(BF)

    up.wait_recv()
    up = send(w_ring.at[zmod(-1)], w_ring.at[zmod(-1)], at_z(1))
    down.wait_recv()
    down = send(w_ring.at[zmod(1)], w_ring.at[zmod(1)], at_z(-1))
    right_top.wait_recv()
    far_top = send(g_ring.at[xmod(-1), top], g_ring.at[xmod(-1), top], at_x(1))
    left_low.wait_recv()
    far_low = send(g_ring.at[xmod(1), low], g_ring.at[xmod(1), low], at_x(-1))
    up.wait_recv()
    up = send(w_ring.at[zmod(-2)], w_ring.at[zmod(-2)], at_z(1))
    down.wait_recv()
    down = send(w_ring.at[zmod(2)], w_ring.at[zmod(2)], at_z(-1))
    over_z = {}
    over_x = {}

    def pair_z(i, start, size):
        at = pl.ds(start, size)
        over_z.setdefault(i, []).extend(
            send(stage.at[i, at, zmod(d)], crossed.at[i, z, at], at_z(d)) for d in range(1, ZS)
        )
        crossed[i, z, at] = stage[i, at, z]

    def pair_x(i):
        for copy in over_z[i]:
            copy.wait_recv()
        over_x[i] = [
            send(crossed.at[i, :, xmod(d)], pair_in.at[i, :, x], at_x(d)) for d in range(1, XS)
        ]
        pair_in[i, :, x] = crossed[i, :, x]

    up.wait_recv()
    up = send(w_ring.at[zmod(-3), first], w_ring.at[zmod(-3), first], at_z(1))
    down.wait_recv()
    down = send(w_ring.at[zmod(3), second], w_ring.at[zmod(3), second], at_z(-1))
    pair_z(1, 0, XS)
    right_low.wait_recv()
    shared.append(send(g_ring.at[xmod(-1)], g_other.at[1], sibling))
    left_top.wait_recv()
    shared.append(send(g_ring.at[xmod(1)], g_other.at[2], sibling))
    w_load.wait()
    g_load.wait()
    up.wait_recv()
    down.wait_recv()
    pair_z(0, 0, XS // 2)

    def rows_for(d, of_core):
        return lax.rem(y + d, YS) * 2 + of_core

    w_shared = [
        send(w_ring.at[rows_for(d, 1 - core)], w_other.at[d], sibling) for d in range(YS)
    ]
    for d in range(YS):
        w_mine[d] = w_ring[rows_for(d, core)]
    for copy in w_shared:
        copy.wait_recv()

    offsets = (0, -1, 1, 2)
    parts = []
    passed = []
    gates = []
    deep = w_ring.shape[1]
    wide = (YS * deep, w_ring.shape[2])

    def pass_on(n):
        for side in range(2):
            parts[n][side].wait_recv()
            relay[n, side] = (hold[n, side] + inbox[n, side, 0].astype(jnp.float32)).astype(BF)
            passed.append(send(relay.at[n, side], final.at[n, side], at_y(1 - 2 * side)))

    for n, off in enumerate(offsets):
        if n == 3:
            far_top.wait_recv()
            far_low.wait_recv()
            gates.extend(
                send(gate_out_hbm.at[xmod(d)], near_gate.at[d], at_x(d)) for d in range(1, XS)
            )
            shared.append(send(g_ring.at[xmod(2)], g_other.at[3], sibling))
        shared[n].wait_recv()

        @pl.loop(0, g_ring.shape[1] // CHUNK)
        def _(i, n=n, off=off):
            at = pl.ds(pl.multiple_of(i * CHUNK, CHUNK), CHUNK)
            form = (((1,), (1,)), ((), ()))
            total = lax.dot_general(
                w_mine[...].reshape(wide), g_ring[xmod(off), at, :], form,
                preferred_element_type=jnp.float32,
            ) + lax.dot_general(
                w_other[...].reshape(wide), g_other[n, at, :], form,
                preferred_element_type=jnp.float32,
            )
            total = total.reshape(YS, deep, CHUNK)
            own[n, :, at] = total[0]
            hold[n, 0, :, at] = total[1, :half_w]
            hold[n, 1, :, at] = total[3, half_w:]
            part[n, 0, 0, :, at] = total[2, :half_w].astype(BF)
            part[n, 0, 1, :, at] = total[1, half_w:].astype(BF)
            part[n, 1, 0, :, at] = total[2, half_w:].astype(BF)
            part[n, 1, 1, :, at] = total[3, :half_w].astype(BF)

        parts.append([send(part.at[n, side], inbox.at[n, side], at_y(1 - 2 * side)) for side in range(2)])

    arrivals = []
    homes = []

    def total_up(n):
        off = offsets[n]
        for copy in passed[2 * n : 2 * n + 2]:
            copy.wait_recv()
        d = -off % XS
        if d:
            gates[d - 1].wait_recv()
        else:
            gate_load.wait()
        upper = own[n, :half_w] + final[n, 0].astype(jnp.float32) + inbox[n, 1, 1].astype(jnp.float32)
        lower = own[n, half_w:] + final[n, 1].astype(jnp.float32) + inbox[n, 0, 1].astype(jnp.float32)
        back = jnp.concatenate([upper, lower], 0)
        result = back * near_gate[d].astype(jnp.float32)
        gated[n] = result.astype(BF).reshape(gated.shape[1:])
        for d in range(1, ZS):
            arrivals.append(send(gated.at[n, zmod(d)], gated_in.at[z, xmod(off)], at_z(d)))
        gated_in[z, xmod(off)] = gated[n, z]
        back_bf[n] = back.astype(BF)

    inner = g_ring.shape[2]
    rows = g_ring.shape[1]
    into, twist, across = (in_hi, in_lo), (cos, sin), (ac_hi, ac_lo)

    def pair_block(i):
        return lambda at: pair_in[i, :, :, :, at].reshape(rows, CHUNK)

    pass_on(0)
    pass_on(1)
    pass_on(2)
    total_up(0)
    pass_on(3)
    total_up(1)
    total_up(2)
    pair_x(1)
    total_up(3)
    pair_z(0, XS // 2, XS // 2)
    for copy in table_loads:
        copy.wait()
    for copy in over_x[1]:
        copy.wait_recv()
    for piece in forward_pieces(pair_block(1), into, twist, across, z_ref, spec_f):
        piece()
    home_out[x] = back_bf[0]
    for copy in arrivals:
        copy.wait_recv()
    for piece in forward_pieces(
        lambda at: gated_in[:, :, :, at].reshape(rows, CHUNK), into, twist, across[:1], z_ref, spec_g
    ):
        piece()

    width = gated_in.shape[2]
    lanes = skip_ref.shape[1]
    pick = lax.broadcasted_iota(jnp.int32, (width, lanes), 1) == z * width + lax.broadcasted_iota(
        jnp.int32, (width, lanes), 0
    )
    scale = jnp.sum(jnp.where(pick, skip_ref[pl.ds(x, 1), :], 0.0), axis=1, keepdims=True)
    spec_rows = z_ref.shape[0]
    gone = []
    turns = []

    def turn_x(k):
        for copy in gone[k]:
            copy.wait_recv()
        which, c = divmod(k, 2)
        result = (mixed_out, filters_out)[which]
        at = pl.ds(c * CHUNK, CHUNK)
        turns.extend(
            send(landed.at[k, :, xmod(d)], result.at[x, :, :, at], at_x(d))
            for d in range(1, XS)
        )
        result[x, :, :, at] = landed[k, :, x]

    def leave(k):
        which, c = divmod(k, 2)
        if c == 0:
            combine(spec_g, (spec_f, spec_p)[which], z_ref, inner)
        at, far = pl.ds(c * CHUNK, CHUNK), pl.ds(inner + c * CHUNK, CHUNK)
        values_z = z_ref[...]
        real = dot(values_z, ac_hi[:, at]) + dot(values_z, ac_lo[:, at])
        imag = dot(values_z, ac_hi[:, far]) + dot(values_z, ac_lo[:, far])
        real, imag = turned(real, imag, cos[:, at], sin[:, at])
        u_ref[:spec_rows, :] = real.astype(BF)
        u_ref[spec_rows:, :] = imag.astype(BF)
        u = u_ref[...]
        out = (dot(of_hi[...], u) + dot(of_lo[...], u)).reshape(leaving.shape[1:])
        if which == 0:
            out = out + scale * gated_in[:, :, :, at].astype(jnp.float32)
        leaving[k] = out.astype(BF)
        gone.append(
            [send(leaving.at[k, zmod(d)], landed.at[k, z], at_z(d)) for d in range(1, ZS)]
        )
        landed[k, z] = leaving[k, z]

    leave(0)
    pair_x(0)
    leave(1)
    for n, off in enumerate(offsets):
        if n:
            homes.append(send(back_bf.at[n], home_out.at[x], at_x(off)))
    for copy in over_x[0]:
        copy.wait_recv()
    for piece in forward_pieces(pair_block(0), into, twist, across, z_ref, spec_p):
        piece()
    leave(2)
    turn_x(0)
    leave(3)
    turn_x(1)
    turn_x(2)
    turn_x(3)
    for copy in homes + turns:
        copy.wait_recv()
    for copy in copies:
        copy.wait_send()


def layer(grad_out, out_weight, gate_in, gate_out, values, filters, skip_scale):
    rows, inner = gate_in.shape
    deep, wide = out_weight.shape
    width = rows // (ZS * XS)
    into, out_of, cos, sin, across = make_tables(ZS * XS, width, inner)
    tables = (*into, *out_of, cos, sin, *across)
    spec_rows = cos.shape[0]
    split = (XS, ZS, width, inner)
    parts = inner // CHUNK
    count = 139

    def vmem(shape, dtype=BF):
        return pltpu.VMEM(shape, dtype)

    spec = vmem((spec_rows, 2 * inner), jnp.float32)
    return pl.pallas_call(
        layer_kernel,
        out_shape=[
            jax.ShapeDtypeStruct((XS, deep, inner), BF),
            jax.ShapeDtypeStruct(split, BF),
            jax.ShapeDtypeStruct(split, BF),
        ],
        in_specs=[pl.BlockSpec(memory_space=pl.ANY)] * 6
        + [VMEM]
        + [pl.BlockSpec(memory_space=pl.ANY)] * len(tables),
        out_specs=[VMEM] * 3,
        scratch_shapes=[
            vmem(split),
            vmem(split),
            vmem(split, jnp.float32),
            *[vmem(t.shape, t.dtype) for t in tables],
            vmem((ZS, deep, wide)),
            vmem((YS, deep, wide)),
            vmem((YS, deep, wide)),
            vmem((XS,) + grad_out.shape),
            vmem((XS,) + grad_out.shape),
            vmem((XS, deep, inner), jnp.float32),
            vmem((XS, 2, deep // 2, inner), jnp.float32),
            vmem((XS, 2, 2, deep // 2, inner)),
            vmem((XS, 2, 2, deep // 2, inner)),
            vmem((XS, 2, deep // 2, inner)),
            vmem((XS, 2, deep // 2, inner)),
            vmem((XS, deep, inner)),
            vmem((XS, deep, inner)),
            vmem((XS, ZS, width, inner)),
            vmem((ZS, XS, width, inner)),
            vmem((2,) + split),
            vmem((2, ZS, XS, width, inner)),
            vmem((2, ZS, XS, width, inner)),
            vmem((spec_rows, 2 * inner)),
            vmem((2 * spec_rows, CHUNK)),
            spec,
            spec,
            spec,
            vmem((2 * parts, ZS, XS, width, CHUNK)),
            vmem((2 * parts, ZS, XS, width, CHUNK)),
            pltpu.SemaphoreType.DMA((count,)),
            pltpu.SemaphoreType.DMA((count,)),
            pltpu.SemaphoreType.DMA((14,)),
        ],
        compiler_params=pltpu.CompilerParams(
            collective_id=0, has_side_effects=True, vmem_limit_bytes=58 * 1024 * 1024
        ),
        cost_estimate=pl.CostEstimate(flops=20 * 10**9, bytes_accessed=20 * 10**6, transcendentals=0),
    )(
        out_weight,
        grad_out,
        gate_in.reshape(split),
        values.reshape(split),
        gate_out.reshape(XS, deep, inner),
        filters.reshape(split),
        skip_scale.reshape(XS, deep),
        *tables,
    )


def shards(grad_out, out_weight, gate_in, gate_out, values, conv_out, filters, skip_scale):
    rows, inner = gate_in.shape
    home, grad_filters, mixed = layer(
        grad_out, out_weight, gate_in, gate_out, values, filters, skip_scale
    )

    def wide(block):
        return block.reshape(rows, inner).astype(jnp.float32)

    grad_gate_out = (wide(home) * wide(conv_out)).astype(BF)
    grad_gate_in = (wide(mixed) * wide(values)).astype(BF)
    grad_values = (wide(mixed) * wide(gate_in)).astype(BF)
    return (grad_gate_in, grad_values, grad_gate_out, wide(grad_filters))


def solution(mesh):
    placed = (
        P("seq", "ch"),
        P("seq", "ch"),
        P("ch", "seq"),
        P("ch", "seq"),
        P("ch", "seq"),
        P("ch", "seq"),
        P("ch", "seq"),
        P("ch"),
    )
    return jax.shard_map(
        shards,
        mesh=mesh,
        in_specs=placed,
        out_specs=(P("ch", "seq"), P("ch", "seq"), P("ch", "seq"), P("ch", "seq")),
        check_vma=False,
    )
```

```python
import functools

import jax
import jax.numpy as jnp
import ml_dtypes
import numpy as np
from jax import lax
from jax.experimental import pallas as pl
from jax.experimental.pallas import tpu as pltpu
from jax.sharding import PartitionSpec as P

OUTER = 64
CHUNK = 256


def split_pair(table):
    high = table.astype(np.float32).astype(ml_dtypes.bfloat16)
    low = (table - high.astype(np.float64)).astype(np.float32).astype(ml_dtypes.bfloat16)
    return high, low


def make_tables(blocks, width, inner):
    total = OUTER * inner
    half = OUTER // 2 + 1
    k = np.arange(half)
    a = np.arange(blocks)
    b = np.arange(inner)
    first = 2.0 * np.pi * (np.outer(k, a) % OUTER) / OUTER
    eye = np.eye(width)
    k_cos = np.kron(np.cos(first), eye)
    k_sin = np.kron(np.sin(first), eye)
    into = np.concatenate([k_cos, -k_sin], 0)
    weight = np.full((half, 1), 2.0)
    weight[0] = 1.0
    weight[-1] = 1.0
    weight = weight / total
    back_cos = np.kron((weight * np.cos(first)).T, eye)
    back_sin = np.kron((weight * np.sin(first)).T, eye)
    out_of = np.concatenate([back_cos, back_sin], 1)
    turn = 2.0 * np.pi * (np.outer(k, b) % total) / total
    turn = np.repeat(turn, width, axis=0)
    second = 2.0 * np.pi * (np.outer(b, b) % inner) / inner
    c, s = np.cos(second), np.sin(second)
    across = np.concatenate([np.concatenate([c, -s], 1), np.concatenate([s, c], 1)], 0)
    return (
        split_pair(into),
        split_pair(out_of),
        np.cos(turn).astype(np.float32),
        np.sin(turn).astype(np.float32),
        split_pair(across),
    )


def dot(left, right):
    return jnp.dot(left, right, preferred_element_type=jnp.float32)


def turned(real, imag, cos, sin):
    return real * cos + imag * sin, imag * cos - real * sin


ZS, XS, YS = 8, 4, 4
VMEM = pl.BlockSpec(memory_space=pltpu.VMEM)
MESH = pl.DeviceIdType.MESH
BF = jnp.bfloat16


def forward_pieces(block_of, into, twist, across, z_ref, out_ref):
    rows = z_ref.shape[0]
    inner = z_ref.shape[1] // 2

    def spread(c):
        at = pl.ds(c * CHUNK, CHUNK)
        block = block_of(at)
        y = sum(dot(table[...], block) for table in into)
        real, imag = turned(y[:rows], y[rows:], twist[0][:, at], twist[1][:, at])
        z_ref[:, at] = real.astype(BF)
        z_ref[:, pl.ds(inner + c * CHUNK, CHUNK)] = imag.astype(BF)

    def columns(c):
        at = pl.ds(c * CHUNK, CHUNK)
        z = z_ref[...]
        out_ref[:, at] = sum(dot(z, table[:, at]) for table in across)

    pieces = [functools.partial(spread, c) for c in range(inner // CHUNK)]
    pieces += [functools.partial(columns, c) for c in range(2 * inner // CHUNK)]
    return pieces


def combine(grad_ref, other_ref, z_ref, inner):
    @pl.loop(0, inner // CHUNK)
    def _(i):
        at = pl.ds(pl.multiple_of(i * CHUNK, CHUNK), CHUNK)
        far = pl.ds(pl.multiple_of(inner + i * CHUNK, CHUNK), CHUNK)
        g_re, g_im = grad_ref[:, at], grad_ref[:, far]
        o_re, o_im = other_ref[:, at], other_ref[:, far]
        z_ref[:, at] = (g_re * o_re + g_im * o_im).astype(BF)
        z_ref[:, far] = (g_re * o_im - g_im * o_re).astype(BF)


def layer_kernel(
    w_hbm, g_hbm, gate_in_hbm, values_hbm, gate_out_hbm, filters_hbm, skip_ref,
    in_hi_h, in_lo_h, of_hi_h, of_lo_h, cos_h, sin_h, ac_hi_h, ac_lo_h,
    home_out, filters_out, mixed_out,
    gate_in, values, filters, in_hi, in_lo, of_hi, of_lo, cos, sin, ac_hi, ac_lo,
    w_ring, w_mine, w_other, g_ring, g_other, own, hold, part, inbox, relay, final,
    near_gate, back_bf, gated, gated_in, stage, crossed, pair_in,
    z_ref, u_ref, spec_g, spec_p, spec_f, leaving, landed, way_pair, way_gated, way_out,
    send_sems, recv_sems, local_sems,
):
    s, h = lax.axis_index("seq"), lax.axis_index("ch")
    z, x = s // XS, s % XS
    y, core = h // 2, h % 2

    def zmod(d):
        return lax.rem(z + d + ZS, ZS)

    def xmod(d):
        return lax.rem(x + d + XS, XS)

    def at_z(d):
        return (zmod(d) * XS + x, h)

    def at_x(d):
        return (z * XS + xmod(d), h)

    def at_y(d):
        return (s, lax.rem(y + d + YS, YS) * 2 + core)

    sibling = (s, y * 2 + 1 - core)
    peers = [at_z(d) for d in range(1, ZS)] + [at_x(d) for d in range(1, XS)]
    peers += [at_y(d) for d in (1, -1)] + [sibling]

    barrier = pltpu.get_barrier_semaphore()
    for peer in peers:
        pl.semaphore_signal(barrier, inc=1, device_id=peer, device_id_type=MESH)

    loads = []

    def load(src, dst):
        copy = pltpu.make_async_copy(src, dst, local_sems.at[len(loads)])
        copy.start()
        loads.append(copy)
        return copy

    w_load = load(w_hbm, w_ring.at[z])
    g_load = load(g_hbm, g_ring.at[x])
    pair_loads = [load(gate_in_hbm, gate_in), load(values_hbm, values), load(filters_hbm, filters)]
    gate_load = load(gate_out_hbm.at[x], near_gate.at[0])
    table_loads = [
        load(src, dst)
        for src, dst in (
            (in_hi_h, in_hi), (in_lo_h, in_lo), (ac_hi_h, ac_hi), (ac_lo_h, ac_lo),
            (cos_h, cos), (sin_h, sin), (of_hi_h, of_hi), (of_lo_h, of_lo),
        )
    ]
    pl.semaphore_wait(barrier, len(peers))

    copies = []

    def send(src, dst, device):
        k = len(copies)
        copy = pltpu.make_async_remote_copy(
            src_ref=src, dst_ref=dst, send_sem=send_sems.at[k], recv_sem=recv_sems.at[k],
            device_id=device, device_id_type=MESH,
        )
        copy.start()
        copies.append(copy)
        return copy

    half_w = w_ring.shape[1] // 2
    half_g = g_ring.shape[1] // 2
    first, second = pl.ds(0, half_w), pl.ds(half_w, half_w)
    top, low = pl.ds(0, half_g), pl.ds(half_g, half_g)

    up = send(w_hbm, w_ring.at[z], at_z(1))
    down = send(w_hbm, w_ring.at[z], at_z(-1))
    right_top = send(g_hbm.at[top], g_ring.at[x, top], at_x(1))
    left_low = send(g_hbm.at[low], g_ring.at[x, low], at_x(-1))
    right_low = send(g_hbm.at[low], g_ring.at[x, low], at_x(1))
    left_top = send(g_hbm.at[top], g_ring.at[x, top], at_x(-1))
    shared = [send(g_hbm, g_other.at[0], sibling)]
    for copy in pair_loads:
        copy.wait()
    for i in range(XS):
        product = gate_in[i].astype(jnp.float32) * values[i].astype(jnp.float32)
        stage[0, i] = product.astype(BF)
        stage[1, i] = filters[i].astype(BF)

    up.wait_recv()
    up = send(w_ring.at[zmod(-1)], w_ring.at[zmod(-1)], at_z(1))
    down.wait_recv()
    down = send(w_ring.at[zmod(1)], w_ring.at[zmod(1)], at_z(-1))
    right_top.wait_recv()
    far_top = send(g_ring.at[xmod(-1), top], g_ring.at[xmod(-1), top], at_x(1))
    left_low.wait_recv()
    far_low = send(g_ring.at[xmod(1), low], g_ring.at[xmod(1), low], at_x(-1))
    up.wait_recv()
    up = send(w_ring.at[zmod(-2)], w_ring.at[zmod(-2)], at_z(1))
    down.wait_recv()
    down = send(w_ring.at[zmod(2)], w_ring.at[zmod(2)], at_z(-1))
    over_z = {}
    over_x = {}

    def ring_z(source, target, halves, way, sides=(0, 1)):
        hops = {}
        for side in sides:
            block = source(ZS // 2, halves[side])
            hops[side] = send(block, way.at[side], at_z(2 - 4 * side))
        there = [send(source(d, None), target(z, None), at_z(d)) for d in (3, -3, 2, -2, 1, -1)]

        def forward():
            for side in sides:
                hops[side].wait_recv()
                turn = 2 - 4 * side
                there.append(send(way.at[side], target(zmod(-turn), halves[side]), at_z(turn)))

        return there, forward

    def pair_z(i, start, size):
        at = pl.ds(start, size)
        half = size // 2

        def source(d, part):
            return stage.at[i, at if part is None else part, zmod(d)]

        def target(origin, part):
            return crossed.at[i, origin, at if part is None else part]

        there, forward = ring_z(
            source, target, (pl.ds(start, half), pl.ds(start + half, half)),
            way_pair.at[i, :, pl.ds(start // 2, half)],
        )
        over_z.setdefault(i, []).append(there)
        crossed[i, z, at] = stage[i, at, z]
        return forward

    def pair_x(i):
        for copy in sum(over_z[i], []):
            copy.wait_recv()
        over_x[i] = [
            send(crossed.at[i, :, xmod(d)], pair_in.at[i, :, x], at_x(d)) for d in range(1, XS)
        ]
        pair_in[i, :, x] = crossed[i, :, x]

    up.wait_recv()
    up = send(w_ring.at[zmod(-3), first], w_ring.at[zmod(-3), first], at_z(1))
    down.wait_recv()
    down = send(w_ring.at[zmod(3), second], w_ring.at[zmod(3), second], at_z(-1))
    filters_on = pair_z(1, 0, XS)
    right_low.wait_recv()
    shared.append(send(g_ring.at[xmod(-1)], g_other.at[1], sibling))
    left_top.wait_recv()
    shared.append(send(g_ring.at[xmod(1)], g_other.at[2], sibling))
    w_load.wait()
    g_load.wait()
    up.wait_recv()
    down.wait_recv()
    product_on = pair_z(0, 0, XS // 2)

    def rows_for(d, of_core):
        return lax.rem(y + d, YS) * 2 + of_core

    w_shared = [
        send(w_ring.at[rows_for(d, 1 - core)], w_other.at[d], sibling) for d in range(YS)
    ]
    for d in range(YS):
        w_mine[d] = w_ring[rows_for(d, core)]
    for copy in w_shared:
        copy.wait_recv()
    filters_on()

    offsets = (0, -1, 1, 2)
    parts = []
    passed = []
    gates = []
    deep = w_ring.shape[1]
    wide = (YS * deep, w_ring.shape[2])

    def pass_on(n):
        for side in range(2):
            parts[n][side].wait_recv()
            relay[n, side] = (hold[n, side] + inbox[n, side, 0].astype(jnp.float32)).astype(BF)
            passed.append(send(relay.at[n, side], final.at[n, side], at_y(1 - 2 * side)))

    for n, off in enumerate(offsets):
        if n == 3:
            far_top.wait_recv()
            far_low.wait_recv()
            gates.extend(
                send(gate_out_hbm.at[xmod(d)], near_gate.at[d], at_x(d)) for d in range(1, XS)
            )
            shared.append(send(g_ring.at[xmod(2)], g_other.at[3], sibling))
        shared[n].wait_recv()

        @pl.loop(0, g_ring.shape[1] // CHUNK)
        def _(i, n=n, off=off):
            at = pl.ds(pl.multiple_of(i * CHUNK, CHUNK), CHUNK)
            form = (((1,), (1,)), ((), ()))
            total = lax.dot_general(
                w_mine[...].reshape(wide), g_ring[xmod(off), at, :], form,
                preferred_element_type=jnp.float32,
            ) + lax.dot_general(
                w_other[...].reshape(wide), g_other[n, at, :], form,
                preferred_element_type=jnp.float32,
            )
            total = total.reshape(YS, deep, CHUNK)
            own[n, :, at] = total[0]
            hold[n, 0, :, at] = total[1, :half_w]
            hold[n, 1, :, at] = total[3, half_w:]
            part[n, 0, 0, :, at] = total[2, :half_w].astype(BF)
            part[n, 0, 1, :, at] = total[1, half_w:].astype(BF)
            part[n, 1, 0, :, at] = total[2, half_w:].astype(BF)
            part[n, 1, 1, :, at] = total[3, :half_w].astype(BF)

        parts.append([send(part.at[n, side], inbox.at[n, side], at_y(1 - 2 * side)) for side in range(2)])

    arrivals = []
    gated_on = []
    homes = []

    def total_up(n):
        off = offsets[n]
        for copy in passed[2 * n : 2 * n + 2]:
            copy.wait_recv()
        d = -off % XS
        if d:
            gates[d - 1].wait_recv()
        else:
            gate_load.wait()
        upper = own[n, :half_w] + final[n, 0].astype(jnp.float32) + inbox[n, 1, 1].astype(jnp.float32)
        lower = own[n, half_w:] + final[n, 1].astype(jnp.float32) + inbox[n, 0, 1].astype(jnp.float32)
        back = jnp.concatenate([upper, lower], 0)
        result = back * near_gate[d].astype(jnp.float32)
        gated[n] = result.astype(BF).reshape(gated.shape[1:])
        there, forward = ring_z(
            lambda d, part: gated.at[n, zmod(d)],
            lambda origin, part: gated_in.at[origin, xmod(off)],
            (None, None), way_gated.at[n], (n % 2,),
        )
        arrivals.append(there)
        gated_on.append(forward)
        gated_in[z, xmod(off)] = gated[n, z]
        back_bf[n] = back.astype(BF)

    inner = g_ring.shape[2]
    rows = g_ring.shape[1]
    into, twist, across = (in_hi, in_lo), (cos, sin), (ac_hi, ac_lo)

    def pair_block(i):
        return lambda at: pair_in[i, :, :, :, at].reshape(rows, CHUNK)

    pass_on(0)
    pass_on(1)
    product_on()
    pass_on(2)
    total_up(0)
    pass_on(3)
    total_up(1)
    gated_on[0]()
    total_up(2)
    gated_on[1]()
    pair_x(1)
    total_up(3)
    gated_on[2]()
    product_on = pair_z(0, XS // 2, XS // 2)
    for copy in table_loads:
        copy.wait()
    gated_on[3]()
    for copy in over_x[1]:
        copy.wait_recv()
    pieces = forward_pieces(pair_block(1), into, twist, across, z_ref, spec_f)
    for piece in pieces[:2]:
        piece()
    product_on()
    for piece in pieces[2:]:
        piece()
    home_out[x] = back_bf[0]
    for copy in sum(arrivals, []):
        copy.wait_recv()
    for piece in forward_pieces(
        lambda at: gated_in[:, :, :, at].reshape(rows, CHUNK), into, twist, across[:1], z_ref, spec_g
    ):
        piece()

    width = gated_in.shape[2]
    lanes = skip_ref.shape[1]
    pick = lax.broadcasted_iota(jnp.int32, (width, lanes), 1) == z * width + lax.broadcasted_iota(
        jnp.int32, (width, lanes), 0
    )
    scale = jnp.sum(jnp.where(pick, skip_ref[pl.ds(x, 1), :], 0.0), axis=1, keepdims=True)
    spec_rows = z_ref.shape[0]
    gone = []
    gone_on = []
    turns = []

    def turn_x(k):
        for copy in gone[k]:
            copy.wait_recv()
        which, c = divmod(k, 2)
        result = (mixed_out, filters_out)[which]
        at = pl.ds(c * CHUNK, CHUNK)
        turns.extend(
            send(landed.at[k, :, xmod(d)], result.at[x, :, :, at], at_x(d))
            for d in range(1, XS)
        )
        result[x, :, :, at] = landed[k, :, x]

    def leave(k):
        which, c = divmod(k, 2)
        if c == 0:
            combine(spec_g, (spec_f, spec_p)[which], z_ref, inner)
        at, far = pl.ds(c * CHUNK, CHUNK), pl.ds(inner + c * CHUNK, CHUNK)
        values_z = z_ref[...]
        real = dot(values_z, ac_hi[:, at]) + dot(values_z, ac_lo[:, at])
        imag = dot(values_z, ac_hi[:, far]) + dot(values_z, ac_lo[:, far])
        real, imag = turned(real, imag, cos[:, at], sin[:, at])
        u_ref[:spec_rows, :] = real.astype(BF)
        u_ref[spec_rows:, :] = imag.astype(BF)
        u = u_ref[...]
        out = (dot(of_hi[...], u) + dot(of_lo[...], u)).reshape(leaving.shape[1:])
        if which == 0:
            out = out + scale * gated_in[:, :, :, at].astype(jnp.float32)
        leaving[k] = out.astype(BF)


        def source(d, part):
            return leaving.at[k, zmod(d)] if part is None else leaving.at[k, zmod(d), part]

        def target(origin, part):
            return landed.at[k, origin] if part is None else landed.at[k, origin, part]

        half = XS // 2
        there, forward = ring_z(source, target, (pl.ds(0, half), pl.ds(half, half)), way_out.at[k])
        gone.append(there)
        gone_on.append(forward)
        landed[k, z] = leaving[k, z]

    leave(0)
    pair_x(0)
    leave(1)
    gone_on[0]()
    for n, off in enumerate(offsets):
        if n:
            homes.append(send(back_bf.at[n], home_out.at[x], at_x(off)))
    for copy in over_x[0]:
        copy.wait_recv()
    pieces = forward_pieces(pair_block(0), into, twist, across, z_ref, spec_p)
    for piece in pieces[:2]:
        piece()
    gone_on[1]()
    for piece in pieces[2:]:
        piece()
    leave(2)
    turn_x(0)
    leave(3)
    gone_on[2]()
    turn_x(1)
    gone_on[3]()
    turn_x(2)
    turn_x(3)
    for copy in homes + turns:
        copy.wait_recv()
    for copy in copies:
        copy.wait_send()


def layer(grad_out, out_weight, gate_in, gate_out, values, filters, skip_scale):
    rows, inner = gate_in.shape
    deep, wide = out_weight.shape
    width = rows // (ZS * XS)
    into, out_of, cos, sin, across = make_tables(ZS * XS, width, inner)
    tables = (*into, *out_of, cos, sin, *across)
    spec_rows = cos.shape[0]
    split = (XS, ZS, width, inner)
    parts = inner // CHUNK
    count = 164

    def vmem(shape, dtype=BF):
        return pltpu.VMEM(shape, dtype)

    spec = vmem((spec_rows, 2 * inner), jnp.float32)
    return pl.pallas_call(
        layer_kernel,
        out_shape=[
            jax.ShapeDtypeStruct((XS, deep, inner), BF),
            jax.ShapeDtypeStruct(split, BF),
            jax.ShapeDtypeStruct(split, BF),
        ],
        in_specs=[pl.BlockSpec(memory_space=pl.ANY)] * 6
        + [VMEM]
        + [pl.BlockSpec(memory_space=pl.ANY)] * len(tables),
        out_specs=[VMEM] * 3,
        scratch_shapes=[
            vmem(split),
            vmem(split),
            vmem(split, jnp.float32),
            *[vmem(t.shape, t.dtype) for t in tables],
            vmem((ZS, deep, wide)),
            vmem((YS, deep, wide)),
            vmem((YS, deep, wide)),
            vmem((XS,) + grad_out.shape),
            vmem((XS,) + grad_out.shape),
            vmem((XS, deep, inner), jnp.float32),
            vmem((XS, 2, deep // 2, inner), jnp.float32),
            vmem((XS, 2, 2, deep // 2, inner)),
            vmem((XS, 2, 2, deep // 2, inner)),
            vmem((XS, 2, deep // 2, inner)),
            vmem((XS, 2, deep // 2, inner)),
            vmem((XS, deep, inner)),
            vmem((XS, deep, inner)),
            vmem((XS, ZS, width, inner)),
            vmem((ZS, XS, width, inner)),
            vmem((2,) + split),
            vmem((2, ZS, XS, width, inner)),
            vmem((2, ZS, XS, width, inner)),
            vmem((spec_rows, 2 * inner)),
            vmem((2 * spec_rows, CHUNK)),
            spec,
            spec,
            spec,
            vmem((2 * parts, ZS, XS, width, CHUNK)),
            vmem((2 * parts, ZS, XS, width, CHUNK)),
            vmem((2, 2, XS // 2, width, inner)),
            vmem((XS, 2, width, inner)),
            vmem((2 * parts, 2, XS // 2, width, CHUNK)),
            pltpu.SemaphoreType.DMA((count,)),
            pltpu.SemaphoreType.DMA((count,)),
            pltpu.SemaphoreType.DMA((14,)),
        ],
        compiler_params=pltpu.CompilerParams(
            collective_id=0, has_side_effects=True, vmem_limit_bytes=58 * 1024 * 1024
        ),
        cost_estimate=pl.CostEstimate(flops=20 * 10**9, bytes_accessed=20 * 10**6, transcendentals=0),
    )(
        out_weight,
        grad_out,
        gate_in.reshape(split),
        values.reshape(split),
        gate_out.reshape(XS, deep, inner),
        filters.reshape(split),
        skip_scale.reshape(XS, deep),
        *tables,
    )


def shards(grad_out, out_weight, gate_in, gate_out, values, conv_out, filters, skip_scale):
    rows, inner = gate_in.shape
    home, grad_filters, mixed = layer(
        grad_out, out_weight, gate_in, gate_out, values, filters, skip_scale
    )

    def wide(block):
        return block.reshape(rows, inner).astype(jnp.float32)

    grad_gate_out = (wide(home) * wide(conv_out)).astype(BF)
    grad_gate_in = (wide(mixed) * wide(values)).astype(BF)
    grad_values = (wide(mixed) * wide(gate_in)).astype(BF)
    return (grad_gate_in, grad_values, grad_gate_out, wide(grad_filters))


def solution(mesh):
    placed = (
        P("seq", "ch"),
        P("seq", "ch"),
        P("ch", "seq"),
        P("ch", "seq"),
        P("ch", "seq"),
        P("ch", "seq"),
        P("ch", "seq"),
        P("ch"),
    )
    return jax.shard_map(
        shards,
        mesh=mesh,
        in_specs=placed,
        out_specs=(P("ch", "seq"), P("ch", "seq"), P("ch", "seq"), P("ch", "seq")),
        check_vma=False,
    )
```

```python
import jax
import jax.numpy as jnp
import ml_dtypes
import numpy as np
from jax import lax
from jax.experimental import pallas as pl
from jax.experimental.pallas import tpu as pltpu
from jax.sharding import PartitionSpec as P

OUTER = 64
CHUNK = 256
STEP = 16


def split_pair(table):
    high = table.astype(np.float32).astype(ml_dtypes.bfloat16)
    low = (table - high.astype(np.float64)).astype(np.float32).astype(ml_dtypes.bfloat16)
    return high, low


def make_tables(blocks, width, inner):
    total = OUTER * inner
    half = OUTER // 2 + 1
    k = np.arange(half)
    a = np.arange(blocks)
    b = np.arange(inner)
    first = 2.0 * np.pi * (np.outer(k, a) % OUTER) / OUTER
    eye = np.eye(width)
    k_cos = np.kron(np.cos(first), eye)
    k_sin = np.kron(np.sin(first), eye)
    into = np.concatenate([k_cos, -k_sin], 0)
    weight = np.full((half, 1), 2.0)
    weight[0] = 1.0
    weight[-1] = 1.0
    weight = weight / total
    back_cos = np.kron((weight * np.cos(first)).T, eye)
    back_sin = np.kron((weight * np.sin(first)).T, eye)
    out_of = np.concatenate([back_cos, back_sin], 1)
    turn = 2.0 * np.pi * (np.outer(k, b) % total) / total
    turn = np.repeat(turn, width, axis=0)
    quarter = inner // 4
    c = np.arange(quarter)
    second = 2.0 * np.pi * (np.outer(c, c) % quarter) / quarter
    fourth = 2.0 * np.pi * np.outer(np.arange(4), c) / inner
    fourth = np.concatenate([np.cos(fourth), np.sin(fourth)], 0)
    c, s = np.cos(second), np.sin(second)
    across = np.concatenate([np.concatenate([c, -s], 1), np.concatenate([s, c], 1)], 0)
    return (
        split_pair(into),
        split_pair(out_of),
        np.cos(turn).astype(np.float32),
        np.sin(turn).astype(np.float32),
        split_pair(across),
        fourth.astype(np.float32),
    )


def dot(left, right):
    return jnp.dot(left, right, preferred_element_type=jnp.float32)


def turned(real, imag, cos, sin):
    return real * cos + imag * sin, imag * cos - real * sin


ZS, XS, YS = 8, 4, 4
VMEM = pl.BlockSpec(memory_space=pltpu.VMEM)
MESH = pl.DeviceIdType.MESH
BF = jnp.bfloat16


def four_way(parts):
    (re0, im0), (re1, im1), (re2, im2), (re3, im3) = parts
    sum_re, sum_im, dif_re, dif_im = re0 + re2, im0 + im2, re0 - re2, im0 - im2
    odd_re, odd_im, gap_re, gap_im = re1 + re3, im1 + im3, re1 - re3, im1 - im3
    return (
        (sum_re + odd_re, sum_im + odd_im),
        (dif_re + gap_im, dif_im - gap_re),
        (sum_re - odd_re, sum_im - odd_im),
        (dif_re - gap_im, dif_im + gap_re),
    )


def by_rows(rows, body):
    @pl.loop(0, rows // STEP, unroll=3)
    def _(i):
        body(pl.ds(pl.multiple_of(i * STEP, STEP), STEP), i * STEP)


def turn_fourth(part, fourth, r):
    if r == 0:
        return part
    return turned(*part, fourth[pl.ds(r, 1), :], fourth[pl.ds(4 + r, 1), :])


def forward(block_of, into, twist, fourth, across, y_ref, z_ref, out_ref):
    rows = z_ref.shape[1]
    quarter = z_ref.shape[2] // 2

    for c in range(y_ref.shape[1] // CHUNK):
        at = pl.ds(c * CHUNK, CHUNK)
        block = block_of(at)
        y_ref[:, at] = sum(dot(table[...], block) for table in into)

    def body(at, start):
        far = pl.ds(pl.multiple_of(rows + start, STEP), STEP)
        parts = []
        for q in range(4):
            col = pl.ds(q * quarter, quarter)
            parts.append(turned(y_ref[at, col], y_ref[far, col], twist[0][at, col], twist[1][at, col]))
        for r, part in enumerate(four_way(parts)):
            real, imag = turn_fourth(part, fourth, r)
            z_ref[r, at, :quarter] = real.astype(BF)
            z_ref[r, at, quarter:] = imag.astype(BF)

    by_rows(rows, body)
    columns(z_ref, across, out_ref)


def columns(z_ref, across, out_ref):
    for r in range(4):
        z = z_ref[r]
        out_ref[r] = sum(dot(z, table[...]) for table in across)


def combine(grad_ref, other_ref, z_ref):
    rows = z_ref.shape[1]
    quarter = z_ref.shape[2] // 2

    def body(at, _):
        for r in range(4):
            g_re, g_im = grad_ref[r, at, :quarter], grad_ref[r, at, quarter:]
            o_re, o_im = other_ref[r, at, :quarter], other_ref[r, at, quarter:]
            z_ref[r, at, :quarter] = (g_re * o_re + g_im * o_im).astype(BF)
            z_ref[r, at, quarter:] = (g_re * o_im - g_im * o_re).astype(BF)

    by_rows(rows, body)


def unfold(spec_ref, twist, fourth, u_ref):
    rows = spec_ref.shape[1]
    quarter = spec_ref.shape[2] // 2

    def body(at, start):
        far = pl.ds(pl.multiple_of(rows + start, STEP), STEP)
        parts = [
            turn_fourth((spec_ref[r, at, :quarter], spec_ref[r, at, quarter:]), fourth, r)
            for r in range(4)
        ]
        for q, part in enumerate(four_way(parts)):
            col = pl.ds(q * quarter, quarter)
            real, imag = turned(*part, twist[0][at, col], twist[1][at, col])
            u_ref[at, col] = real.astype(BF)
            u_ref[far, col] = imag.astype(BF)

    by_rows(rows, body)


def layer_kernel(
    w_hbm, g_hbm, gate_in_hbm, values_hbm, gate_out_hbm, filters_hbm, skip_ref,
    in_hi_h, in_lo_h, of_hi_h, of_lo_h, cos_h, sin_h, ac_hi_h, ac_lo_h, fourth_h,
    home_out, filters_out, mixed_out,
    gate_in, values, filters, in_hi, in_lo, of_hi, of_lo, cos, sin, ac_hi, ac_lo, fourth,
    w_ring, w_mine, w_other, g_ring, g_other, own, hold, part, inbox, relay, final,
    near_gate, back_bf, gated, gated_in, stage, crossed, pair_in,
    y_ref, z_ref, u_ref, spec_r, spec_g, spec_p, spec_f, leaving, landed,
    send_sems, recv_sems, local_sems,
):
    s, h = lax.axis_index("seq"), lax.axis_index("ch")
    z, x = s // XS, s % XS
    y, core = h // 2, h % 2

    def zmod(d):
        return lax.rem(z + d + ZS, ZS)

    def xmod(d):
        return lax.rem(x + d + XS, XS)

    def at_z(d):
        return (zmod(d) * XS + x, h)

    def at_x(d):
        return (z * XS + xmod(d), h)

    def at_y(d):
        return (s, lax.rem(y + d + YS, YS) * 2 + core)

    sibling = (s, y * 2 + 1 - core)
    peers = [at_z(d) for d in range(1, ZS)] + [at_x(d) for d in range(1, XS)]
    peers += [at_y(d) for d in (1, -1)] + [sibling]

    barrier = pltpu.get_barrier_semaphore()
    for peer in peers:
        pl.semaphore_signal(barrier, inc=1, device_id=peer, device_id_type=MESH)

    loads = []

    def load(src, dst):
        copy = pltpu.make_async_copy(src, dst, local_sems.at[len(loads)])
        copy.start()
        loads.append(copy)
        return copy

    w_load = load(w_hbm, w_ring.at[z])
    g_load = load(g_hbm, g_ring.at[x])
    pair_loads = [load(gate_in_hbm, gate_in), load(values_hbm, values), load(filters_hbm, filters)]
    gate_load = load(gate_out_hbm.at[x], near_gate.at[0])
    table_loads = [
        load(src, dst)
        for src, dst in (
            (in_hi_h, in_hi), (in_lo_h, in_lo), (ac_hi_h, ac_hi), (ac_lo_h, ac_lo),
            (cos_h, cos), (sin_h, sin), (fourth_h, fourth), (of_hi_h, of_hi), (of_lo_h, of_lo),
        )
    ]
    pl.semaphore_wait(barrier, len(peers))

    copies = []

    def send(src, dst, device):
        k = len(copies)
        copy = pltpu.make_async_remote_copy(
            src_ref=src, dst_ref=dst, send_sem=send_sems.at[k], recv_sem=recv_sems.at[k],
            device_id=device, device_id_type=MESH,
        )
        copy.start()
        copies.append(copy)
        return copy

    half_w = w_ring.shape[1] // 2
    half_g = g_ring.shape[1] // 2
    first, second = pl.ds(0, half_w), pl.ds(half_w, half_w)
    top, low = pl.ds(0, half_g), pl.ds(half_g, half_g)

    up = send(w_hbm, w_ring.at[z], at_z(1))
    down = send(w_hbm, w_ring.at[z], at_z(-1))
    right_top = send(g_hbm.at[top], g_ring.at[x, top], at_x(1))
    left_low = send(g_hbm.at[low], g_ring.at[x, low], at_x(-1))
    right_low = send(g_hbm.at[low], g_ring.at[x, low], at_x(1))
    left_top = send(g_hbm.at[top], g_ring.at[x, top], at_x(-1))
    shared = [send(g_hbm, g_other.at[0], sibling)]
    for copy in pair_loads:
        copy.wait()
    for i in range(XS):
        product = gate_in[i].astype(jnp.float32) * values[i].astype(jnp.float32)
        stage[0, i] = product.astype(BF)
        stage[1, i] = filters[i].astype(BF)

    up.wait_recv()
    up = send(w_ring.at[zmod(-1)], w_ring.at[zmod(-1)], at_z(1))
    down.wait_recv()
    down = send(w_ring.at[zmod(1)], w_ring.at[zmod(1)], at_z(-1))
    right_top.wait_recv()
    far_top = send(g_ring.at[xmod(-1), top], g_ring.at[xmod(-1), top], at_x(1))
    left_low.wait_recv()
    far_low = send(g_ring.at[xmod(1), low], g_ring.at[xmod(1), low], at_x(-1))
    up.wait_recv()
    up = send(w_ring.at[zmod(-2)], w_ring.at[zmod(-2)], at_z(1))
    down.wait_recv()
    down = send(w_ring.at[zmod(2)], w_ring.at[zmod(2)], at_z(-1))
    over_z = {}
    over_x = {}

    def pair_z(i, start, size):
        at = pl.ds(start, size)
        over_z.setdefault(i, []).extend(
            send(stage.at[i, at, zmod(d)], crossed.at[i, z, at], at_z(d)) for d in range(1, ZS)
        )
        crossed[i, z, at] = stage[i, at, z]

    def pair_x(i):
        for copy in over_z[i]:
            copy.wait_recv()
        over_x[i] = [
            send(crossed.at[i, :, xmod(d)], pair_in.at[i, :, x], at_x(d)) for d in range(1, XS)
        ]
        pair_in[i, :, x] = crossed[i, :, x]

    up.wait_recv()
    up = send(w_ring.at[zmod(-3), first], w_ring.at[zmod(-3), first], at_z(1))
    down.wait_recv()
    down = send(w_ring.at[zmod(3), second], w_ring.at[zmod(3), second], at_z(-1))
    pair_z(1, 0, XS)
    right_low.wait_recv()
    shared.append(send(g_ring.at[xmod(-1)], g_other.at[1], sibling))
    left_top.wait_recv()
    shared.append(send(g_ring.at[xmod(1)], g_other.at[2], sibling))
    w_load.wait()
    g_load.wait()
    up.wait_recv()
    down.wait_recv()
    pair_z(0, 0, XS // 2)

    def rows_for(d, of_core):
        return lax.rem(y + d, YS) * 2 + of_core

    w_shared = [
        send(w_ring.at[rows_for(d, 1 - core)], w_other.at[d], sibling) for d in range(YS)
    ]
    for d in range(YS):
        w_mine[d] = w_ring[rows_for(d, core)]
    for copy in w_shared:
        copy.wait_recv()

    offsets = (0, -1, 1, 2)
    parts = []
    passed = []
    gates = []
    deep = w_ring.shape[1]
    wide = (YS * deep, w_ring.shape[2])

    def pass_on(n):
        for side in range(2):
            parts[n][side].wait_recv()
            relay[n, side] = (hold[n, side] + inbox[n, side, 0].astype(jnp.float32)).astype(BF)
            passed.append(send(relay.at[n, side], final.at[n, side], at_y(1 - 2 * side)))

    for n, off in enumerate(offsets):
        if n == 3:
            far_top.wait_recv()
            far_low.wait_recv()
            gates.extend(
                send(gate_out_hbm.at[xmod(d)], near_gate.at[d], at_x(d)) for d in range(1, XS)
            )
            shared.append(send(g_ring.at[xmod(2)], g_other.at[3], sibling))
        shared[n].wait_recv()

        @pl.loop(0, g_ring.shape[1] // CHUNK)
        def _(i, n=n, off=off):
            at = pl.ds(pl.multiple_of(i * CHUNK, CHUNK), CHUNK)
            form = (((1,), (1,)), ((), ()))
            total = lax.dot_general(
                w_mine[...].reshape(wide), g_ring[xmod(off), at, :], form,
                preferred_element_type=jnp.float32,
            ) + lax.dot_general(
                w_other[...].reshape(wide), g_other[n, at, :], form,
                preferred_element_type=jnp.float32,
            )
            total = total.reshape(YS, deep, CHUNK)
            own[n, :, at] = total[0]
            hold[n, 0, :, at] = total[1, :half_w]
            hold[n, 1, :, at] = total[3, half_w:]
            part[n, 0, 0, :, at] = total[2, :half_w].astype(BF)
            part[n, 0, 1, :, at] = total[1, half_w:].astype(BF)
            part[n, 1, 0, :, at] = total[2, half_w:].astype(BF)
            part[n, 1, 1, :, at] = total[3, :half_w].astype(BF)

        parts.append([send(part.at[n, side], inbox.at[n, side], at_y(1 - 2 * side)) for side in range(2)])

    arrivals = []
    homes = []

    def total_up(n):
        off = offsets[n]
        for copy in passed[2 * n : 2 * n + 2]:
            copy.wait_recv()
        d = -off % XS
        if d:
            gates[d - 1].wait_recv()
        else:
            gate_load.wait()
        upper = own[n, :half_w] + final[n, 0].astype(jnp.float32) + inbox[n, 1, 1].astype(jnp.float32)
        lower = own[n, half_w:] + final[n, 1].astype(jnp.float32) + inbox[n, 0, 1].astype(jnp.float32)
        back = jnp.concatenate([upper, lower], 0)
        result = back * near_gate[d].astype(jnp.float32)
        gated[n] = result.astype(BF).reshape(gated.shape[1:])
        for d in range(1, ZS):
            arrivals.append(send(gated.at[n, zmod(d)], gated_in.at[z, xmod(off)], at_z(d)))
        gated_in[z, xmod(off)] = gated[n, z]
        back_bf[n] = back.astype(BF)

    inner = g_ring.shape[2]
    rows = g_ring.shape[1]
    into, twist, across = (in_hi, in_lo), (cos, sin), (ac_hi, ac_lo)

    def pair_block(i):
        return lambda at: pair_in[i, :, :, :, at].reshape(rows, CHUNK)

    pass_on(0)
    pass_on(1)
    pass_on(2)
    total_up(0)
    pass_on(3)
    total_up(1)
    total_up(2)
    pair_x(1)
    total_up(3)
    pair_z(0, XS // 2, XS // 2)
    for copy in table_loads:
        copy.wait()
    for copy in over_x[1]:
        copy.wait_recv()
    forward(pair_block(1), into, twist, fourth, across, y_ref, z_ref, spec_f)
    home_out[x] = back_bf[0]
    for copy in arrivals:
        copy.wait_recv()
    forward(
        lambda at: gated_in[:, :, :, at].reshape(rows, CHUNK),
        into, twist, fourth, across, y_ref, z_ref, spec_g,
    )

    width = gated_in.shape[2]
    lanes = skip_ref.shape[1]
    pick = lax.broadcasted_iota(jnp.int32, (width, lanes), 1) == z * width + lax.broadcasted_iota(
        jnp.int32, (width, lanes), 0
    )
    scale = jnp.sum(jnp.where(pick, skip_ref[pl.ds(x, 1), :], 0.0), axis=1, keepdims=True)
    gone = []
    turns = []

    def turn_x(k):
        for copy in gone[k]:
            copy.wait_recv()
        which, c = divmod(k, 2)
        result = (mixed_out, filters_out)[which]
        at = pl.ds(c * CHUNK, CHUNK)
        turns.extend(
            send(landed.at[k, :, xmod(d)], result.at[x, :, :, at], at_x(d))
            for d in range(1, XS)
        )
        result[x, :, :, at] = landed[k, :, x]

    def leave(k):
        which, c = divmod(k, 2)
        if c == 0:
            combine(spec_g, (spec_f, spec_p)[which], z_ref)
            columns(z_ref, across, spec_r)
            unfold(spec_r, twist, fourth, u_ref)
        at = pl.ds(c * CHUNK, CHUNK)
        u = u_ref[:, at]
        out = (dot(of_hi[...], u) + dot(of_lo[...], u)).reshape(leaving.shape[1:])
        if which == 0:
            out = out + scale * gated_in[:, :, :, at].astype(jnp.float32)
        leaving[k] = out.astype(BF)
        gone.append(
            [send(leaving.at[k, zmod(d)], landed.at[k, z], at_z(d)) for d in range(1, ZS)]
        )
        landed[k, z] = leaving[k, z]

    leave(0)
    pair_x(0)
    leave(1)
    for n, off in enumerate(offsets):
        if n:
            homes.append(send(back_bf.at[n], home_out.at[x], at_x(off)))
    for copy in over_x[0]:
        copy.wait_recv()
    forward(pair_block(0), into, twist, fourth, across, y_ref, z_ref, spec_p)
    leave(2)
    turn_x(0)
    leave(3)
    turn_x(1)
    turn_x(2)
    turn_x(3)
    for copy in homes + turns:
        copy.wait_recv()
    for copy in copies:
        copy.wait_send()


def layer(grad_out, out_weight, gate_in, gate_out, values, filters, skip_scale):
    rows, inner = gate_in.shape
    deep, wide = out_weight.shape
    width = rows // (ZS * XS)
    into, out_of, cos, sin, across, fourth = make_tables(ZS * XS, width, inner)
    tables = (*into, *out_of, cos, sin, *across, fourth)
    spec_rows = cos.shape[0]
    split = (XS, ZS, width, inner)
    parts = inner // CHUNK
    count = 139

    def vmem(shape, dtype=BF):
        return pltpu.VMEM(shape, dtype)

    spec = vmem((4, spec_rows, inner // 2), jnp.float32)
    return pl.pallas_call(
        layer_kernel,
        out_shape=[
            jax.ShapeDtypeStruct((XS, deep, inner), BF),
            jax.ShapeDtypeStruct(split, BF),
            jax.ShapeDtypeStruct(split, BF),
        ],
        in_specs=[pl.BlockSpec(memory_space=pl.ANY)] * 6
        + [VMEM]
        + [pl.BlockSpec(memory_space=pl.ANY)] * len(tables),
        out_specs=[VMEM] * 3,
        scratch_shapes=[
            vmem(split),
            vmem(split),
            vmem(split, jnp.float32),
            *[vmem(t.shape, t.dtype) for t in tables],
            vmem((ZS, deep, wide)),
            vmem((YS, deep, wide)),
            vmem((YS, deep, wide)),
            vmem((XS,) + grad_out.shape),
            vmem((XS,) + grad_out.shape),
            vmem((XS, deep, inner), jnp.float32),
            vmem((XS, 2, deep // 2, inner), jnp.float32),
            vmem((XS, 2, 2, deep // 2, inner)),
            vmem((XS, 2, 2, deep // 2, inner)),
            vmem((XS, 2, deep // 2, inner)),
            vmem((XS, 2, deep // 2, inner)),
            vmem((XS, deep, inner)),
            vmem((XS, deep, inner)),
            vmem((XS, ZS, width, inner)),
            vmem((ZS, XS, width, inner)),
            vmem((2,) + split),
            vmem((2, ZS, XS, width, inner)),
            vmem((2, ZS, XS, width, inner)),
            vmem((2 * spec_rows, inner), jnp.float32),
            vmem((4, spec_rows, inner // 2)),
            vmem((2 * spec_rows, inner)),
            spec,
            spec,
            spec,
            spec,
            vmem((2 * parts, ZS, XS, width, CHUNK)),
            vmem((2 * parts, ZS, XS, width, CHUNK)),
            pltpu.SemaphoreType.DMA((count,)),
            pltpu.SemaphoreType.DMA((count,)),
            pltpu.SemaphoreType.DMA((15,)),
        ],
        compiler_params=pltpu.CompilerParams(
            collective_id=0, has_side_effects=True, vmem_limit_bytes=58 * 1024 * 1024
        ),
        cost_estimate=pl.CostEstimate(flops=10 * 10**9, bytes_accessed=20 * 10**6, transcendentals=0),
    )(
        out_weight,
        grad_out,
        gate_in.reshape(split),
        values.reshape(split),
        gate_out.reshape(XS, deep, inner),
        filters.reshape(split),
        skip_scale.reshape(XS, deep),
        *tables,
    )


def shards(grad_out, out_weight, gate_in, gate_out, values, conv_out, filters, skip_scale):
    rows, inner = gate_in.shape
    home, grad_filters, mixed = layer(
        grad_out, out_weight, gate_in, gate_out, values, filters, skip_scale
    )

    def wide(block):
        return block.reshape(rows, inner).astype(jnp.float32)

    grad_gate_out = (wide(home) * wide(conv_out)).astype(BF)
    grad_gate_in = (wide(mixed) * wide(values)).astype(BF)
    grad_values = (wide(mixed) * wide(gate_in)).astype(BF)
    return (grad_gate_in, grad_values, grad_gate_out, wide(grad_filters))


def solution(mesh):
    placed = (
        P("seq", "ch"),
        P("seq", "ch"),
        P("ch", "seq"),
        P("ch", "seq"),
        P("ch", "seq"),
        P("ch", "seq"),
        P("ch", "seq"),
        P("ch"),
    )
    return jax.shard_map(
        shards,
        mesh=mesh,
        in_specs=placed,
        out_specs=(P("ch", "seq"), P("ch", "seq"), P("ch", "seq"), P("ch", "seq")),
        check_vma=False,
    )
```

```python
import jax
import jax.numpy as jnp
import ml_dtypes
import numpy as np
from jax import lax
from jax.experimental import pallas as pl
from jax.experimental.pallas import tpu as pltpu
from jax.sharding import PartitionSpec as P

OUTER = 64
CHUNK = 256
STEP = 16


def split_pair(table):
    high = table.astype(np.float32).astype(ml_dtypes.bfloat16)
    low = (table - high.astype(np.float64)).astype(np.float32).astype(ml_dtypes.bfloat16)
    return high, low


def make_tables(blocks, width, inner):
    total = OUTER * inner
    half = OUTER // 2 + 1
    k = np.arange(half)
    a = np.arange(blocks)
    b = np.arange(inner)
    first = 2.0 * np.pi * (np.outer(k, a) % OUTER) / OUTER
    eye = np.eye(width)
    k_cos = np.kron(np.cos(first), eye)
    k_sin = np.kron(np.sin(first), eye)
    into = np.concatenate([k_cos, -k_sin], 0)
    weight = np.full((half, 1), 2.0)
    weight[0] = 1.0
    weight[-1] = 1.0
    weight = weight / total
    back_cos = np.kron((weight * np.cos(first)).T, eye)
    back_sin = np.kron((weight * np.sin(first)).T, eye)
    out_of = np.concatenate([back_cos, back_sin], 1)
    turn = 2.0 * np.pi * (np.outer(k, b) % total) / total
    turn = np.repeat(turn, width, axis=0)
    quarter = inner // 4
    c = np.arange(quarter)
    second = 2.0 * np.pi * (np.outer(c, c) % quarter) / quarter
    fourth = 2.0 * np.pi * np.outer(np.arange(4), c) / inner
    fourth = np.concatenate([np.cos(fourth), np.sin(fourth)], 0)
    c, s = np.cos(second), np.sin(second)
    across = np.concatenate([np.concatenate([c, -s], 1), np.concatenate([s, c], 1)], 0)
    return (
        split_pair(into),
        split_pair(out_of),
        np.cos(turn).astype(np.float32),
        np.sin(turn).astype(np.float32),
        split_pair(across),
        fourth.astype(np.float32),
    )


def dot(left, right):
    return jnp.dot(left, right, preferred_element_type=jnp.float32)


def turned(real, imag, cos, sin):
    return real * cos + imag * sin, imag * cos - real * sin


ZS, XS, YS = 8, 4, 4
VMEM = pl.BlockSpec(memory_space=pltpu.VMEM)
MESH = pl.DeviceIdType.MESH
BF = jnp.bfloat16


def four_way(parts):
    (re0, im0), (re1, im1), (re2, im2), (re3, im3) = parts
    sum_re, sum_im, dif_re, dif_im = re0 + re2, im0 + im2, re0 - re2, im0 - im2
    odd_re, odd_im, gap_re, gap_im = re1 + re3, im1 + im3, re1 - re3, im1 - im3
    return (
        (sum_re + odd_re, sum_im + odd_im),
        (dif_re + gap_im, dif_im - gap_re),
        (sum_re - odd_re, sum_im - odd_im),
        (dif_re - gap_im, dif_im + gap_re),
    )


def by_rows(rows, body):
    @pl.loop(0, rows // STEP, unroll=3)
    def _(i):
        body(pl.ds(pl.multiple_of(i * STEP, STEP), STEP), i * STEP)


def turn_fourth(part, fourth, r):
    if r == 0:
        return part
    return turned(*part, fourth[pl.ds(r, 1), :], fourth[pl.ds(4 + r, 1), :])


def forward(block_of, into, twist, fourth, across, y_ref, z_ref, out_ref):
    rows = z_ref.shape[1]
    quarter = z_ref.shape[2] // 2

    for c in range(y_ref.shape[1] // CHUNK):
        at = pl.ds(c * CHUNK, CHUNK)
        block = block_of(at)
        y_ref[:, at] = sum(dot(table[...], block) for table in into)

    def body(at, start):
        far = pl.ds(pl.multiple_of(rows + start, STEP), STEP)
        parts = []
        for q in range(4):
            col = pl.ds(q * quarter, quarter)
            parts.append(turned(y_ref[at, col], y_ref[far, col], twist[0][at, col], twist[1][at, col]))
        for r, part in enumerate(four_way(parts)):
            real, imag = turn_fourth(part, fourth, r)
            z_ref[r, at, :quarter] = real.astype(BF)
            z_ref[r, at, quarter:] = imag.astype(BF)

    by_rows(rows, body)
    columns(z_ref, across, out_ref)


def columns(z_ref, across, out_ref):
    for r in range(4):
        z = z_ref[r]
        out_ref[r] = sum(dot(z, table[...]) for table in across)


def combine(grad_ref, other_ref, z_ref):
    rows = z_ref.shape[1]
    quarter = z_ref.shape[2] // 2

    def body(at, _):
        for r in range(4):
            g_re, g_im = grad_ref[r, at, :quarter], grad_ref[r, at, quarter:]
            o_re, o_im = other_ref[r, at, :quarter], other_ref[r, at, quarter:]
            z_ref[r, at, :quarter] = (g_re * o_re + g_im * o_im).astype(BF)
            z_ref[r, at, quarter:] = (g_re * o_im - g_im * o_re).astype(BF)

    by_rows(rows, body)


def unfold(spec_ref, twist, fourth, u_ref):
    rows = spec_ref.shape[1]
    quarter = spec_ref.shape[2] // 2

    def body(at, start):
        far = pl.ds(pl.multiple_of(rows + start, STEP), STEP)
        parts = [
            turn_fourth((spec_ref[r, at, :quarter], spec_ref[r, at, quarter:]), fourth, r)
            for r in range(4)
        ]
        for q, part in enumerate(four_way(parts)):
            col = pl.ds(q * quarter, quarter)
            real, imag = turned(*part, twist[0][at, col], twist[1][at, col])
            u_ref[at, col] = real.astype(BF)
            u_ref[far, col] = imag.astype(BF)

    by_rows(rows, body)


def layer_kernel(
    w_hbm, g_hbm, gate_in_hbm, values_hbm, gate_out_hbm, filters_hbm, skip_ref,
    in_hi_h, in_lo_h, of_hi_h, of_lo_h, cos_h, sin_h, ac_hi_h, ac_lo_h, fourth_h,
    home_out, filters_out, mixed_out,
    gate_in, values, filters, in_hi, in_lo, of_hi, of_lo, cos, sin, ac_hi, ac_lo, fourth,
    w_ring, w_mine, w_other, g_ring, g_other, own, hold, part, inbox, relay, final,
    near_gate, back_bf, gated, gated_in, stage, crossed, pair_in,
    y_ref, z_ref, u_ref, spec_r, spec_g, spec_p, spec_f, leaving, landed,
    send_sems, recv_sems, local_sems,
):
    s, h = lax.axis_index("seq"), lax.axis_index("ch")
    z, x = s // XS, s % XS
    y, core = h // 2, h % 2

    def zmod(d):
        return lax.rem(z + d + ZS, ZS)

    def xmod(d):
        return lax.rem(x + d + XS, XS)

    def at_z(d):
        return (zmod(d) * XS + x, h)

    def at_x(d):
        return (z * XS + xmod(d), h)

    def at_y(d):
        return (s, lax.rem(y + d + YS, YS) * 2 + core)

    sibling = (s, y * 2 + 1 - core)
    peers = [at_z(d) for d in range(1, ZS)] + [at_x(d) for d in range(1, XS)]
    peers += [at_y(d) for d in (1, -1)] + [sibling]

    barrier = pltpu.get_barrier_semaphore()
    for peer in peers:
        pl.semaphore_signal(barrier, inc=1, device_id=peer, device_id_type=MESH)

    loads = []

    def load(src, dst):
        copy = pltpu.make_async_copy(src, dst, local_sems.at[len(loads)])
        copy.start()
        loads.append(copy)
        return copy

    w_load = load(w_hbm, w_ring.at[z])
    g_load = load(g_hbm, g_ring.at[x])
    pair_loads = [load(gate_in_hbm, gate_in), load(values_hbm, values), load(filters_hbm, filters)]
    gate_load = load(gate_out_hbm.at[x], near_gate.at[0])
    table_loads = [
        load(src, dst)
        for src, dst in (
            (in_hi_h, in_hi), (in_lo_h, in_lo), (ac_hi_h, ac_hi), (ac_lo_h, ac_lo),
            (cos_h, cos), (sin_h, sin), (fourth_h, fourth), (of_hi_h, of_hi), (of_lo_h, of_lo),
        )
    ]
    pl.semaphore_wait(barrier, len(peers))

    copies = []

    def send(src, dst, device):
        k = len(copies)
        copy = pltpu.make_async_remote_copy(
            src_ref=src, dst_ref=dst, send_sem=send_sems.at[k], recv_sem=recv_sems.at[k],
            device_id=device, device_id_type=MESH,
        )
        copy.start()
        copies.append(copy)
        return copy

    waited = [0]

    def flush(count):
        for copy in copies[waited[0] : count]:
            copy.wait_send()
        waited[0] = count

    half_w = w_ring.shape[1] // 2
    half_g = g_ring.shape[1] // 2
    first, second = pl.ds(0, half_w), pl.ds(half_w, half_w)
    top, low = pl.ds(0, half_g), pl.ds(half_g, half_g)

    up = send(w_hbm, w_ring.at[z], at_z(1))
    down = send(w_hbm, w_ring.at[z], at_z(-1))
    right_top = send(g_hbm.at[top], g_ring.at[x, top], at_x(1))
    left_low = send(g_hbm.at[low], g_ring.at[x, low], at_x(-1))
    right_low = send(g_hbm.at[low], g_ring.at[x, low], at_x(1))
    left_top = send(g_hbm.at[top], g_ring.at[x, top], at_x(-1))
    shared = [send(g_hbm, g_other.at[0], sibling)]
    for copy in pair_loads:
        copy.wait()
    for i in range(XS):
        product = gate_in[i].astype(jnp.float32) * values[i].astype(jnp.float32)
        stage[0, i] = product.astype(BF)
        stage[1, i] = filters[i].astype(BF)

    up.wait_recv()
    up = send(w_ring.at[zmod(-1)], w_ring.at[zmod(-1)], at_z(1))
    down.wait_recv()
    down = send(w_ring.at[zmod(1)], w_ring.at[zmod(1)], at_z(-1))
    right_top.wait_recv()
    far_top = send(g_ring.at[xmod(-1), top], g_ring.at[xmod(-1), top], at_x(1))
    left_low.wait_recv()
    far_low = send(g_ring.at[xmod(1), low], g_ring.at[xmod(1), low], at_x(-1))
    up.wait_recv()
    up = send(w_ring.at[zmod(-2)], w_ring.at[zmod(-2)], at_z(1))
    down.wait_recv()
    down = send(w_ring.at[zmod(2)], w_ring.at[zmod(2)], at_z(-1))
    over_z = {}
    over_x = {}

    def pair_z(i, start, size):
        at = pl.ds(start, size)
        over_z.setdefault(i, []).extend(
            send(stage.at[i, at, zmod(d)], crossed.at[i, z, at], at_z(d)) for d in range(1, ZS)
        )
        crossed[i, z, at] = stage[i, at, z]

    def pair_x(i):
        for copy in over_z[i]:
            copy.wait_recv()
        over_x[i] = [
            send(crossed.at[i, :, xmod(d)], pair_in.at[i, :, x], at_x(d)) for d in range(1, XS)
        ]
        pair_in[i, :, x] = crossed[i, :, x]

    up.wait_recv()
    up = send(w_ring.at[zmod(-3), first], w_ring.at[zmod(-3), first], at_z(1))
    down.wait_recv()
    down = send(w_ring.at[zmod(3), second], w_ring.at[zmod(3), second], at_z(-1))
    pair_z(1, 0, XS)
    right_low.wait_recv()
    shared.append(send(g_ring.at[xmod(-1)], g_other.at[1], sibling))
    left_top.wait_recv()
    shared.append(send(g_ring.at[xmod(1)], g_other.at[2], sibling))
    w_load.wait()
    g_load.wait()
    up.wait_recv()
    down.wait_recv()
    pair_z(0, 0, XS // 2)

    def rows_for(d, of_core):
        return lax.rem(y + d, YS) * 2 + of_core

    w_shared = [
        send(w_ring.at[rows_for(d, 1 - core)], w_other.at[d], sibling) for d in range(YS)
    ]
    for d in range(YS):
        w_mine[d] = w_ring[rows_for(d, core)]
    for copy in w_shared:
        copy.wait_recv()

    offsets = (0, -1, 1, 2)
    parts = []
    passed = []
    gates = []
    deep = w_ring.shape[1]
    wide = (YS * deep, w_ring.shape[2])

    def pass_on(n):
        for side in range(2):
            parts[n][side].wait_recv()
            relay[n, side] = (hold[n, side] + inbox[n, side, 0].astype(jnp.float32)).astype(BF)
            passed.append(send(relay.at[n, side], final.at[n, side], at_y(1 - 2 * side)))

    for n, off in enumerate(offsets):
        if n == 3:
            far_top.wait_recv()
            far_low.wait_recv()
            gates.extend(
                send(gate_out_hbm.at[xmod(d)], near_gate.at[d], at_x(d)) for d in range(1, XS)
            )
            shared.append(send(g_ring.at[xmod(2)], g_other.at[3], sibling))
        shared[n].wait_recv()

        @pl.loop(0, g_ring.shape[1] // CHUNK)
        def _(i, n=n, off=off):
            at = pl.ds(pl.multiple_of(i * CHUNK, CHUNK), CHUNK)
            form = (((1,), (1,)), ((), ()))
            total = lax.dot_general(
                w_mine[...].reshape(wide), g_ring[xmod(off), at, :], form,
                preferred_element_type=jnp.float32,
            ) + lax.dot_general(
                w_other[...].reshape(wide), g_other[n, at, :], form,
                preferred_element_type=jnp.float32,
            )
            total = total.reshape(YS, deep, CHUNK)
            own[n, :, at] = total[0]
            hold[n, 0, :, at] = total[1, :half_w]
            hold[n, 1, :, at] = total[3, half_w:]
            part[n, 0, 0, :, at] = total[2, :half_w].astype(BF)
            part[n, 0, 1, :, at] = total[1, half_w:].astype(BF)
            part[n, 1, 0, :, at] = total[2, half_w:].astype(BF)
            part[n, 1, 1, :, at] = total[3, :half_w].astype(BF)

        parts.append([send(part.at[n, side], inbox.at[n, side], at_y(1 - 2 * side)) for side in range(2)])

    arrivals = []
    homes = []

    def total_up(n):
        for copy in passed[2 * n : 2 * n + 2]:
            copy.wait_recv()
        d = -offsets[n] % XS
        if d:
            gates[d - 1].wait_recv()
        else:
            gate_load.wait()
        upper = own[n, :half_w] + final[n, 0].astype(jnp.float32) + inbox[n, 1, 1].astype(jnp.float32)
        lower = own[n, half_w:] + final[n, 1].astype(jnp.float32) + inbox[n, 0, 1].astype(jnp.float32)
        back = jnp.concatenate([upper, lower], 0)
        result = back * near_gate[d].astype(jnp.float32)
        gated[n] = result.astype(BF).reshape(gated.shape[1:])
        gated_in[z, n] = gated[n, z]
        if n % 2:
            both = pl.ds(n - 1, 2)
            for d in range(1, ZS):
                arrivals.append(send(gated.at[both, zmod(d)], gated_in.at[z, both], at_z(d)))
        back_bf[n] = back.astype(BF)

    inner = g_ring.shape[2]
    rows = g_ring.shape[1]
    into, twist, across = (in_hi, in_lo), (cos, sin), (ac_hi, ac_lo)

    def pair_block(i):
        return lambda at: pair_in[i, :, :, :, at].reshape(rows, CHUNK)

    early = len(copies)
    pass_on(0)
    pass_on(1)
    pass_on(2)
    total_up(0)
    pass_on(3)
    total_up(1)
    total_up(2)
    pair_x(1)
    total_up(3)
    pair_z(0, XS // 2, XS // 2)
    for copy in table_loads:
        copy.wait()
    for copy in over_x[1]:
        copy.wait_recv()
    forward(pair_block(1), into, twist, fourth, across, y_ref, z_ref, spec_f)
    stays = [load(back_bf.at[0], home_out.at[x])]
    flush(early)

    def gated_block(at):
        blocks = []
        for i in range(XS):
            e = lax.rem(i - x + XS, XS)
            blocks.append(gated_in[:, 2 * e - e // 2 - 4 * (e // 3), :, at])
        return jnp.stack(blocks, 1).reshape(rows, CHUNK)

    for copy in arrivals:
        copy.wait_recv()
    forward(
        gated_block,
        into, twist, fourth, across, y_ref, z_ref, spec_g,
    )

    width = gated_in.shape[2]
    lanes = skip_ref.shape[1]
    pick = lax.broadcasted_iota(jnp.int32, (width, lanes), 1) == z * width + lax.broadcasted_iota(
        jnp.int32, (width, lanes), 0
    )
    scale = jnp.sum(jnp.where(pick, skip_ref[pl.ds(x, 1), :], 0.0), axis=1, keepdims=True)
    gone = []
    turns = []

    def turn_x(k):
        which, at = groups[k]
        result = (mixed_out, filters_out)[which]
        for copy in gone[k]:
            copy.wait_recv()
        turns.extend(
            send(landed.at[which, :, xmod(d), :, at], result.at[x, :, :, at], at_x(d))
            for d in range(1, XS)
        )
        stays.append(load(landed.at[which, :, x, :, at], result.at[x, :, :, at]))

    groups = []

    def leave(which, start, size):
        if start == 0:
            combine(spec_g, (spec_f, spec_p)[which], z_ref)
            columns(z_ref, across, spec_r)
            unfold(spec_r, twist, fourth, u_ref)
        for c in range(start, start + size, CHUNK):
            at = pl.ds(c, CHUNK)
            u = u_ref[:, at]
            out = dot(of_hi[...], u) + dot(of_lo[...], u)
            if which == 0:
                out = out.reshape(ZS * XS, width, CHUNK)
                out = out + scale * gated_block(at).reshape(out.shape).astype(jnp.float32)
            leaving[which, :, :, :, at] = out.astype(BF).reshape(ZS, XS, width, CHUNK)
        at = pl.ds(start, size)
        groups.append((which, at))
        gone.append(
            [
                send(leaving.at[which, zmod(d), :, :, at], landed.at[which, z, :, :, at], at_z(d))
                for d in range(1, ZS)
            ]
        )
        landed[which, z, :, :, at] = leaving[which, z, :, :, at]

    leave(0, 0, inner)
    pair_x(0)
    for n, off in enumerate(offsets):
        if n:
            homes.append(send(back_bf.at[n], home_out.at[x], at_x(off)))
    for copy in over_x[0]:
        copy.wait_recv()
    forward(pair_block(0), into, twist, fourth, across, y_ref, z_ref, spec_p)
    middle = len(copies)
    leave(1, 0, CHUNK)
    leave(1, CHUNK, CHUNK)
    turn_x(0)
    flush(middle)
    turn_x(1)
    turn_x(2)
    for copy in stays:
        copy.wait()
    for copy in homes + turns:
        copy.wait_recv()
    flush(len(copies))
    assert len(copies) == send_sems.shape[0]
    assert len(loads) == local_sems.shape[0]


def layer(grad_out, out_weight, gate_in, gate_out, values, filters, skip_scale):
    rows, inner = gate_in.shape
    deep, wide = out_weight.shape
    width = rows // (ZS * XS)
    into, out_of, cos, sin, across, fourth = make_tables(ZS * XS, width, inner)
    tables = (*into, *out_of, cos, sin, *across, fourth)
    spec_rows = cos.shape[0]
    split = (XS, ZS, width, inner)
    count = 115

    def vmem(shape, dtype=BF):
        return pltpu.VMEM(shape, dtype)

    spec = vmem((4, spec_rows, inner // 2), jnp.float32)
    return pl.pallas_call(
        layer_kernel,
        out_shape=[
            jax.ShapeDtypeStruct((XS, deep, inner), BF),
            jax.ShapeDtypeStruct(split, BF),
            jax.ShapeDtypeStruct(split, BF),
        ],
        in_specs=[pl.BlockSpec(memory_space=pl.ANY)] * 6
        + [VMEM]
        + [pl.BlockSpec(memory_space=pl.ANY)] * len(tables),
        out_specs=[pl.BlockSpec(memory_space=pl.ANY)] * 3,
        scratch_shapes=[
            vmem(split),
            vmem(split),
            vmem(split, jnp.float32),
            *[vmem(t.shape, t.dtype) for t in tables],
            vmem((ZS, deep, wide)),
            vmem((YS, deep, wide)),
            vmem((YS, deep, wide)),
            vmem((XS,) + grad_out.shape),
            vmem((XS,) + grad_out.shape),
            vmem((XS, deep, inner), jnp.float32),
            vmem((XS, 2, deep // 2, inner), jnp.float32),
            vmem((XS, 2, 2, deep // 2, inner)),
            vmem((XS, 2, 2, deep // 2, inner)),
            vmem((XS, 2, deep // 2, inner)),
            vmem((XS, 2, deep // 2, inner)),
            vmem((XS, deep, inner)),
            vmem((XS, deep, inner)),
            vmem((XS, ZS, width, inner)),
            vmem((ZS, XS, width, inner)),
            vmem((2,) + split),
            vmem((2, ZS, XS, width, inner)),
            vmem((2, ZS, XS, width, inner)),
            vmem((2 * spec_rows, inner), jnp.float32),
            vmem((4, spec_rows, inner // 2)),
            vmem((2 * spec_rows, inner)),
            spec,
            spec,
            spec,
            spec,
            vmem((2, ZS, XS, width, inner)),
            vmem((2, ZS, XS, width, inner)),
            pltpu.SemaphoreType.DMA((count,)),
            pltpu.SemaphoreType.DMA((count,)),
            pltpu.SemaphoreType.DMA((19,)),
        ],
        compiler_params=pltpu.CompilerParams(
            collective_id=0, has_side_effects=True, vmem_limit_bytes=58 * 1024 * 1024
        ),
        cost_estimate=pl.CostEstimate(flops=10 * 10**9, bytes_accessed=20 * 10**6, transcendentals=0),
    )(
        out_weight,
        grad_out,
        gate_in.reshape(split),
        values.reshape(split),
        gate_out.reshape(XS, deep, inner),
        filters.reshape(split),
        skip_scale.reshape(XS, deep),
        *tables,
    )


def shards(grad_out, out_weight, gate_in, gate_out, values, conv_out, filters, skip_scale):
    rows, inner = gate_in.shape
    home, grad_filters, mixed = layer(
        grad_out, out_weight, gate_in, gate_out, values, filters, skip_scale
    )

    def wide(block):
        return block.reshape(rows, inner).astype(jnp.float32)

    grad_gate_out = (wide(home) * wide(conv_out)).astype(BF)
    grad_gate_in = (wide(mixed) * wide(values)).astype(BF)
    grad_values = (wide(mixed) * wide(gate_in)).astype(BF)
    return (grad_gate_in, grad_values, grad_gate_out, wide(grad_filters))


def solution(mesh):
    placed = (
        P("seq", "ch"),
        P("seq", "ch"),
        P("ch", "seq"),
        P("ch", "seq"),
        P("ch", "seq"),
        P("ch", "seq"),
        P("ch", "seq"),
        P("ch"),
    )
    return jax.shard_map(
        shards,
        mesh=mesh,
        in_specs=placed,
        out_specs=(P("ch", "seq"), P("ch", "seq"), P("ch", "seq"), P("ch", "seq")),
        check_vma=False,
    )
```

```python
import jax
import jax.numpy as jnp
import ml_dtypes
import numpy as np
from jax import lax
from jax.experimental import pallas as pl
from jax.experimental.pallas import tpu as pltpu
from jax.sharding import PartitionSpec as P

OUTER = 64
CHUNK = 256
STEP = 16


def split_pair(table):
    high = table.astype(np.float32).astype(ml_dtypes.bfloat16)
    low = (table - high.astype(np.float64)).astype(np.float32).astype(ml_dtypes.bfloat16)
    return high, low


def make_tables(blocks, width, inner):
    total = OUTER * inner
    half = OUTER // 2 + 1
    k = np.arange(half)
    a = np.arange(blocks)
    b = np.arange(inner)
    first = 2.0 * np.pi * (np.outer(k, a) % OUTER) / OUTER
    eye = np.eye(width)
    k_cos = np.kron(np.cos(first), eye)
    k_sin = np.kron(np.sin(first), eye)
    into = np.concatenate([k_cos, -k_sin], 0)
    weight = np.full((half, 1), 2.0)
    weight[0] = 1.0
    weight[-1] = 1.0
    weight = weight / total
    back_cos = np.kron((weight * np.cos(first)).T, eye)
    back_sin = np.kron((weight * np.sin(first)).T, eye)
    out_of = np.concatenate([back_cos, back_sin], 1)
    turn = 2.0 * np.pi * (np.outer(k, b) % total) / total
    turn = np.repeat(turn, width, axis=0)
    quarter = inner // 4
    c = np.arange(quarter)
    second = 2.0 * np.pi * (np.outer(c, c) % quarter) / quarter
    fourth = 2.0 * np.pi * np.outer(np.arange(4), c) / inner
    fourth = np.concatenate([np.cos(fourth), np.sin(fourth)], 0)
    c, s = np.cos(second), np.sin(second)
    across = np.concatenate([np.concatenate([c, -s], 1), np.concatenate([s, c], 1)], 0)
    return (
        split_pair(into),
        split_pair(out_of),
        np.cos(turn).astype(np.float32),
        np.sin(turn).astype(np.float32),
        split_pair(across),
        fourth.astype(np.float32),
    )


def dot(left, right):
    return jnp.dot(left, right, preferred_element_type=jnp.float32)


def turned(real, imag, cos, sin):
    return real * cos + imag * sin, imag * cos - real * sin


ZS, XS, YS = 8, 4, 4
VMEM = pl.BlockSpec(memory_space=pltpu.VMEM)
MESH = pl.DeviceIdType.MESH
BF = jnp.bfloat16


def four_way(parts):
    (re0, im0), (re1, im1), (re2, im2), (re3, im3) = parts
    sum_re, sum_im, dif_re, dif_im = re0 + re2, im0 + im2, re0 - re2, im0 - im2
    odd_re, odd_im, gap_re, gap_im = re1 + re3, im1 + im3, re1 - re3, im1 - im3
    return (
        (sum_re + odd_re, sum_im + odd_im),
        (dif_re + gap_im, dif_im - gap_re),
        (sum_re - odd_re, sum_im - odd_im),
        (dif_re - gap_im, dif_im + gap_re),
    )


def by_rows(rows, body):
    @pl.loop(0, rows // STEP, unroll=3)
    def _(i):
        body(pl.ds(pl.multiple_of(i * STEP, STEP), STEP), i * STEP)


def turn_fourth(part, fourth, r):
    if r == 0:
        return part
    return turned(*part, fourth[pl.ds(r, 1), :], fourth[pl.ds(4 + r, 1), :])


def forward(block_of, into, twist, fourth, across, y_ref, z_ref, out_ref):
    rows = z_ref.shape[1]
    quarter = z_ref.shape[2] // 2

    for c in range(y_ref.shape[1] // CHUNK):
        at = pl.ds(c * CHUNK, CHUNK)
        block = block_of(at)
        y_ref[:, at] = sum(dot(table[...], block) for table in into)

    def body(at, start):
        far = pl.ds(pl.multiple_of(rows + start, STEP), STEP)
        parts = []
        for q in range(4):
            col = pl.ds(q * quarter, quarter)
            parts.append(turned(y_ref[at, col], y_ref[far, col], twist[0][at, col], twist[1][at, col]))
        for r, part in enumerate(four_way(parts)):
            real, imag = turn_fourth(part, fourth, r)
            z_ref[r, at, :quarter] = real.astype(BF)
            z_ref[r, at, quarter:] = imag.astype(BF)

    by_rows(rows, body)
    columns(z_ref, across, out_ref)


def columns(z_ref, across, out_ref):
    for r in range(4):
        z = z_ref[r]
        out_ref[r] = sum(dot(z, table[...]) for table in across)


def combine(grad_ref, other_ref, z_ref):
    rows = z_ref.shape[1]
    quarter = z_ref.shape[2] // 2

    def body(at, _):
        for r in range(4):
            g_re, g_im = grad_ref[r, at, :quarter], grad_ref[r, at, quarter:]
            o_re, o_im = other_ref[r, at, :quarter], other_ref[r, at, quarter:]
            z_ref[r, at, :quarter] = (g_re * o_re + g_im * o_im).astype(BF)
            z_ref[r, at, quarter:] = (g_re * o_im - g_im * o_re).astype(BF)

    by_rows(rows, body)


def unfold(spec_ref, twist, fourth, u_ref):
    rows = spec_ref.shape[1]
    quarter = spec_ref.shape[2] // 2

    def body(at, start):
        far = pl.ds(pl.multiple_of(rows + start, STEP), STEP)
        parts = [
            turn_fourth((spec_ref[r, at, :quarter], spec_ref[r, at, quarter:]), fourth, r)
            for r in range(4)
        ]
        for q, part in enumerate(four_way(parts)):
            col = pl.ds(q * quarter, quarter)
            real, imag = turned(*part, twist[0][at, col], twist[1][at, col])
            u_ref[at, col] = real.astype(BF)
            u_ref[far, col] = imag.astype(BF)

    by_rows(rows, body)


def layer_kernel(
    w_hbm, g_hbm, gate_in_hbm, values_hbm, gate_out_hbm, filters_hbm, skip_ref,
    in_hi_h, in_lo_h, of_hi_h, of_lo_h, cos_h, sin_h, ac_hi_h, ac_lo_h, fourth_h,
    home_out, filters_out, mixed_out,
    gate_in, values, filters, in_hi, in_lo, of_hi, of_lo, cos, sin, ac_hi, ac_lo, fourth,
    w_ring, w_mine, w_other, g_ring, g_other, own, hold, part, inbox, relay, final,
    near_gate, back_bf, gated, gated_in, stage, crossed, pair_in,
    y_ref, z_ref, u_ref, spec_r, spec_g, spec_p, spec_f, leaving, landed,
    send_sems, recv_sems, local_sems,
):
    s, h = lax.axis_index("seq"), lax.axis_index("ch")
    z, x = s // XS, s % XS
    y, core = h // 2, h % 2

    def zmod(d):
        return lax.rem(z + d + ZS, ZS)

    def xmod(d):
        return lax.rem(x + d + XS, XS)

    def at_z(d):
        return (zmod(d) * XS + x, h)

    def at_x(d):
        return (z * XS + xmod(d), h)

    def at_y(d):
        return (s, lax.rem(y + d + YS, YS) * 2 + core)

    sibling = (s, y * 2 + 1 - core)
    peers = [at_z(d) for d in range(1, ZS)] + [at_x(d) for d in range(1, XS)]
    peers += [at_y(d) for d in (1, -1)] + [sibling]

    barrier = pltpu.get_barrier_semaphore()
    for peer in peers:
        pl.semaphore_signal(barrier, inc=1, device_id=peer, device_id_type=MESH)

    loads = []

    def load(src, dst):
        copy = pltpu.make_async_copy(src, dst, local_sems.at[len(loads)])
        copy.start()
        loads.append(copy)
        return copy

    w_load = load(w_hbm, w_ring.at[z])
    g_load = load(g_hbm, g_ring.at[x])
    pair_loads = [load(gate_in_hbm, gate_in), load(values_hbm, values), load(filters_hbm, filters)]
    gate_load = load(gate_out_hbm.at[x], near_gate.at[0])
    table_loads = [
        load(src, dst)
        for src, dst in (
            (in_hi_h, in_hi), (in_lo_h, in_lo), (ac_hi_h, ac_hi), (ac_lo_h, ac_lo),
            (cos_h, cos), (sin_h, sin), (fourth_h, fourth), (of_hi_h, of_hi), (of_lo_h, of_lo),
        )
    ]
    pl.semaphore_wait(barrier, len(peers))

    copies = []

    def send(src, dst, device):
        k = len(copies)
        copy = pltpu.make_async_remote_copy(
            src_ref=src, dst_ref=dst, send_sem=send_sems.at[k], recv_sem=recv_sems.at[k],
            device_id=device, device_id_type=MESH,
        )
        copy.start()
        copies.append(copy)
        return copy

    waited = [0]

    def flush(count):
        for copy in copies[waited[0] : count]:
            copy.wait_send()
        waited[0] = count

    half_w = w_ring.shape[1] // 2
    half_g = g_ring.shape[1] // 2
    first, second = pl.ds(0, half_w), pl.ds(half_w, half_w)
    top, low = pl.ds(0, half_g), pl.ds(half_g, half_g)

    halves = (first, second)
    ring = {}
    for side in (0, 1):
        for way in (1, -1):
            rows = halves[side if way == 1 else 1 - side]
            ring[way, side] = send(w_hbm.at[rows], w_ring.at[z, rows], at_z(way))
    right_top = send(g_hbm.at[top], g_ring.at[x, top], at_x(1))
    left_low = send(g_hbm.at[low], g_ring.at[x, low], at_x(-1))
    right_low = send(g_hbm.at[low], g_ring.at[x, low], at_x(1))
    left_top = send(g_hbm.at[top], g_ring.at[x, top], at_x(-1))
    shared = [send(g_hbm, g_other.at[0], sibling)]
    w_load.wait()
    for copy in pair_loads:
        copy.wait()
    for i in range(XS):
        product = gate_in[i].astype(jnp.float32) * values[i].astype(jnp.float32)
        stage[0, i] = product.astype(BF)
        stage[1, i] = filters[i].astype(BF)

    w_shared = []

    def step(r):
        for side in (0, 1):
            for way in (1, -1):
                if r == ZS // 2 and side:
                    continue
                ring[way, side].wait_recv()
                if r == ZS // 2 or (r == ZS // 2 - 1 and side):
                    continue
                block = w_ring.at[zmod(-r * way), halves[side if way == 1 else 1 - side]]
                ring[way, side] = send(block, block, at_z(way))
        even, odd = (0, 2, -2, 4)[r - 1], (1, -1, 3, -3)[r - 1]
        e = lax.rem(1 - core + z, 2)
        row = zmod(even + e * (odd - even))
        w_shared.append(send(w_ring.at[row], w_other.at[lax.rem(row // 2 - y + YS, YS)], sibling))

    step(1)
    right_top.wait_recv()
    far_top = send(g_ring.at[xmod(-1), top], g_ring.at[xmod(-1), top], at_x(1))
    left_low.wait_recv()
    far_low = send(g_ring.at[xmod(1), low], g_ring.at[xmod(1), low], at_x(-1))
    step(2)
    step(3)
    over_z = {}
    over_x = {}

    def pair_z(i, start, size):
        at = pl.ds(start, size)
        over_z.setdefault(i, []).extend(
            send(stage.at[i, at, zmod(d)], crossed.at[i, z, at], at_z(d)) for d in range(1, ZS)
        )
        crossed[i, z, at] = stage[i, at, z]

    def pair_x(i):
        for copy in over_z[i]:
            copy.wait_recv()
        over_x[i] = [
            send(crossed.at[i, :, xmod(d)], pair_in.at[i, :, x], at_x(d)) for d in range(1, XS)
        ]
        pair_in[i, :, x] = crossed[i, :, x]

    pair_z(1, 0, XS)
    right_low.wait_recv()
    shared.append(send(g_ring.at[xmod(-1)], g_other.at[1], sibling))
    left_top.wait_recv()
    shared.append(send(g_ring.at[xmod(1)], g_other.at[2], sibling))
    g_load.wait()
    step(4)
    pair_z(0, 0, XS)

    def rows_for(d, of_core):
        return lax.rem(y + d, YS) * 2 + of_core

    for d in range(YS):
        w_mine[d] = w_ring[rows_for(d, core)]
    for copy in w_shared:
        copy.wait_recv()

    offsets = (0, -1, 1, 2)
    parts = []
    passed = []
    gates = []
    deep = w_ring.shape[1]
    wide = (YS * deep, w_ring.shape[2])

    def pass_on(n):
        for side in range(2):
            parts[n][side].wait_recv()
            relay[n, side] = (hold[n, side] + inbox[n, side, 0].astype(jnp.float32)).astype(BF)
            passed.append(send(relay.at[n, side], final.at[n, side], at_y(1 - 2 * side)))

    for n, off in enumerate(offsets):
        if n == 3:
            far_top.wait_recv()
            far_low.wait_recv()
            gates.extend(
                send(gate_out_hbm.at[xmod(d)], near_gate.at[d], at_x(d)) for d in range(1, XS)
            )
            shared.append(send(g_ring.at[xmod(2)], g_other.at[3], sibling))
        shared[n].wait_recv()

        @pl.loop(0, g_ring.shape[1] // CHUNK)
        def _(i, n=n, off=off):
            at = pl.ds(pl.multiple_of(i * CHUNK, CHUNK), CHUNK)
            form = (((1,), (1,)), ((), ()))
            total = lax.dot_general(
                w_mine[...].reshape(wide), g_ring[xmod(off), at, :], form,
                preferred_element_type=jnp.float32,
            ) + lax.dot_general(
                w_other[...].reshape(wide), g_other[n, at, :], form,
                preferred_element_type=jnp.float32,
            )
            total = total.reshape(YS, deep, CHUNK)
            own[n, :, at] = total[0]
            hold[n, 0, :, at] = total[1, :half_w]
            hold[n, 1, :, at] = total[3, half_w:]
            part[n, 0, 0, :, at] = total[2, :half_w].astype(BF)
            part[n, 0, 1, :, at] = total[1, half_w:].astype(BF)
            part[n, 1, 0, :, at] = total[2, half_w:].astype(BF)
            part[n, 1, 1, :, at] = total[3, :half_w].astype(BF)

        parts.append([send(part.at[n, side], inbox.at[n, side], at_y(1 - 2 * side)) for side in range(2)])

    arrivals = []
    homes = []

    def total_up(n):
        for copy in passed[2 * n : 2 * n + 2]:
            copy.wait_recv()
        d = -offsets[n] % XS
        if d:
            gates[d - 1].wait_recv()
        else:
            gate_load.wait()
        upper = own[n, :half_w] + final[n, 0].astype(jnp.float32) + inbox[n, 1, 1].astype(jnp.float32)
        lower = own[n, half_w:] + final[n, 1].astype(jnp.float32) + inbox[n, 0, 1].astype(jnp.float32)
        back = jnp.concatenate([upper, lower], 0)
        result = back * near_gate[d].astype(jnp.float32)
        gated[n] = result.astype(BF).reshape(gated.shape[1:])
        gated_in[z, n] = gated[n, z]
        if n:
            some = pl.ds(0, 2) if n == 1 else pl.ds(n, 1)
            for d in range(1, ZS):
                arrivals.append(send(gated.at[some, zmod(d)], gated_in.at[z, some], at_z(d)))
        back_bf[n] = back.astype(BF)

    inner = g_ring.shape[2]
    rows = g_ring.shape[1]
    into, twist, across = (in_hi, in_lo), (cos, sin), (ac_hi, ac_lo)

    def pair_block(i):
        return lambda at: pair_in[i, :, :, :, at].reshape(rows, CHUNK)

    early = len(copies)
    pass_on(0)
    pass_on(1)
    pass_on(2)
    total_up(0)
    pass_on(3)
    total_up(1)
    total_up(2)
    pair_x(1)
    total_up(3)
    pair_x(0)
    for copy in table_loads:
        copy.wait()
    for copy in over_x[1]:
        copy.wait_recv()
    forward(pair_block(1), into, twist, fourth, across, y_ref, z_ref, spec_f)
    stays = [load(back_bf.at[0], home_out.at[x])]
    flush(early)

    def gated_block(at):
        blocks = []
        for i in range(XS):
            e = lax.rem(i - x + XS, XS)
            blocks.append(gated_in[:, 2 * e - e // 2 - 4 * (e // 3), :, at])
        return jnp.stack(blocks, 1).reshape(rows, CHUNK)

    for copy in arrivals:
        copy.wait_recv()
    forward(
        gated_block,
        into, twist, fourth, across, y_ref, z_ref, spec_g,
    )

    width = gated_in.shape[2]
    lanes = skip_ref.shape[1]
    pick = lax.broadcasted_iota(jnp.int32, (width, lanes), 1) == z * width + lax.broadcasted_iota(
        jnp.int32, (width, lanes), 0
    )
    scale = jnp.sum(jnp.where(pick, skip_ref[pl.ds(x, 1), :], 0.0), axis=1, keepdims=True)
    gone = []
    turns = []

    def turn_x(k):
        which, at = groups[k]
        result = (mixed_out, filters_out)[which]
        for copy in gone[k]:
            copy.wait_recv()
        turns.extend(
            send(landed.at[which, :, xmod(d), :, at], result.at[x, :, :, at], at_x(d))
            for d in range(1, XS)
        )
        stays.append(load(landed.at[which, :, x, :, at], result.at[x, :, :, at]))

    groups = []

    def leave(which, start, size):
        if start == 0:
            combine(spec_g, (spec_f, spec_p)[which], z_ref)
            columns(z_ref, across, spec_r)
            unfold(spec_r, twist, fourth, u_ref)
        for c in range(start, start + size, CHUNK):
            at = pl.ds(c, CHUNK)
            u = u_ref[:, at]
            out = dot(of_hi[...], u) + dot(of_lo[...], u)
            if which == 0:
                out = out.reshape(ZS * XS, width, CHUNK)
                out = out + scale * gated_block(at).reshape(out.shape).astype(jnp.float32)
            leaving[which, :, :, :, at] = out.astype(BF).reshape(ZS, XS, width, CHUNK)
        at = pl.ds(start, size)
        groups.append((which, at))
        gone.append(
            [
                send(leaving.at[which, zmod(d), :, :, at], landed.at[which, z, :, :, at], at_z(d))
                for d in range(1, ZS)
            ]
        )
        landed[which, z, :, :, at] = leaving[which, z, :, :, at]

    leave(0, 0, inner)
    for copy in over_x[0]:
        copy.wait_recv()
    forward(pair_block(0), into, twist, fourth, across, y_ref, z_ref, spec_p)
    for n, off in enumerate(offsets):
        if n:
            homes.append(send(back_bf.at[n], home_out.at[x], at_x(off)))
    middle = len(copies)
    leave(1, 0, CHUNK)
    leave(1, CHUNK, CHUNK)
    turn_x(0)
    flush(middle)
    turn_x(1)
    turn_x(2)
    for copy in stays:
        copy.wait()
    for copy in homes + turns:
        copy.wait_recv()
    flush(len(copies))
    assert len(copies) == send_sems.shape[0]
    assert len(loads) == local_sems.shape[0]


def layer(grad_out, out_weight, gate_in, gate_out, values, filters, skip_scale):
    rows, inner = gate_in.shape
    deep, wide = out_weight.shape
    width = rows // (ZS * XS)
    into, out_of, cos, sin, across, fourth = make_tables(ZS * XS, width, inner)
    tables = (*into, *out_of, cos, sin, *across, fourth)
    spec_rows = cos.shape[0]
    split = (XS, ZS, width, inner)
    count = 121

    def vmem(shape, dtype=BF):
        return pltpu.VMEM(shape, dtype)

    spec = vmem((4, spec_rows, inner // 2), jnp.float32)
    return pl.pallas_call(
        layer_kernel,
        out_shape=[
            jax.ShapeDtypeStruct((XS, deep, inner), BF),
            jax.ShapeDtypeStruct(split, BF),
            jax.ShapeDtypeStruct(split, BF),
        ],
        in_specs=[pl.BlockSpec(memory_space=pl.ANY)] * 6
        + [VMEM]
        + [pl.BlockSpec(memory_space=pl.ANY)] * len(tables),
        out_specs=[pl.BlockSpec(memory_space=pl.ANY)] * 3,
        scratch_shapes=[
            vmem(split),
            vmem(split),
            vmem(split, jnp.float32),
            *[vmem(t.shape, t.dtype) for t in tables],
            vmem((ZS, deep, wide)),
            vmem((YS, deep, wide)),
            vmem((YS, deep, wide)),
            vmem((XS,) + grad_out.shape),
            vmem((XS,) + grad_out.shape),
            vmem((XS, deep, inner), jnp.float32),
            vmem((XS, 2, deep // 2, inner), jnp.float32),
            vmem((XS, 2, 2, deep // 2, inner)),
            vmem((XS, 2, 2, deep // 2, inner)),
            vmem((XS, 2, deep // 2, inner)),
            vmem((XS, 2, deep // 2, inner)),
            vmem((XS, deep, inner)),
            vmem((XS, deep, inner)),
            vmem((XS, ZS, width, inner)),
            vmem((ZS, XS, width, inner)),
            vmem((2,) + split),
            vmem((2, ZS, XS, width, inner)),
            vmem((2, ZS, XS, width, inner)),
            vmem((2 * spec_rows, inner), jnp.float32),
            vmem((4, spec_rows, inner // 2)),
            vmem((2 * spec_rows, inner)),
            spec,
            spec,
            spec,
            spec,
            vmem((2, ZS, XS, width, inner)),
            vmem((2, ZS, XS, width, inner)),
            pltpu.SemaphoreType.DMA((count,)),
            pltpu.SemaphoreType.DMA((count,)),
            pltpu.SemaphoreType.DMA((19,)),
        ],
        compiler_params=pltpu.CompilerParams(
            collective_id=0, has_side_effects=True, vmem_limit_bytes=58 * 1024 * 1024
        ),
        cost_estimate=pl.CostEstimate(flops=10 * 10**9, bytes_accessed=20 * 10**6, transcendentals=0),
    )(
        out_weight,
        grad_out,
        gate_in.reshape(split),
        values.reshape(split),
        gate_out.reshape(XS, deep, inner),
        filters.reshape(split),
        skip_scale.reshape(XS, deep),
        *tables,
    )


def shards(grad_out, out_weight, gate_in, gate_out, values, conv_out, filters, skip_scale):
    rows, inner = gate_in.shape
    home, grad_filters, mixed = layer(
        grad_out, out_weight, gate_in, gate_out, values, filters, skip_scale
    )

    def wide(block):
        return block.reshape(rows, inner).astype(jnp.float32)

    grad_gate_out = (wide(home) * wide(conv_out)).astype(BF)
    grad_gate_in = (wide(mixed) * wide(values)).astype(BF)
    grad_values = (wide(mixed) * wide(gate_in)).astype(BF)
    return (grad_gate_in, grad_values, grad_gate_out, wide(grad_filters))


def solution(mesh):
    placed = (
        P("seq", "ch"),
        P("seq", "ch"),
        P("ch", "seq"),
        P("ch", "seq"),
        P("ch", "seq"),
        P("ch", "seq"),
        P("ch", "seq"),
        P("ch"),
    )
    return jax.shard_map(
        shards,
        mesh=mesh,
        in_specs=placed,
        out_specs=(P("ch", "seq"), P("ch", "seq"), P("ch", "seq"), P("ch", "seq")),
        check_vma=False,
    )
```

```python
import jax
import jax.numpy as jnp
import ml_dtypes
import numpy as np
from jax import lax
from jax.experimental import pallas as pl
from jax.experimental.pallas import tpu as pltpu
from jax.sharding import PartitionSpec as P

OUTER = 64
CHUNK = 256
STEP = 16


def split_pair(table):
    high = table.astype(np.float32).astype(ml_dtypes.bfloat16)
    low = (table - high.astype(np.float64)).astype(np.float32).astype(ml_dtypes.bfloat16)
    return high, low


def make_tables(blocks, width, inner):
    total = OUTER * inner
    half = OUTER // 2 + 1
    k = np.arange(half)
    a = np.arange(blocks)
    b = np.arange(inner)
    first = 2.0 * np.pi * (np.outer(k, a) % OUTER) / OUTER
    eye = np.eye(width)
    k_cos = np.kron(np.cos(first), eye)
    k_sin = np.kron(np.sin(first), eye)
    into = np.concatenate([k_cos, -k_sin], 0)
    weight = np.full((half, 1), 2.0)
    weight[0] = 1.0
    weight[-1] = 1.0
    weight = weight / total
    back_cos = np.kron((weight * np.cos(first)).T, eye)
    back_sin = np.kron((weight * np.sin(first)).T, eye)
    out_of = np.concatenate([back_cos, back_sin], 1)
    turn = 2.0 * np.pi * (np.outer(k, b) % total) / total
    turn = np.repeat(turn, width, axis=0)
    quarter = inner // 4
    c = np.arange(quarter)
    second = 2.0 * np.pi * (np.outer(c, c) % quarter) / quarter
    fourth = 2.0 * np.pi * np.outer(np.arange(4), c) / inner
    fourth = np.concatenate([np.cos(fourth), np.sin(fourth)], 0)
    c, s = np.cos(second), np.sin(second)
    across = np.concatenate([np.concatenate([c, -s], 1), np.concatenate([s, c], 1)], 0)
    return (
        split_pair(into),
        split_pair(out_of),
        np.cos(turn).astype(np.float32),
        np.sin(turn).astype(np.float32),
        split_pair(across),
        fourth.astype(np.float32),
    )


def dot(left, right):
    return jnp.dot(left, right, preferred_element_type=jnp.float32)


def turned(real, imag, cos, sin):
    return real * cos + imag * sin, imag * cos - real * sin


ZS, XS, YS = 8, 4, 4
VMEM = pl.BlockSpec(memory_space=pltpu.VMEM)
MESH = pl.DeviceIdType.MESH
BF = jnp.bfloat16


def four_way(parts):
    (re0, im0), (re1, im1), (re2, im2), (re3, im3) = parts
    sum_re, sum_im, dif_re, dif_im = re0 + re2, im0 + im2, re0 - re2, im0 - im2
    odd_re, odd_im, gap_re, gap_im = re1 + re3, im1 + im3, re1 - re3, im1 - im3
    return (
        (sum_re + odd_re, sum_im + odd_im),
        (dif_re + gap_im, dif_im - gap_re),
        (sum_re - odd_re, sum_im - odd_im),
        (dif_re - gap_im, dif_im + gap_re),
    )


def by_rows(rows, body):
    @pl.loop(0, rows // STEP, unroll=3)
    def _(i):
        body(pl.ds(pl.multiple_of(i * STEP, STEP), STEP), i * STEP)


def turn_fourth(part, fourth, r):
    if r == 0:
        return part
    return turned(*part, fourth[pl.ds(r, 1), :], fourth[pl.ds(4 + r, 1), :])


def forward(block_of, into, twist, fourth, across, y_ref, z_ref, out_ref):
    rows = z_ref.shape[1]
    quarter = z_ref.shape[2] // 2

    for c in range(y_ref.shape[1] // CHUNK):
        at = pl.ds(c * CHUNK, CHUNK)
        block = block_of(at)
        y_ref[:, at] = sum(dot(table[...], block) for table in into)

    def body(at, start):
        far = pl.ds(pl.multiple_of(rows + start, STEP), STEP)
        parts = []
        for q in range(4):
            col = pl.ds(q * quarter, quarter)
            parts.append(turned(y_ref[at, col], y_ref[far, col], twist[0][at, col], twist[1][at, col]))
        for r, part in enumerate(four_way(parts)):
            real, imag = turn_fourth(part, fourth, r)
            z_ref[r, at, :quarter] = real.astype(BF)
            z_ref[r, at, quarter:] = imag.astype(BF)

    by_rows(rows, body)
    columns(z_ref, across, out_ref)


def columns(z_ref, across, out_ref):
    for r in range(4):
        z = z_ref[r]
        out_ref[r] = sum(dot(z, table[...]) for table in across)


def combine(grad_ref, other_ref, z_ref):
    rows = z_ref.shape[1]
    quarter = z_ref.shape[2] // 2

    def body(at, _):
        for r in range(4):
            g_re, g_im = grad_ref[r, at, :quarter], grad_ref[r, at, quarter:]
            o_re, o_im = other_ref[r, at, :quarter], other_ref[r, at, quarter:]
            z_ref[r, at, :quarter] = (g_re * o_re + g_im * o_im).astype(BF)
            z_ref[r, at, quarter:] = (g_re * o_im - g_im * o_re).astype(BF)

    by_rows(rows, body)


def unfold(spec_ref, twist, fourth, u_ref):
    rows = spec_ref.shape[1]
    quarter = spec_ref.shape[2] // 2

    def body(at, start):
        far = pl.ds(pl.multiple_of(rows + start, STEP), STEP)
        parts = [
            turn_fourth((spec_ref[r, at, :quarter], spec_ref[r, at, quarter:]), fourth, r)
            for r in range(4)
        ]
        for q, part in enumerate(four_way(parts)):
            col = pl.ds(q * quarter, quarter)
            real, imag = turned(*part, twist[0][at, col], twist[1][at, col])
            u_ref[at, col] = real.astype(BF)
            u_ref[far, col] = imag.astype(BF)

    by_rows(rows, body)


def layer_kernel(
    w_hbm, g_hbm, gate_in_hbm, values_hbm, gate_out_hbm, filters_hbm, skip_ref,
    in_hi_h, in_lo_h, of_hi_h, of_lo_h, cos_h, sin_h, ac_hi_h, ac_lo_h, fourth_h,
    home_out, filters_out, mixed_out,
    gate_in, values, filters, in_hi, in_lo, of_hi, of_lo, cos, sin, ac_hi, ac_lo, fourth,
    w_ring, w_mine, w_other, g_ring, g_other, own, hold, part, inbox, relay, final,
    near_gate, back_bf, gated, gated_in, stage, crossed, pair_in,
    y_ref, z_ref, u_ref, spec_r, spec_g, spec_p, spec_f, leaving, landed, held,
    send_sems, recv_sems, local_sems,
):
    s, h = lax.axis_index("seq"), lax.axis_index("ch")
    z, x = s // XS, s % XS
    y, core = h // 2, h % 2

    def zmod(d):
        return lax.rem(z + d + ZS, ZS)

    def xmod(d):
        return lax.rem(x + d + XS, XS)

    def at_z(d):
        return (zmod(d) * XS + x, h)

    def at_x(d):
        return (z * XS + xmod(d), h)

    def at_y(d):
        return (s, lax.rem(y + d + YS, YS) * 2 + core)

    sibling = (s, y * 2 + 1 - core)
    peers = [at_z(d) for d in range(1, ZS)] + [at_x(d) for d in range(1, XS)]
    peers += [at_y(d) for d in (1, -1)] + [sibling]

    barrier = pltpu.get_barrier_semaphore()
    for peer in peers:
        pl.semaphore_signal(barrier, inc=1, device_id=peer, device_id_type=MESH)

    loads = []

    def load(src, dst):
        copy = pltpu.make_async_copy(src, dst, local_sems.at[len(loads)])
        copy.start()
        loads.append(copy)
        return copy

    w_load = load(w_hbm, w_ring.at[z])
    g_load = load(g_hbm, g_ring.at[x])
    pair_loads = [load(gate_in_hbm, gate_in), load(values_hbm, values), load(filters_hbm, filters)]
    gate_load = load(gate_out_hbm.at[x], near_gate.at[0])
    table_loads = [
        load(src, dst)
        for src, dst in (
            (in_hi_h, in_hi), (in_lo_h, in_lo), (ac_hi_h, ac_hi), (ac_lo_h, ac_lo),
            (cos_h, cos), (sin_h, sin), (fourth_h, fourth), (of_hi_h, of_hi), (of_lo_h, of_lo),
        )
    ]
    pl.semaphore_wait(barrier, len(peers))

    copies = []

    def send(src, dst, device):
        k = len(copies)
        copy = pltpu.make_async_remote_copy(
            src_ref=src, dst_ref=dst, send_sem=send_sems.at[k], recv_sem=recv_sems.at[k],
            device_id=device, device_id_type=MESH,
        )
        copy.start()
        copies.append(copy)
        return copy

    waited = [0]

    def flush(count):
        for copy in copies[waited[0] : count]:
            copy.wait_send()
        waited[0] = count

    half_w = w_ring.shape[1] // 2
    half_g = g_ring.shape[1] // 2
    first, second = pl.ds(0, half_w), pl.ds(half_w, half_w)
    top, low = pl.ds(0, half_g), pl.ds(half_g, half_g)

    halves = (first, second)
    ring = {}
    for side in (0, 1):
        for way in (1, -1):
            rows = halves[side if way == 1 else 1 - side]
            ring[way, side] = send(w_hbm.at[rows], w_ring.at[z, rows], at_z(way))
    right_top = send(g_hbm.at[top], g_ring.at[x, top], at_x(1))
    left_low = send(g_hbm.at[low], g_ring.at[x, low], at_x(-1))
    right_low = send(g_hbm.at[low], g_ring.at[x, low], at_x(1))
    left_top = send(g_hbm.at[top], g_ring.at[x, top], at_x(-1))
    shared = [send(g_hbm, g_other.at[0], sibling)]
    w_load.wait()
    for copy in pair_loads:
        copy.wait()
    for i in range(XS):
        product = gate_in[i].astype(jnp.float32) * values[i].astype(jnp.float32)
        stage[0, i] = product.astype(BF)
        stage[1, i] = filters[i].astype(BF)

    w_shared = []

    def step(r):
        for side in (0, 1):
            for way in (1, -1):
                if r == ZS // 2 and side:
                    continue
                ring[way, side].wait_recv()
                if r == ZS // 2 or (r == ZS // 2 - 1 and side):
                    continue
                block = w_ring.at[zmod(-r * way), halves[side if way == 1 else 1 - side]]
                ring[way, side] = send(block, block, at_z(way))
        even, odd = (0, 2, -2, 4)[r - 1], (1, -1, 3, -3)[r - 1]
        e = lax.rem(1 - core + z, 2)
        row = zmod(even + e * (odd - even))
        w_shared.append(send(w_ring.at[row], w_other.at[lax.rem(row // 2 - y + YS, YS)], sibling))

    step(1)
    right_top.wait_recv()
    far_top = send(g_ring.at[xmod(-1), top], g_ring.at[xmod(-1), top], at_x(1))
    left_low.wait_recv()
    far_low = send(g_ring.at[xmod(1), low], g_ring.at[xmod(1), low], at_x(-1))
    step(2)
    step(3)
    over_z = {}
    over_x = {}

    def ring_z(source, target, held):
        turns = (2, -2)
        hops = [send(source(4, n), held(n), at_z(turn)) for n, turn in enumerate(turns)]
        there = [send(source(d, None), target(z, None), at_z(d)) for d in (3, -3, 2, -2, 1, -1)]

        def forward_on():
            for n, turn in enumerate(turns):
                hops[n].wait_recv()
                there.append(send(held(n), target(zmod(-turn), n), at_z(turn)))

        return there, forward_on

    half = XS // 2

    def half_at(n):
        return pl.ds(0, XS) if n is None else pl.ds(n * half, half)

    def pair_z(i):
        there, forward_on = ring_z(
            lambda d, n: stage.at[i, half_at(n), zmod(d)],
            lambda origin, n: crossed.at[i, origin, half_at(n)],
            lambda n: held.at[i, n],
        )
        over_z[i] = there
        crossed[i, z] = stage[i, :, z]
        return forward_on

    def pair_x(i):
        for copy in over_z[i]:
            copy.wait_recv()
        over_x[i] = [
            send(crossed.at[i, :, xmod(d)], pair_in.at[i, :, x], at_x(d)) for d in range(1, XS)
        ]
        pair_in[i, :, x] = crossed[i, :, x]

    filters_on = pair_z(1)
    right_low.wait_recv()
    shared.append(send(g_ring.at[xmod(-1)], g_other.at[1], sibling))
    left_top.wait_recv()
    shared.append(send(g_ring.at[xmod(1)], g_other.at[2], sibling))
    g_load.wait()
    step(4)
    product_on = pair_z(0)

    def rows_for(d, of_core):
        return lax.rem(y + d, YS) * 2 + of_core

    for d in range(YS):
        w_mine[d] = w_ring[rows_for(d, core)]
    for copy in w_shared:
        copy.wait_recv()

    offsets = (0, -1, 1, 2)
    parts = []
    passed = []
    gates = []
    deep = w_ring.shape[1]
    wide = (YS * deep, w_ring.shape[2])

    def pass_on(n):
        for side in range(2):
            parts[n][side].wait_recv()
            relay[n, side] = (hold[n, side] + inbox[n, side, 0].astype(jnp.float32)).astype(BF)
            passed.append(send(relay.at[n, side], final.at[n, side], at_y(1 - 2 * side)))

    for n, off in enumerate(offsets):
        if n == 3:
            far_top.wait_recv()
            far_low.wait_recv()
            gates.extend(
                send(gate_out_hbm.at[xmod(d)], near_gate.at[d], at_x(d)) for d in range(1, XS)
            )
            shared.append(send(g_ring.at[xmod(2)], g_other.at[3], sibling))
        shared[n].wait_recv()

        @pl.loop(0, g_ring.shape[1] // CHUNK)
        def _(i, n=n, off=off):
            at = pl.ds(pl.multiple_of(i * CHUNK, CHUNK), CHUNK)
            form = (((1,), (1,)), ((), ()))
            total = lax.dot_general(
                w_mine[...].reshape(wide), g_ring[xmod(off), at, :], form,
                preferred_element_type=jnp.float32,
            ) + lax.dot_general(
                w_other[...].reshape(wide), g_other[n, at, :], form,
                preferred_element_type=jnp.float32,
            )
            total = total.reshape(YS, deep, CHUNK)
            own[n, :, at] = total[0]
            hold[n, 0, :, at] = total[1, :half_w]
            hold[n, 1, :, at] = total[3, half_w:]
            part[n, 0, 0, :, at] = total[2, :half_w].astype(BF)
            part[n, 0, 1, :, at] = total[1, half_w:].astype(BF)
            part[n, 1, 0, :, at] = total[2, half_w:].astype(BF)
            part[n, 1, 1, :, at] = total[3, :half_w].astype(BF)

        parts.append([send(part.at[n, side], inbox.at[n, side], at_y(1 - 2 * side)) for side in range(2)])

    arrivals = []
    gated_on = []
    homes = []

    def total_up(n):
        for copy in passed[2 * n : 2 * n + 2]:
            copy.wait_recv()
        d = -offsets[n] % XS
        if d:
            gates[d - 1].wait_recv()
        else:
            gate_load.wait()
        upper = own[n, :half_w] + final[n, 0].astype(jnp.float32) + inbox[n, 1, 1].astype(jnp.float32)
        lower = own[n, half_w:] + final[n, 1].astype(jnp.float32) + inbox[n, 0, 1].astype(jnp.float32)
        back = jnp.concatenate([upper, lower], 0)
        result = back * near_gate[d].astype(jnp.float32)
        gated[n] = result.astype(BF).reshape(gated.shape[1:])
        gated_in[z, n] = gated[n, z]
        if n == 1:

            def pick(part):
                return pl.ds(0, 2) if part is None else pl.ds(part, 1)

            there, forward_on = ring_z(
                lambda d, part: gated.at[pick(part), zmod(d)],
                lambda origin, part: gated_in.at[origin, pick(part)],
                lambda part: held.at[2, part, pl.ds(0, 1)],
            )
            arrivals.append(there)
            gated_on.append(forward_on)
        if n > 1:
            some = pl.ds(n, 1)
            arrivals.append([])
            for d in range(1, ZS):
                arrivals[-1].append(send(gated.at[some, zmod(d)], gated_in.at[z, some], at_z(d)))
        back_bf[n] = back.astype(BF)

    inner = g_ring.shape[2]
    rows = g_ring.shape[1]
    into, twist, across = (in_hi, in_lo), (cos, sin), (ac_hi, ac_lo)

    def pair_block(i):
        return lambda at: pair_in[i, :, :, :, at].reshape(rows, CHUNK)

    early = len(copies)
    filters_on()
    pass_on(0)
    pass_on(1)
    pass_on(2)
    total_up(0)
    pass_on(3)
    total_up(1)
    total_up(2)
    product_on()
    total_up(3)
    gated_on[0]()
    pair_x(1)
    pair_x(0)
    for copy in table_loads:
        copy.wait()
    for copy in over_x[1]:
        copy.wait_recv()
    forward(pair_block(1), into, twist, fourth, across, y_ref, z_ref, spec_f)
    stays = [load(back_bf.at[0], home_out.at[x])]
    flush(early)

    def gated_block(at):
        blocks = []
        for i in range(XS):
            e = lax.rem(i - x + XS, XS)
            blocks.append(gated_in[:, 2 * e - e // 2 - 4 * (e // 3), :, at])
        return jnp.stack(blocks, 1).reshape(rows, CHUNK)

    for copy in sum(arrivals, []):
        copy.wait_recv()
    forward(
        gated_block,
        into, twist, fourth, across, y_ref, z_ref, spec_g,
    )

    width = gated_in.shape[2]
    lanes = skip_ref.shape[1]
    pick = lax.broadcasted_iota(jnp.int32, (width, lanes), 1) == z * width + lax.broadcasted_iota(
        jnp.int32, (width, lanes), 0
    )
    scale = jnp.sum(jnp.where(pick, skip_ref[pl.ds(x, 1), :], 0.0), axis=1, keepdims=True)
    gone = []
    gone_on = []
    turns = []

    def turn_x(k):
        which, at = groups[k]
        result = (mixed_out, filters_out)[which]
        for copy in gone[k]:
            copy.wait_recv()
        turns.extend(
            send(landed.at[which, :, xmod(d), :, at], result.at[x, :, :, at], at_x(d))
            for d in range(1, XS)
        )
        stays.append(load(landed.at[which, :, x, :, at], result.at[x, :, :, at]))

    groups = []

    def leave(which, start, size):
        if start == 0:
            combine(spec_g, (spec_f, spec_p)[which], z_ref)
            columns(z_ref, across, spec_r)
            unfold(spec_r, twist, fourth, u_ref)
        for c in range(start, start + size, CHUNK):
            at = pl.ds(c, CHUNK)
            u = u_ref[:, at]
            out = dot(of_hi[...], u) + dot(of_lo[...], u)
            if which == 0:
                out = out.reshape(ZS * XS, width, CHUNK)
                out = out + scale * gated_block(at).reshape(out.shape).astype(jnp.float32)
            leaving[which, :, :, :, at] = out.astype(BF).reshape(ZS, XS, width, CHUNK)
        at = pl.ds(start, size)
        groups.append((which, at))
        if which and start:
            gone.append(
                [
                    send(leaving.at[which, zmod(d), :, :, at], landed.at[which, z, :, :, at], at_z(d))
                    for d in range(1, ZS)
                ]
            )
        else:
            there, forward_on = ring_z(
                lambda d, n: leaving.at[which, zmod(d), half_at(n), :, at],
                lambda origin, n: landed.at[which, origin, half_at(n), :, at],
                lambda n: held.at[3 + which, n, :, :, at],
            )
            gone.append(there)
            gone_on.append(forward_on)
        landed[which, z, :, :, at] = leaving[which, z, :, :, at]

    leave(0, 0, inner)
    for copy in over_x[0]:
        copy.wait_recv()
    forward(pair_block(0), into, twist, fourth, across, y_ref, z_ref, spec_p)
    for n, off in enumerate(offsets):
        if n:
            homes.append(send(back_bf.at[n], home_out.at[x], at_x(off)))
    gone_on[0]()
    middle = len(copies)
    leave(1, 0, CHUNK)
    leave(1, CHUNK, CHUNK)
    gone_on[1]()
    turn_x(0)
    flush(middle)
    turn_x(1)
    turn_x(2)
    for copy in stays:
        copy.wait()
    for copy in homes + turns:
        copy.wait_recv()
    flush(len(copies))
    assert len(copies) == send_sems.shape[0]
    assert len(loads) == local_sems.shape[0]


def layer(grad_out, out_weight, gate_in, gate_out, values, filters, skip_scale):
    rows, inner = gate_in.shape
    deep, wide = out_weight.shape
    width = rows // (ZS * XS)
    into, out_of, cos, sin, across, fourth = make_tables(ZS * XS, width, inner)
    tables = (*into, *out_of, cos, sin, *across, fourth)
    spec_rows = cos.shape[0]
    split = (XS, ZS, width, inner)
    count = 136

    def vmem(shape, dtype=BF):
        return pltpu.VMEM(shape, dtype)

    spec = vmem((4, spec_rows, inner // 2), jnp.float32)
    return pl.pallas_call(
        layer_kernel,
        out_shape=[
            jax.ShapeDtypeStruct((XS, deep, inner), BF),
            jax.ShapeDtypeStruct(split, BF),
            jax.ShapeDtypeStruct(split, BF),
        ],
        in_specs=[pl.BlockSpec(memory_space=pl.ANY)] * 6
        + [VMEM]
        + [pl.BlockSpec(memory_space=pl.ANY)] * len(tables),
        out_specs=[pl.BlockSpec(memory_space=pl.ANY)] * 3,
        scratch_shapes=[
            vmem(split),
            vmem(split),
            vmem(split, jnp.float32),
            *[vmem(t.shape, t.dtype) for t in tables],
            vmem((ZS, deep, wide)),
            vmem((YS, deep, wide)),
            vmem((YS, deep, wide)),
            vmem((XS,) + grad_out.shape),
            vmem((XS,) + grad_out.shape),
            vmem((XS, deep, inner), jnp.float32),
            vmem((XS, 2, deep // 2, inner), jnp.float32),
            vmem((XS, 2, 2, deep // 2, inner)),
            vmem((XS, 2, 2, deep // 2, inner)),
            vmem((XS, 2, deep // 2, inner)),
            vmem((XS, 2, deep // 2, inner)),
            vmem((XS, deep, inner)),
            vmem((XS, deep, inner)),
            vmem((XS, ZS, width, inner)),
            vmem((ZS, XS, width, inner)),
            vmem((2,) + split),
            vmem((2, ZS, XS, width, inner)),
            vmem((2, ZS, XS, width, inner)),
            vmem((2 * spec_rows, inner), jnp.float32),
            vmem((4, spec_rows, inner // 2)),
            vmem((2 * spec_rows, inner)),
            spec,
            spec,
            spec,
            spec,
            vmem((2, ZS, XS, width, inner)),
            vmem((2, ZS, XS, width, inner)),
            vmem((5, 2, XS // 2, width, inner)),
            pltpu.SemaphoreType.DMA((count,)),
            pltpu.SemaphoreType.DMA((count,)),
            pltpu.SemaphoreType.DMA((19,)),
        ],
        compiler_params=pltpu.CompilerParams(
            collective_id=0, has_side_effects=True, vmem_limit_bytes=58 * 1024 * 1024
        ),
        cost_estimate=pl.CostEstimate(flops=10 * 10**9, bytes_accessed=20 * 10**6, transcendentals=0),
    )(
        out_weight,
        grad_out,
        gate_in.reshape(split),
        values.reshape(split),
        gate_out.reshape(XS, deep, inner),
        filters.reshape(split),
        skip_scale.reshape(XS, deep),
        *tables,
    )


def shards(grad_out, out_weight, gate_in, gate_out, values, conv_out, filters, skip_scale):
    rows, inner = gate_in.shape
    home, grad_filters, mixed = layer(
        grad_out, out_weight, gate_in, gate_out, values, filters, skip_scale
    )

    def wide(block):
        return block.reshape(rows, inner).astype(jnp.float32)

    grad_gate_out = (wide(home) * wide(conv_out)).astype(BF)
    grad_gate_in = (wide(mixed) * wide(values)).astype(BF)
    grad_values = (wide(mixed) * wide(gate_in)).astype(BF)
    return (grad_gate_in, grad_values, grad_gate_out, wide(grad_filters))


def solution(mesh):
    placed = (
        P("seq", "ch"),
        P("seq", "ch"),
        P("ch", "seq"),
        P("ch", "seq"),
        P("ch", "seq"),
        P("ch", "seq"),
        P("ch", "seq"),
        P("ch"),
    )
    return jax.shard_map(
        shards,
        mesh=mesh,
        in_specs=placed,
        out_specs=(P("ch", "seq"), P("ch", "seq"), P("ch", "seq"), P("ch", "seq")),
        check_vma=False,
    )
```

```python
import jax
import jax.numpy as jnp
import ml_dtypes
import numpy as np
from jax import lax
from jax.experimental import pallas as pl
from jax.experimental.pallas import tpu as pltpu
from jax.sharding import PartitionSpec as P

OUTER = 64
CHUNK = 256
STEP = 16


def split_pair(table):
    high = table.astype(np.float32).astype(ml_dtypes.bfloat16)
    low = (table - high.astype(np.float64)).astype(np.float32).astype(ml_dtypes.bfloat16)
    return high, low


def make_tables(blocks, width, inner):
    total = OUTER * inner
    half = OUTER // 2 + 1
    k = np.arange(half)
    a = np.arange(blocks)
    b = np.arange(inner)
    first = 2.0 * np.pi * (np.outer(k, a) % OUTER) / OUTER
    eye = np.eye(width)
    k_cos = np.kron(np.cos(first), eye)
    k_sin = np.kron(np.sin(first), eye)
    into = np.concatenate([k_cos, -k_sin], 0)
    weight = np.full((half, 1), 2.0)
    weight[0] = 1.0
    weight[-1] = 1.0
    weight = weight / total
    back_cos = np.kron((weight * np.cos(first)).T, eye)
    back_sin = np.kron((weight * np.sin(first)).T, eye)
    out_of = np.concatenate([back_cos, back_sin], 1)
    turn = 2.0 * np.pi * (np.outer(k, b) % total) / total
    turn = np.repeat(turn, width, axis=0)
    quarter = inner // 4
    c = np.arange(quarter)
    second = 2.0 * np.pi * (np.outer(c, c) % quarter) / quarter
    fourth = 2.0 * np.pi * np.outer(np.arange(4), c) / inner
    fourth = np.concatenate([np.cos(fourth), np.sin(fourth)], 0)
    c, s = np.cos(second), np.sin(second)
    across = np.concatenate([np.concatenate([c, -s], 1), np.concatenate([s, c], 1)], 0)
    return (
        split_pair(into),
        split_pair(out_of),
        np.cos(turn).astype(np.float32),
        np.sin(turn).astype(np.float32),
        split_pair(across),
        fourth.astype(np.float32),
    )


def dot(left, right):
    return jnp.dot(left, right, preferred_element_type=jnp.float32)


def turned(real, imag, cos, sin):
    return real * cos + imag * sin, imag * cos - real * sin


ZS, XS, YS = 8, 4, 4
VMEM = pl.BlockSpec(memory_space=pltpu.VMEM)
MESH = pl.DeviceIdType.MESH
BF = jnp.bfloat16


def four_way(parts):
    (re0, im0), (re1, im1), (re2, im2), (re3, im3) = parts
    sum_re, sum_im, dif_re, dif_im = re0 + re2, im0 + im2, re0 - re2, im0 - im2
    odd_re, odd_im, gap_re, gap_im = re1 + re3, im1 + im3, re1 - re3, im1 - im3
    return (
        (sum_re + odd_re, sum_im + odd_im),
        (dif_re + gap_im, dif_im - gap_re),
        (sum_re - odd_re, sum_im - odd_im),
        (dif_re - gap_im, dif_im + gap_re),
    )


def by_rows(rows, body):
    @pl.loop(0, rows // STEP, unroll=3)
    def _(i):
        body(pl.ds(pl.multiple_of(i * STEP, STEP), STEP), i * STEP)


def turn_fourth(part, fourth, r):
    if r == 0:
        return part
    return turned(*part, fourth[pl.ds(r, 1), :], fourth[pl.ds(4 + r, 1), :])


def forward(block_of, into, twist, fourth, across, y_ref, z_ref, out_ref):
    rows = z_ref.shape[1]
    quarter = z_ref.shape[2] // 2

    for c in range(y_ref.shape[1] // CHUNK):
        at = pl.ds(c * CHUNK, CHUNK)
        block = block_of(at)
        y_ref[:, at] = sum(dot(table[...], block) for table in into)

    def body(at, start):
        far = pl.ds(pl.multiple_of(rows + start, STEP), STEP)
        parts = []
        for q in range(4):
            col = pl.ds(q * quarter, quarter)
            parts.append(turned(y_ref[at, col], y_ref[far, col], twist[0][at, col], twist[1][at, col]))
        for r, part in enumerate(four_way(parts)):
            real, imag = turn_fourth(part, fourth, r)
            z_ref[r, at, :quarter] = real.astype(BF)
            z_ref[r, at, quarter:] = imag.astype(BF)

    by_rows(rows, body)
    columns(z_ref, across, out_ref)


def columns(z_ref, across, out_ref):
    for r in range(4):
        z = z_ref[r]
        out_ref[r] = sum(dot(z, table[...]) for table in across)


def combine(grad_ref, other_ref, z_ref):
    rows = z_ref.shape[1]
    quarter = z_ref.shape[2] // 2

    def body(at, _):
        for r in range(4):
            g_re, g_im = grad_ref[r, at, :quarter], grad_ref[r, at, quarter:]
            o_re, o_im = other_ref[r, at, :quarter], other_ref[r, at, quarter:]
            z_ref[r, at, :quarter] = (g_re * o_re + g_im * o_im).astype(BF)
            z_ref[r, at, quarter:] = (g_re * o_im - g_im * o_re).astype(BF)

    by_rows(rows, body)


def unfold(spec_ref, twist, fourth, u_ref):
    rows = spec_ref.shape[1]
    quarter = spec_ref.shape[2] // 2

    def body(at, start):
        far = pl.ds(pl.multiple_of(rows + start, STEP), STEP)
        parts = [
            turn_fourth((spec_ref[r, at, :quarter], spec_ref[r, at, quarter:]), fourth, r)
            for r in range(4)
        ]
        for q, part in enumerate(four_way(parts)):
            col = pl.ds(q * quarter, quarter)
            real, imag = turned(*part, twist[0][at, col], twist[1][at, col])
            u_ref[at, col] = real.astype(BF)
            u_ref[far, col] = imag.astype(BF)

    by_rows(rows, body)


def layer_kernel(
    w_hbm, g_hbm, gate_in_hbm, values_hbm, gate_out_hbm, filters_hbm, skip_ref,
    in_hi_h, in_lo_h, of_hi_h, of_lo_h, cos_h, sin_h, ac_hi_h, ac_lo_h, fourth_h,
    home_out, filters_out, mixed_out,
    gate_in, values, filters, in_hi, in_lo, of_hi, of_lo, cos, sin, ac_hi, ac_lo, fourth,
    w_ring, w_mine, w_other, g_ring, g_other, own, hold, part, inbox, relay, final,
    near_gate, back_bf, gated, gated_in, stage, crossed, pair_in,
    y_ref, z_ref, u_ref, spec_r, spec_g, spec_p, spec_f, leaving, landed,
    send_sems, recv_sems, local_sems,
):
    s, h = lax.axis_index("seq"), lax.axis_index("ch")
    z, x = s // XS, s % XS
    y, core = h // 2, h % 2

    def zmod(d):
        return lax.rem(z + d + ZS, ZS)

    def xmod(d):
        return lax.rem(x + d + XS, XS)

    def at_z(d):
        return (zmod(d) * XS + x, h)

    def at_x(d):
        return (z * XS + xmod(d), h)

    def at_y(d):
        return (s, lax.rem(y + d + YS, YS) * 2 + core)

    sibling = (s, y * 2 + 1 - core)
    peers = [at_z(d) for d in range(1, ZS)] + [at_x(d) for d in range(1, XS)]
    peers += [at_y(d) for d in (1, -1)] + [sibling]

    barrier = pltpu.get_barrier_semaphore()
    for peer in peers:
        pl.semaphore_signal(barrier, inc=1, device_id=peer, device_id_type=MESH)

    loads = []

    def load(src, dst):
        copy = pltpu.make_async_copy(src, dst, local_sems.at[len(loads)])
        copy.start()
        loads.append(copy)
        return copy

    w_load = load(w_hbm, w_ring.at[z])
    g_load = load(g_hbm, g_ring.at[x])
    pair_loads = [load(gate_in_hbm, gate_in), load(values_hbm, values), load(filters_hbm, filters)]
    gate_load = load(gate_out_hbm.at[x], near_gate.at[0])
    table_loads = [
        load(src, dst)
        for src, dst in (
            (in_hi_h, in_hi), (in_lo_h, in_lo), (ac_hi_h, ac_hi), (ac_lo_h, ac_lo),
            (cos_h, cos), (sin_h, sin), (fourth_h, fourth), (of_hi_h, of_hi), (of_lo_h, of_lo),
        )
    ]
    pl.semaphore_wait(barrier, len(peers))

    copies = []

    def send(src, dst, device):
        k = len(copies)
        copy = pltpu.make_async_remote_copy(
            src_ref=src, dst_ref=dst, send_sem=send_sems.at[k], recv_sem=recv_sems.at[k],
            device_id=device, device_id_type=MESH,
        )
        copy.start()
        copies.append(copy)
        return copy

    waited = [0]

    def flush(count):
        for copy in copies[waited[0] : count]:
            copy.wait_send()
        waited[0] = count

    half_w = w_ring.shape[1] // 2
    half_g = g_ring.shape[1] // 2
    first, second = pl.ds(0, half_w), pl.ds(half_w, half_w)
    top, low = pl.ds(0, half_g), pl.ds(half_g, half_g)

    halves = (first, second)
    ring = {}
    for side in (0, 1):
        for way in (1, -1):
            rows = halves[side if way == 1 else 1 - side]
            ring[way, side] = send(w_hbm.at[rows], w_ring.at[z, rows], at_z(way))
    right_top = send(g_hbm.at[top], g_ring.at[x, top], at_x(1))
    left_low = send(g_hbm.at[low], g_ring.at[x, low], at_x(-1))
    right_low = send(g_hbm.at[low], g_ring.at[x, low], at_x(1))
    left_top = send(g_hbm.at[top], g_ring.at[x, top], at_x(-1))
    shared = [send(g_hbm, g_other.at[0], sibling)]
    w_load.wait()
    for copy in pair_loads:
        copy.wait()
    for i in range(XS):
        product = gate_in[i].astype(jnp.float32) * values[i].astype(jnp.float32)
        stage[0, i] = product.astype(BF)
        stage[1, i] = filters[i].astype(BF)

    w_shared = []

    def step(r):
        for side in (0, 1):
            for way in (1, -1):
                if r == ZS // 2 and side:
                    continue
                ring[way, side].wait_recv()
                if r == ZS // 2 or (r == ZS // 2 - 1 and side):
                    continue
                block = w_ring.at[zmod(-r * way), halves[side if way == 1 else 1 - side]]
                ring[way, side] = send(block, block, at_z(way))
        even, odd = (0, 2, -2, 4)[r - 1], (1, -1, 3, -3)[r - 1]
        e = lax.rem(1 - core + z, 2)
        row = zmod(even + e * (odd - even))
        w_shared.append(send(w_ring.at[row], w_other.at[lax.rem(row // 2 - y + YS, YS)], sibling))

    step(1)
    right_top.wait_recv()
    far_top = send(g_ring.at[xmod(-1), top], g_ring.at[xmod(-1), top], at_x(1))
    left_low.wait_recv()
    far_low = send(g_ring.at[xmod(1), low], g_ring.at[xmod(1), low], at_x(-1))
    step(2)
    step(3)
    over_z = {}
    over_x = {}

    def pair_z(i, start, size):
        at = pl.ds(start, size)
        over_z.setdefault(i, []).extend(
            send(stage.at[i, at, zmod(d)], crossed.at[i, z, at], at_z(d)) for d in range(1, ZS)
        )
        crossed[i, z, at] = stage[i, at, z]

    def pair_x(i):
        for copy in over_z[i]:
            copy.wait_recv()
        over_x[i] = [
            send(crossed.at[i, :, xmod(d)], pair_in.at[i, :, x], at_x(d)) for d in range(1, XS)
        ]
        pair_in[i, :, x] = crossed[i, :, x]

    pair_z(1, 0, XS)
    right_low.wait_recv()
    shared.append(send(g_ring.at[xmod(-1)], g_other.at[1], sibling))
    left_top.wait_recv()
    shared.append(send(g_ring.at[xmod(1)], g_other.at[2], sibling))
    g_load.wait()
    step(4)
    pair_z(0, 0, XS)

    def rows_for(d, of_core):
        return lax.rem(y + d, YS) * 2 + of_core

    for d in range(YS):
        w_mine[d] = w_ring[rows_for(d, core)]
    for copy in w_shared:
        copy.wait_recv()

    offsets = (0, -1, 1, 2)
    parts = []
    passed = []
    gates = []
    deep = w_ring.shape[1]
    wide = (YS * deep, w_ring.shape[2])

    def pass_on(n):
        for side in range(2):
            parts[n][side].wait_recv()
            relay[n, side] = (hold[n, side] + inbox[n, side, 0].astype(jnp.float32)).astype(BF)
            passed.append(send(relay.at[n, side], final.at[n, side], at_y(1 - 2 * side)))

    for n, off in enumerate(offsets):
        if n == 3:
            far_top.wait_recv()
            far_low.wait_recv()
            gates.extend(
                send(gate_out_hbm.at[xmod(d)], near_gate.at[d], at_x(d)) for d in range(1, XS)
            )
            shared.append(send(g_ring.at[xmod(2)], g_other.at[3], sibling))
        shared[n].wait_recv()

        @pl.loop(0, g_ring.shape[1] // CHUNK)
        def _(i, n=n, off=off):
            at = pl.ds(pl.multiple_of(i * CHUNK, CHUNK), CHUNK)
            form = (((1,), (1,)), ((), ()))
            total = lax.dot_general(
                w_mine[...].reshape(wide), g_ring[xmod(off), at, :], form,
                preferred_element_type=jnp.float32,
            ) + lax.dot_general(
                w_other[...].reshape(wide), g_other[n, at, :], form,
                preferred_element_type=jnp.float32,
            )
            total = total.reshape(YS, deep, CHUNK)
            own[n, :, at] = total[0]
            hold[n, 0, :, at] = total[1, :half_w]
            hold[n, 1, :, at] = total[3, half_w:]
            part[n, 0, 0, :, at] = total[2, :half_w].astype(BF)
            part[n, 0, 1, :, at] = total[1, half_w:].astype(BF)
            part[n, 1, 0, :, at] = total[2, half_w:].astype(BF)
            part[n, 1, 1, :, at] = total[3, :half_w].astype(BF)

        parts.append([send(part.at[n, side], inbox.at[n, side], at_y(1 - 2 * side)) for side in range(2)])

    arrivals = []
    homes = []

    def total_up(n):
        for copy in passed[2 * n : 2 * n + 2]:
            copy.wait_recv()
        d = -offsets[n] % XS
        if d:
            gates[d - 1].wait_recv()
        else:
            gate_load.wait()
        upper = own[n, :half_w] + final[n, 0].astype(jnp.float32) + inbox[n, 1, 1].astype(jnp.float32)
        lower = own[n, half_w:] + final[n, 1].astype(jnp.float32) + inbox[n, 0, 1].astype(jnp.float32)
        back = jnp.concatenate([upper, lower], 0)
        result = back * near_gate[d].astype(jnp.float32)
        gated[n] = result.astype(BF).reshape(gated.shape[1:])
        gated_in[z, n] = gated[n, z]
        if n:
            some = pl.ds(0, 2) if n == 1 else pl.ds(n, 1)
            for d in range(1, ZS):
                arrivals.append(send(gated.at[some, zmod(d)], gated_in.at[z, some], at_z(d)))
        back_bf[n] = back.astype(BF)

    inner = g_ring.shape[2]
    rows = g_ring.shape[1]
    into, twist, across = (in_hi, in_lo), (cos, sin), (ac_hi, ac_lo)

    def pair_block(i):
        return lambda at: pair_in[i, :, :, :, at].reshape(rows, CHUNK)

    early = len(copies)
    pass_on(0)
    pass_on(1)
    pass_on(2)
    total_up(0)
    pass_on(3)
    total_up(1)
    total_up(2)
    pair_x(1)
    total_up(3)
    pair_x(0)
    for copy in table_loads:
        copy.wait()
    for copy in over_x[1]:
        copy.wait_recv()
    forward(pair_block(1), into, twist, fourth, across, y_ref, z_ref, spec_f)
    stays = [load(back_bf.at[0], home_out.at[x])]
    flush(early)

    def gated_block(at):
        blocks = []
        for i in range(XS):
            e = lax.rem(i - x + XS, XS)
            blocks.append(gated_in[:, 2 * e - e // 2 - 4 * (e // 3), :, at])
        return jnp.stack(blocks, 1).reshape(rows, CHUNK)

    for copy in arrivals:
        copy.wait_recv()
    forward(
        gated_block,
        into, twist, fourth, across, y_ref, z_ref, spec_g,
    )

    width = gated_in.shape[2]
    lanes = skip_ref.shape[1]
    pick = lax.broadcasted_iota(jnp.int32, (width, lanes), 1) == z * width + lax.broadcasted_iota(
        jnp.int32, (width, lanes), 0
    )
    scale = jnp.sum(jnp.where(pick, skip_ref[pl.ds(x, 1), :], 0.0), axis=1, keepdims=True)
    gone = []
    turns = []

    def mixed_over_x():
        for copy in gone[0]:
            copy.wait_recv()
        turns.extend(
            send(landed.at[0, :, xmod(d)], mixed_out.at[x], at_x(d)) for d in range(1, XS)
        )
        stays.append(load(landed.at[0, :, x], mixed_out.at[x]))

    def filters_over_z(k):
        at = pl.ds((k - 1) * CHUNK, CHUNK)
        for copy in gone[k]:
            copy.wait_recv()
        turns.extend(
            send(landed.at[1, zmod(d), :, :, at], filters_out.at[:, z, :, at], at_z(d))
            for d in range(1, ZS)
        )
        stays.append(load(landed.at[1, z, :, :, at], filters_out.at[:, z, :, at]))

    def leave(which, start, size):
        if start == 0:
            combine(spec_g, (spec_f, spec_p)[which], z_ref)
            columns(z_ref, across, spec_r)
            unfold(spec_r, twist, fourth, u_ref)
        for c in range(start, start + size, CHUNK):
            at = pl.ds(c, CHUNK)
            u = u_ref[:, at]
            out = dot(of_hi[...], u) + dot(of_lo[...], u)
            if which == 0:
                out = out.reshape(ZS * XS, width, CHUNK)
                out = out + scale * gated_block(at).reshape(out.shape).astype(jnp.float32)
            leaving[which, :, :, :, at] = out.astype(BF).reshape(ZS, XS, width, CHUNK)
        at = pl.ds(start, size)
        if which == 0:
            gone.append(
                [send(leaving.at[0, zmod(d)], landed.at[0, z], at_z(d)) for d in range(1, ZS)]
            )
            landed[0, z] = leaving[0, z]
        else:
            gone.append(
                [
                    send(leaving.at[1, :, xmod(d), :, at], landed.at[1, :, x, :, at], at_x(d))
                    for d in range(1, XS)
                ]
            )
            landed[1, :, x, :, at] = leaving[1, :, x, :, at]

    leave(0, 0, inner)
    for copy in over_x[0]:
        copy.wait_recv()
    forward(pair_block(0), into, twist, fourth, across, y_ref, z_ref, spec_p)
    middle = len(copies)
    leave(1, 0, CHUNK)
    leave(1, CHUNK, CHUNK)
    filters_over_z(1)
    filters_over_z(2)
    for n, off in enumerate(offsets):
        if n:
            homes.append(send(back_bf.at[n], home_out.at[x], at_x(off)))
    mixed_over_x()
    flush(middle)
    for copy in stays:
        copy.wait()
    for copy in homes + turns:
        copy.wait_recv()
    flush(len(copies))
    assert len(copies) == send_sems.shape[0]
    assert len(loads) == local_sems.shape[0]


def layer(grad_out, out_weight, gate_in, gate_out, values, filters, skip_scale):
    rows, inner = gate_in.shape
    deep, wide = out_weight.shape
    width = rows // (ZS * XS)
    into, out_of, cos, sin, across, fourth = make_tables(ZS * XS, width, inner)
    tables = (*into, *out_of, cos, sin, *across, fourth)
    spec_rows = cos.shape[0]
    split = (XS, ZS, width, inner)
    count = 121

    def vmem(shape, dtype=BF):
        return pltpu.VMEM(shape, dtype)

    spec = vmem((4, spec_rows, inner // 2), jnp.float32)
    return pl.pallas_call(
        layer_kernel,
        out_shape=[
            jax.ShapeDtypeStruct((XS, deep, inner), BF),
            jax.ShapeDtypeStruct(split, BF),
            jax.ShapeDtypeStruct(split, BF),
        ],
        in_specs=[pl.BlockSpec(memory_space=pl.ANY)] * 6
        + [VMEM]
        + [pl.BlockSpec(memory_space=pl.ANY)] * len(tables),
        out_specs=[pl.BlockSpec(memory_space=pl.ANY)] * 3,
        scratch_shapes=[
            vmem(split),
            vmem(split),
            vmem(split, jnp.float32),
            *[vmem(t.shape, t.dtype) for t in tables],
            vmem((ZS, deep, wide)),
            vmem((YS, deep, wide)),
            vmem((YS, deep, wide)),
            vmem((XS,) + grad_out.shape),
            vmem((XS,) + grad_out.shape),
            vmem((XS, deep, inner), jnp.float32),
            vmem((XS, 2, deep // 2, inner), jnp.float32),
            vmem((XS, 2, 2, deep // 2, inner)),
            vmem((XS, 2, 2, deep // 2, inner)),
            vmem((XS, 2, deep // 2, inner)),
            vmem((XS, 2, deep // 2, inner)),
            vmem((XS, deep, inner)),
            vmem((XS, deep, inner)),
            vmem((XS, ZS, width, inner)),
            vmem((ZS, XS, width, inner)),
            vmem((2,) + split),
            vmem((2, ZS, XS, width, inner)),
            vmem((2, ZS, XS, width, inner)),
            vmem((2 * spec_rows, inner), jnp.float32),
            vmem((4, spec_rows, inner // 2)),
            vmem((2 * spec_rows, inner)),
            spec,
            spec,
            spec,
            spec,
            vmem((2, ZS, XS, width, inner)),
            vmem((2, ZS, XS, width, inner)),
            pltpu.SemaphoreType.DMA((count,)),
            pltpu.SemaphoreType.DMA((count,)),
            pltpu.SemaphoreType.DMA((19,)),
        ],
        compiler_params=pltpu.CompilerParams(
            collective_id=0, has_side_effects=True, vmem_limit_bytes=58 * 1024 * 1024
        ),
        cost_estimate=pl.CostEstimate(flops=10 * 10**9, bytes_accessed=20 * 10**6, transcendentals=0),
    )(
        out_weight,
        grad_out,
        gate_in.reshape(split),
        values.reshape(split),
        gate_out.reshape(XS, deep, inner),
        filters.reshape(split),
        skip_scale.reshape(XS, deep),
        *tables,
    )


def shards(grad_out, out_weight, gate_in, gate_out, values, conv_out, filters, skip_scale):
    rows, inner = gate_in.shape
    home, grad_filters, mixed = layer(
        grad_out, out_weight, gate_in, gate_out, values, filters, skip_scale
    )

    def wide(block):
        return block.reshape(rows, inner).astype(jnp.float32)

    grad_gate_out = (wide(home) * wide(conv_out)).astype(BF)
    grad_gate_in = (wide(mixed) * wide(values)).astype(BF)
    grad_values = (wide(mixed) * wide(gate_in)).astype(BF)
    return (grad_gate_in, grad_values, grad_gate_out, wide(grad_filters))


def solution(mesh):
    placed = (
        P("seq", "ch"),
        P("seq", "ch"),
        P("ch", "seq"),
        P("ch", "seq"),
        P("ch", "seq"),
        P("ch", "seq"),
        P("ch", "seq"),
        P("ch"),
    )
    return jax.shard_map(
        shards,
        mesh=mesh,
        in_specs=placed,
        out_specs=(P("ch", "seq"), P("ch", "seq"), P("ch", "seq"), P("ch", "seq")),
        check_vma=False,
    )
```

```python
import jax
import jax.numpy as jnp
import ml_dtypes
import numpy as np
from jax import lax
from jax.experimental import pallas as pl
from jax.experimental.pallas import tpu as pltpu
from jax.sharding import PartitionSpec as P

OUTER = 64
CHUNK = 256
STEP = 16


def split_pair(table):
    high = table.astype(np.float32).astype(ml_dtypes.bfloat16)
    low = (table - high.astype(np.float64)).astype(np.float32).astype(ml_dtypes.bfloat16)
    return high, low


def make_tables(blocks, width, inner):
    total = OUTER * inner
    half = OUTER // 2 + 1
    k = np.arange(half)
    a = np.arange(blocks)
    b = np.arange(inner)
    first = 2.0 * np.pi * (np.outer(k, a) % OUTER) / OUTER
    eye = np.eye(width)
    k_cos = np.kron(np.cos(first), eye)
    k_sin = np.kron(np.sin(first), eye)
    into = np.concatenate([k_cos, -k_sin], 0)
    weight = np.full((half, 1), 2.0)
    weight[0] = 1.0
    weight[-1] = 1.0
    weight = weight / total
    back_cos = np.kron((weight * np.cos(first)).T, eye)
    back_sin = np.kron((weight * np.sin(first)).T, eye)
    out_of = np.concatenate([back_cos, back_sin], 1)
    turn = 2.0 * np.pi * (np.outer(k, b) % total) / total
    turn = np.repeat(turn, width, axis=0)
    quarter = inner // 4
    c = np.arange(quarter)
    second = 2.0 * np.pi * (np.outer(c, c) % quarter) / quarter
    fourth = 2.0 * np.pi * np.outer(np.arange(4), c) / inner
    fourth = np.concatenate([np.cos(fourth), np.sin(fourth)], 0)
    c, s = np.cos(second), np.sin(second)
    across = np.concatenate([np.concatenate([c, -s], 1), np.concatenate([s, c], 1)], 0)
    return (
        split_pair(into),
        split_pair(out_of),
        np.cos(turn).astype(np.float32),
        np.sin(turn).astype(np.float32),
        split_pair(across),
        fourth.astype(np.float32),
    )


def dot(left, right):
    return jnp.dot(left, right, preferred_element_type=jnp.float32)


def turned(real, imag, cos, sin):
    return real * cos + imag * sin, imag * cos - real * sin


ZS, XS, YS = 8, 4, 4
VMEM = pl.BlockSpec(memory_space=pltpu.VMEM)
MESH = pl.DeviceIdType.MESH
BF = jnp.bfloat16


def four_way(parts):
    (re0, im0), (re1, im1), (re2, im2), (re3, im3) = parts
    sum_re, sum_im, dif_re, dif_im = re0 + re2, im0 + im2, re0 - re2, im0 - im2
    odd_re, odd_im, gap_re, gap_im = re1 + re3, im1 + im3, re1 - re3, im1 - im3
    return (
        (sum_re + odd_re, sum_im + odd_im),
        (dif_re + gap_im, dif_im - gap_re),
        (sum_re - odd_re, sum_im - odd_im),
        (dif_re - gap_im, dif_im + gap_re),
    )


def by_rows(rows, body):
    @pl.loop(0, rows // STEP, unroll=3)
    def _(i):
        body(pl.ds(pl.multiple_of(i * STEP, STEP), STEP), i * STEP)


def turn_fourth(part, fourth, r):
    if r == 0:
        return part
    return turned(*part, fourth[pl.ds(r, 1), :], fourth[pl.ds(4 + r, 1), :])


def forward(block_of, into, twist, fourth, across, y_ref, z_ref, out_ref):
    rows = z_ref.shape[1]
    quarter = z_ref.shape[2] // 2

    for c in range(y_ref.shape[1] // CHUNK):
        at = pl.ds(c * CHUNK, CHUNK)
        block = block_of(at)
        y_ref[:, at] = sum(dot(table[...], block) for table in into)

    def body(at, start):
        far = pl.ds(pl.multiple_of(rows + start, STEP), STEP)
        parts = []
        for q in range(4):
            col = pl.ds(q * quarter, quarter)
            parts.append(turned(y_ref[at, col], y_ref[far, col], twist[0][at, col], twist[1][at, col]))
        for r, part in enumerate(four_way(parts)):
            real, imag = turn_fourth(part, fourth, r)
            z_ref[r, at, :quarter] = real.astype(BF)
            z_ref[r, at, quarter:] = imag.astype(BF)

    by_rows(rows, body)
    columns(z_ref, across, out_ref)


def columns(z_ref, across, out_ref):
    for r in range(4):
        z = z_ref[r]
        out_ref[r] = sum(dot(z, table[...]) for table in across)


def combine(grad_ref, other_ref, z_ref):
    rows = z_ref.shape[1]
    quarter = z_ref.shape[2] // 2

    def body(at, _):
        for r in range(4):
            g_re, g_im = grad_ref[r, at, :quarter], grad_ref[r, at, quarter:]
            o_re, o_im = other_ref[r, at, :quarter], other_ref[r, at, quarter:]
            z_ref[r, at, :quarter] = (g_re * o_re + g_im * o_im).astype(BF)
            z_ref[r, at, quarter:] = (g_re * o_im - g_im * o_re).astype(BF)

    by_rows(rows, body)


def unfold(spec_ref, twist, fourth, u_ref):
    rows = spec_ref.shape[1]
    quarter = spec_ref.shape[2] // 2

    def body(at, start):
        far = pl.ds(pl.multiple_of(rows + start, STEP), STEP)
        parts = [
            turn_fourth((spec_ref[r, at, :quarter], spec_ref[r, at, quarter:]), fourth, r)
            for r in range(4)
        ]
        for q, part in enumerate(four_way(parts)):
            col = pl.ds(q * quarter, quarter)
            real, imag = turned(*part, twist[0][at, col], twist[1][at, col])
            u_ref[at, col] = real.astype(BF)
            u_ref[far, col] = imag.astype(BF)

    by_rows(rows, body)


def layer_kernel(
    w_hbm, g_hbm, gate_in_hbm, values_hbm, gate_out_hbm, filters_hbm, skip_ref,
    in_hi_h, in_lo_h, of_hi_h, of_lo_h, cos_h, sin_h, ac_hi_h, ac_lo_h, fourth_h,
    home_out, filters_out, mixed_out,
    gate_in, values, filters, in_hi, in_lo, of_hi, of_lo, cos, sin, ac_hi, ac_lo, fourth,
    w_ring, w_mine, w_other, g_ring, g_other, own, hold, part, inbox, relay, final,
    near_gate, back_bf, gated, gated_in, stage, crossed, pair_in,
    y_ref, z_ref, u_ref, spec_r, spec_g, spec_p, spec_f, leaving, landed,
    send_sems, recv_sems, local_sems,
):
    s, h = lax.axis_index("seq"), lax.axis_index("ch")
    z, x = s // XS, s % XS
    y, core = h // 2, h % 2

    def zmod(d):
        return lax.rem(z + d + ZS, ZS)

    def xmod(d):
        return lax.rem(x + d + XS, XS)

    def at_z(d):
        return (zmod(d) * XS + x, h)

    def at_x(d):
        return (z * XS + xmod(d), h)

    def at_y(d):
        return (s, lax.rem(y + d + YS, YS) * 2 + core)

    sibling = (s, y * 2 + 1 - core)
    peers = [at_z(d) for d in range(1, ZS)] + [at_x(d) for d in range(1, XS)]
    peers += [at_y(d) for d in (1, -1)] + [sibling]

    barrier = pltpu.get_barrier_semaphore()
    for peer in peers:
        pl.semaphore_signal(barrier, inc=1, device_id=peer, device_id_type=MESH)

    loads = []

    def load(src, dst):
        copy = pltpu.make_async_copy(src, dst, local_sems.at[len(loads)])
        copy.start()
        loads.append(copy)
        return copy

    w_load = load(w_hbm, w_ring.at[z])
    g_load = load(g_hbm, g_ring.at[x])
    pair_loads = [load(gate_in_hbm, gate_in), load(values_hbm, values), load(filters_hbm, filters)]
    gate_load = load(gate_out_hbm.at[x], near_gate.at[0])
    table_loads = [
        load(src, dst)
        for src, dst in (
            (in_hi_h, in_hi), (in_lo_h, in_lo), (ac_hi_h, ac_hi), (ac_lo_h, ac_lo),
            (cos_h, cos), (sin_h, sin), (fourth_h, fourth), (of_hi_h, of_hi), (of_lo_h, of_lo),
        )
    ]
    pl.semaphore_wait(barrier, len(peers))

    copies = []

    def send(src, dst, device):
        k = len(copies)
        copy = pltpu.make_async_remote_copy(
            src_ref=src, dst_ref=dst, send_sem=send_sems.at[k], recv_sem=recv_sems.at[k],
            device_id=device, device_id_type=MESH,
        )
        copy.start()
        copies.append(copy)
        return copy

    waited = [0]

    def flush(count):
        for copy in copies[waited[0] : count]:
            copy.wait_send()
        waited[0] = count

    half_w = w_ring.shape[1] // 2
    half_g = g_ring.shape[1] // 2
    first, second = pl.ds(0, half_w), pl.ds(half_w, half_w)
    top, low = pl.ds(0, half_g), pl.ds(half_g, half_g)

    halves = (first, second)
    ring = {}
    for side in (0, 1):
        for way in (1, -1):
            rows = halves[side if way == 1 else 1 - side]
            ring[way, side] = send(w_hbm.at[rows], w_ring.at[z, rows], at_z(way))
    right_top = send(g_hbm.at[top], g_ring.at[x, top], at_x(1))
    left_low = send(g_hbm.at[low], g_ring.at[x, low], at_x(-1))
    right_low = send(g_hbm.at[low], g_ring.at[x, low], at_x(1))
    left_top = send(g_hbm.at[top], g_ring.at[x, top], at_x(-1))
    shared = [send(g_hbm, g_other.at[0], sibling)]
    w_load.wait()
    for copy in pair_loads:
        copy.wait()
    for i in range(XS):
        product = gate_in[i].astype(jnp.float32) * values[i].astype(jnp.float32)
        stage[0, i] = product.astype(BF)
        stage[1, i] = filters[i].astype(BF)

    w_shared = []

    def step(r):
        for side in (0, 1):
            for way in (1, -1):
                if r == ZS // 2 and side:
                    continue
                ring[way, side].wait_recv()
                if r == ZS // 2 or (r == ZS // 2 - 1 and side):
                    continue
                block = w_ring.at[zmod(-r * way), halves[side if way == 1 else 1 - side]]
                ring[way, side] = send(block, block, at_z(way))
        even, odd = (0, 2, -2, 4)[r - 1], (1, -1, 3, -3)[r - 1]
        e = lax.rem(1 - core + z, 2)
        row = zmod(even + e * (odd - even))
        w_shared.append(send(w_ring.at[row], w_other.at[lax.rem(row // 2 - y + YS, YS)], sibling))

    step(1)
    right_top.wait_recv()
    far_top = send(g_ring.at[xmod(-1), top], g_ring.at[xmod(-1), top], at_x(1))
    left_low.wait_recv()
    far_low = send(g_ring.at[xmod(1), low], g_ring.at[xmod(1), low], at_x(-1))
    step(2)
    step(3)
    product_x = [
        send(stage.at[0, xmod(d)], crossed.at[0, :, x], at_x(d)) for d in range(1, XS)
    ]
    crossed[0, :, x] = stage[0, x]
    product_z = []

    def product_over_z(start, size):
        at = pl.ds(start, size)
        product_z.extend(
            send(crossed.at[0, zmod(d), at], pair_in.at[0, z, at], at_z(d)) for d in range(1, ZS)
        )
        pair_in[0, z, at] = crossed[0, z, at]

    filters_z = [
        send(stage.at[1, :, zmod(d)], crossed.at[1, z], at_z(d)) for d in range(1, ZS)
    ]
    crossed[1, z] = stage[1, :, z]
    filters_x = []

    def filters_over_x():
        for copy in filters_z:
            copy.wait_recv()
        filters_x.extend(
            send(crossed.at[1, :, xmod(d)], pair_in.at[1, :, x], at_x(d)) for d in range(1, XS)
        )
        pair_in[1, :, x] = crossed[1, :, x]

    right_low.wait_recv()
    shared.append(send(g_ring.at[xmod(-1)], g_other.at[1], sibling))
    left_top.wait_recv()
    shared.append(send(g_ring.at[xmod(1)], g_other.at[2], sibling))
    g_load.wait()
    step(4)

    def rows_for(d, of_core):
        return lax.rem(y + d, YS) * 2 + of_core

    for d in range(YS):
        w_mine[d] = w_ring[rows_for(d, core)]
    for copy in w_shared:
        copy.wait_recv()

    offsets = (0, -1, 1, 2)
    parts = []
    passed = []
    gates = []
    deep = w_ring.shape[1]
    wide = (YS * deep, w_ring.shape[2])

    def pass_on(n):
        for side in range(2):
            parts[n][side].wait_recv()
            relay[n, side] = (hold[n, side] + inbox[n, side, 0].astype(jnp.float32)).astype(BF)
            passed.append(send(relay.at[n, side], final.at[n, side], at_y(1 - 2 * side)))

    for n, off in enumerate(offsets):
        if n == 3:
            far_top.wait_recv()
            far_low.wait_recv()
            gates.extend(
                send(gate_out_hbm.at[xmod(d)], near_gate.at[d], at_x(d)) for d in range(1, XS)
            )
            shared.append(send(g_ring.at[xmod(2)], g_other.at[3], sibling))
        shared[n].wait_recv()

        @pl.loop(0, g_ring.shape[1] // CHUNK)
        def _(i, n=n, off=off):
            at = pl.ds(pl.multiple_of(i * CHUNK, CHUNK), CHUNK)
            form = (((1,), (1,)), ((), ()))
            total = lax.dot_general(
                w_mine[...].reshape(wide), g_ring[xmod(off), at, :], form,
                preferred_element_type=jnp.float32,
            ) + lax.dot_general(
                w_other[...].reshape(wide), g_other[n, at, :], form,
                preferred_element_type=jnp.float32,
            )
            total = total.reshape(YS, deep, CHUNK)
            own[n, :, at] = total[0]
            hold[n, 0, :, at] = total[1, :half_w]
            hold[n, 1, :, at] = total[3, half_w:]
            part[n, 0, 0, :, at] = total[2, :half_w].astype(BF)
            part[n, 0, 1, :, at] = total[1, half_w:].astype(BF)
            part[n, 1, 0, :, at] = total[2, half_w:].astype(BF)
            part[n, 1, 1, :, at] = total[3, :half_w].astype(BF)

        parts.append([send(part.at[n, side], inbox.at[n, side], at_y(1 - 2 * side)) for side in range(2)])

    arrivals = []
    homes = []

    def total_up(n):
        for copy in passed[2 * n : 2 * n + 2]:
            copy.wait_recv()
        d = -offsets[n] % XS
        if d:
            gates[d - 1].wait_recv()
        else:
            gate_load.wait()
        upper = own[n, :half_w] + final[n, 0].astype(jnp.float32) + inbox[n, 1, 1].astype(jnp.float32)
        lower = own[n, half_w:] + final[n, 1].astype(jnp.float32) + inbox[n, 0, 1].astype(jnp.float32)
        back = jnp.concatenate([upper, lower], 0)
        result = back * near_gate[d].astype(jnp.float32)
        gated[n] = result.astype(BF).reshape(gated.shape[1:])
        gated_in[z, n] = gated[n, z]
        if n:
            some = pl.ds(0, 2) if n == 1 else pl.ds(n, 1)
            for d in range(1, ZS):
                arrivals.append(send(gated.at[some, zmod(d)], gated_in.at[z, some], at_z(d)))
        back_bf[n] = back.astype(BF)

    inner = g_ring.shape[2]
    rows = g_ring.shape[1]
    into, twist, across = (in_hi, in_lo), (cos, sin), (ac_hi, ac_lo)

    def pair_block(i):
        return lambda at: pair_in[i, :, :, :, at].reshape(rows, CHUNK)

    early = len(copies)
    for copy in product_x:
        copy.wait_recv()
    product_over_z(0, XS // 2)
    pass_on(0)
    pass_on(1)
    pass_on(2)
    total_up(0)
    pass_on(3)
    total_up(1)
    total_up(2)
    filters_over_x()
    total_up(3)
    product_over_z(XS // 2, XS // 2)
    for copy in table_loads:
        copy.wait()
    for copy in filters_x:
        copy.wait_recv()
    forward(pair_block(1), into, twist, fourth, across, y_ref, z_ref, spec_f)
    stays = [load(back_bf.at[0], home_out.at[x])]
    flush(early)

    def gated_block(at):
        blocks = []
        for i in range(XS):
            e = lax.rem(i - x + XS, XS)
            blocks.append(gated_in[:, 2 * e - e // 2 - 4 * (e // 3), :, at])
        return jnp.stack(blocks, 1).reshape(rows, CHUNK)

    for copy in arrivals:
        copy.wait_recv()
    forward(
        gated_block,
        into, twist, fourth, across, y_ref, z_ref, spec_g,
    )

    width = gated_in.shape[2]
    lanes = skip_ref.shape[1]
    pick = lax.broadcasted_iota(jnp.int32, (width, lanes), 1) == z * width + lax.broadcasted_iota(
        jnp.int32, (width, lanes), 0
    )
    scale = jnp.sum(jnp.where(pick, skip_ref[pl.ds(x, 1), :], 0.0), axis=1, keepdims=True)
    gone = []
    turns = []

    def mixed_over_x():
        for copy in gone[0]:
            copy.wait_recv()
        turns.extend(
            send(landed.at[0, :, xmod(d)], mixed_out.at[x], at_x(d)) for d in range(1, XS)
        )
        stays.append(load(landed.at[0, :, x], mixed_out.at[x]))

    def filters_over_z(k):
        at = pl.ds((k - 1) * CHUNK, CHUNK)
        for copy in gone[k]:
            copy.wait_recv()
        turns.extend(
            send(landed.at[1, zmod(d), :, :, at], filters_out.at[:, z, :, at], at_z(d))
            for d in range(1, ZS)
        )
        stays.append(load(landed.at[1, z, :, :, at], filters_out.at[:, z, :, at]))

    def leave(which, start, size):
        if start == 0:
            combine(spec_g, (spec_f, spec_p)[which], z_ref)
            columns(z_ref, across, spec_r)
            unfold(spec_r, twist, fourth, u_ref)
        for c in range(start, start + size, CHUNK):
            at = pl.ds(c, CHUNK)
            u = u_ref[:, at]
            out = dot(of_hi[...], u) + dot(of_lo[...], u)
            if which == 0:
                out = out.reshape(ZS * XS, width, CHUNK)
                out = out + scale * gated_block(at).reshape(out.shape).astype(jnp.float32)
            leaving[which, :, :, :, at] = out.astype(BF).reshape(ZS, XS, width, CHUNK)
        at = pl.ds(start, size)
        if which == 0:
            gone.append(
                [send(leaving.at[0, zmod(d)], landed.at[0, z], at_z(d)) for d in range(1, ZS)]
            )
            landed[0, z] = leaving[0, z]
        else:
            gone.append(
                [
                    send(leaving.at[1, :, xmod(d), :, at], landed.at[1, :, x, :, at], at_x(d))
                    for d in range(1, XS)
                ]
            )
            landed[1, :, x, :, at] = leaving[1, :, x, :, at]

    leave(0, 0, inner)
    for copy in product_z:
        copy.wait_recv()
    forward(pair_block(0), into, twist, fourth, across, y_ref, z_ref, spec_p)
    middle = len(copies)
    leave(1, 0, CHUNK)
    leave(1, CHUNK, CHUNK)
    filters_over_z(1)
    filters_over_z(2)
    for n, off in enumerate(offsets):
        if n:
            homes.append(send(back_bf.at[n], home_out.at[x], at_x(off)))
    mixed_over_x()
    flush(middle)
    for copy in stays:
        copy.wait()
    for copy in homes + turns:
        copy.wait_recv()
    flush(len(copies))
    assert len(copies) == send_sems.shape[0]
    assert len(loads) == local_sems.shape[0]


def layer(grad_out, out_weight, gate_in, gate_out, values, filters, skip_scale):
    rows, inner = gate_in.shape
    deep, wide = out_weight.shape
    width = rows // (ZS * XS)
    into, out_of, cos, sin, across, fourth = make_tables(ZS * XS, width, inner)
    tables = (*into, *out_of, cos, sin, *across, fourth)
    spec_rows = cos.shape[0]
    split = (XS, ZS, width, inner)
    count = 128

    def vmem(shape, dtype=BF):
        return pltpu.VMEM(shape, dtype)

    spec = vmem((4, spec_rows, inner // 2), jnp.float32)
    return pl.pallas_call(
        layer_kernel,
        out_shape=[
            jax.ShapeDtypeStruct((XS, deep, inner), BF),
            jax.ShapeDtypeStruct(split, BF),
            jax.ShapeDtypeStruct(split, BF),
        ],
        in_specs=[pl.BlockSpec(memory_space=pl.ANY)] * 6
        + [VMEM]
        + [pl.BlockSpec(memory_space=pl.ANY)] * len(tables),
        out_specs=[pl.BlockSpec(memory_space=pl.ANY)] * 3,
        scratch_shapes=[
            vmem(split),
            vmem(split),
            vmem(split, jnp.float32),
            *[vmem(t.shape, t.dtype) for t in tables],
            vmem((ZS, deep, wide)),
            vmem((YS, deep, wide)),
            vmem((YS, deep, wide)),
            vmem((XS,) + grad_out.shape),
            vmem((XS,) + grad_out.shape),
            vmem((XS, deep, inner), jnp.float32),
            vmem((XS, 2, deep // 2, inner), jnp.float32),
            vmem((XS, 2, 2, deep // 2, inner)),
            vmem((XS, 2, 2, deep // 2, inner)),
            vmem((XS, 2, deep // 2, inner)),
            vmem((XS, 2, deep // 2, inner)),
            vmem((XS, deep, inner)),
            vmem((XS, deep, inner)),
            vmem((XS, ZS, width, inner)),
            vmem((ZS, XS, width, inner)),
            vmem((2,) + split),
            vmem((2, ZS, XS, width, inner)),
            vmem((2, ZS, XS, width, inner)),
            vmem((2 * spec_rows, inner), jnp.float32),
            vmem((4, spec_rows, inner // 2)),
            vmem((2 * spec_rows, inner)),
            spec,
            spec,
            spec,
            spec,
            vmem((2, ZS, XS, width, inner)),
            vmem((2, ZS, XS, width, inner)),
            pltpu.SemaphoreType.DMA((count,)),
            pltpu.SemaphoreType.DMA((count,)),
            pltpu.SemaphoreType.DMA((19,)),
        ],
        compiler_params=pltpu.CompilerParams(
            collective_id=0, has_side_effects=True, vmem_limit_bytes=58 * 1024 * 1024
        ),
        cost_estimate=pl.CostEstimate(flops=10 * 10**9, bytes_accessed=20 * 10**6, transcendentals=0),
    )(
        out_weight,
        grad_out,
        gate_in.reshape(split),
        values.reshape(split),
        gate_out.reshape(XS, deep, inner),
        filters.reshape(split),
        skip_scale.reshape(XS, deep),
        *tables,
    )


def shards(grad_out, out_weight, gate_in, gate_out, values, conv_out, filters, skip_scale):
    rows, inner = gate_in.shape
    home, grad_filters, mixed = layer(
        grad_out, out_weight, gate_in, gate_out, values, filters, skip_scale
    )

    def wide(block):
        return block.reshape(rows, inner).astype(jnp.float32)

    grad_gate_out = (wide(home) * wide(conv_out)).astype(BF)
    grad_gate_in = (wide(mixed) * wide(values)).astype(BF)
    grad_values = (wide(mixed) * wide(gate_in)).astype(BF)
    return (grad_gate_in, grad_values, grad_gate_out, wide(grad_filters))


def solution(mesh):
    placed = (
        P("seq", "ch"),
        P("seq", "ch"),
        P("ch", "seq"),
        P("ch", "seq"),
        P("ch", "seq"),
        P("ch", "seq"),
        P("ch", "seq"),
        P("ch"),
    )
    return jax.shard_map(
        shards,
        mesh=mesh,
        in_specs=placed,
        out_specs=(P("ch", "seq"), P("ch", "seq"), P("ch", "seq"), P("ch", "seq")),
        check_vma=False,
    )
```

```python
import jax
import jax.numpy as jnp
import ml_dtypes
import numpy as np
from jax import lax
from jax.experimental import pallas as pl
from jax.experimental.pallas import tpu as pltpu
from jax.sharding import PartitionSpec as P

OUTER = 64
CHUNK = 256
STEP = 16


def split_pair(table):
    high = table.astype(np.float32).astype(ml_dtypes.bfloat16)
    low = (table - high.astype(np.float64)).astype(np.float32).astype(ml_dtypes.bfloat16)
    return high, low


def make_tables(blocks, width, inner):
    total = OUTER * inner
    half = OUTER // 2 + 1
    k = np.arange(half)
    a = np.arange(blocks)
    b = np.arange(inner)
    first = 2.0 * np.pi * (np.outer(k, a) % OUTER) / OUTER
    eye = np.eye(width)
    k_cos = np.kron(np.cos(first), eye)
    k_sin = np.kron(np.sin(first), eye)
    into = np.concatenate([k_cos, -k_sin], 0)
    weight = np.full((half, 1), 2.0)
    weight[0] = 1.0
    weight[-1] = 1.0
    weight = weight / total
    back_cos = np.kron((weight * np.cos(first)).T, eye)
    back_sin = np.kron((weight * np.sin(first)).T, eye)
    out_of = np.concatenate([back_cos, back_sin], 1)
    turn = 2.0 * np.pi * (np.outer(k, b) % total) / total
    turn = np.repeat(turn, width, axis=0)
    quarter = inner // 4
    c = np.arange(quarter)
    second = 2.0 * np.pi * (np.outer(c, c) % quarter) / quarter
    fourth = 2.0 * np.pi * np.outer(np.arange(4), c) / inner
    fourth = np.concatenate([np.cos(fourth), np.sin(fourth)], 0)
    c, s = np.cos(second), np.sin(second)
    across = np.concatenate([np.concatenate([c, -s], 1), np.concatenate([s, c], 1)], 0)
    return (
        split_pair(into),
        split_pair(out_of),
        np.cos(turn).astype(np.float32),
        np.sin(turn).astype(np.float32),
        split_pair(across),
        fourth.astype(np.float32),
    )


def dot(left, right):
    return jnp.dot(left, right, preferred_element_type=jnp.float32)


def turned(real, imag, cos, sin):
    return real * cos + imag * sin, imag * cos - real * sin


ZS, XS, YS = 8, 4, 4
VMEM = pl.BlockSpec(memory_space=pltpu.VMEM)
MESH = pl.DeviceIdType.MESH
BF = jnp.bfloat16


def four_way(parts):
    (re0, im0), (re1, im1), (re2, im2), (re3, im3) = parts
    sum_re, sum_im, dif_re, dif_im = re0 + re2, im0 + im2, re0 - re2, im0 - im2
    odd_re, odd_im, gap_re, gap_im = re1 + re3, im1 + im3, re1 - re3, im1 - im3
    return (
        (sum_re + odd_re, sum_im + odd_im),
        (dif_re + gap_im, dif_im - gap_re),
        (sum_re - odd_re, sum_im - odd_im),
        (dif_re - gap_im, dif_im + gap_re),
    )


def by_rows(rows, body):
    @pl.loop(0, rows // STEP, unroll=3)
    def _(i):
        body(pl.ds(pl.multiple_of(i * STEP, STEP), STEP), i * STEP)


def turn_fourth(part, fourth, r):
    if r == 0:
        return part
    return turned(*part, fourth[pl.ds(r, 1), :], fourth[pl.ds(4 + r, 1), :])


def forward(block_of, into, twist, fourth, across, y_ref, z_ref, out_ref):
    rows = z_ref.shape[1]
    quarter = z_ref.shape[2] // 2

    for c in range(y_ref.shape[1] // CHUNK):
        at = pl.ds(c * CHUNK, CHUNK)
        block = block_of(at)
        y_ref[:, at] = sum(dot(table[...], block) for table in into)

    def body(at, start):
        far = pl.ds(pl.multiple_of(rows + start, STEP), STEP)
        parts = []
        for q in range(4):
            col = pl.ds(q * quarter, quarter)
            parts.append(turned(y_ref[at, col], y_ref[far, col], twist[0][at, col], twist[1][at, col]))
        for r, part in enumerate(four_way(parts)):
            real, imag = turn_fourth(part, fourth, r)
            z_ref[r, at, :quarter] = real.astype(BF)
            z_ref[r, at, quarter:] = imag.astype(BF)

    by_rows(rows, body)
    columns(z_ref, across, out_ref)


def columns(z_ref, across, out_ref):
    for r in range(4):
        z = z_ref[r]
        out_ref[r] = sum(dot(z, table[...]) for table in across)


def combine(grad_ref, other_ref, z_ref):
    rows = z_ref.shape[1]
    quarter = z_ref.shape[2] // 2

    def body(at, _):
        for r in range(4):
            g_re, g_im = grad_ref[r, at, :quarter], grad_ref[r, at, quarter:]
            o_re, o_im = other_ref[r, at, :quarter], other_ref[r, at, quarter:]
            z_ref[r, at, :quarter] = (g_re * o_re + g_im * o_im).astype(BF)
            z_ref[r, at, quarter:] = (g_re * o_im - g_im * o_re).astype(BF)

    by_rows(rows, body)


def unfold(spec_ref, twist, fourth, u_ref):
    rows = spec_ref.shape[1]
    quarter = spec_ref.shape[2] // 2

    def body(at, start):
        far = pl.ds(pl.multiple_of(rows + start, STEP), STEP)
        parts = [
            turn_fourth((spec_ref[r, at, :quarter], spec_ref[r, at, quarter:]), fourth, r)
            for r in range(4)
        ]
        for q, part in enumerate(four_way(parts)):
            col = pl.ds(q * quarter, quarter)
            real, imag = turned(*part, twist[0][at, col], twist[1][at, col])
            u_ref[at, col] = real.astype(BF)
            u_ref[far, col] = imag.astype(BF)

    by_rows(rows, body)


def layer_kernel(
    w_hbm, g_hbm, gate_in_hbm, values_hbm, gate_out_hbm, filters_hbm, skip_ref,
    in_hi_h, in_lo_h, of_hi_h, of_lo_h, cos_h, sin_h, ac_hi_h, ac_lo_h, fourth_h,
    home_out, filters_out, mixed_out,
    gate_in, values, filters, in_hi, in_lo, of_hi, of_lo, cos, sin, ac_hi, ac_lo, fourth,
    w_ring, w_mine, w_other, g_own, g_ring, g_other, own, hold, part, inbox, relay, final,
    near_gate, back_bf, gated, gated_in, stage, crossed, pair_in,
    y_ref, z_ref, u_ref, spec_r, spec_g, spec_p, spec_f, leaving, landed,
    send_sems, recv_sems, local_sems,
):
    s, h = lax.axis_index("seq"), lax.axis_index("ch")
    z, x = s // XS, s % XS
    y, core = h // 2, h % 2

    def zmod(d):
        return lax.rem(z + d + ZS, ZS)

    def xmod(d):
        return lax.rem(x + d + XS, XS)

    def at_z(d):
        return (zmod(d) * XS + x, h)

    def at_x(d):
        return (z * XS + xmod(d), h)

    def at_y(d):
        return (s, lax.rem(y + d + YS, YS) * 2 + core)

    sibling = (s, y * 2 + 1 - core)
    peers = [at_z(d) for d in range(1, ZS)] + [at_x(d) for d in range(1, XS)]
    peers += [at_y(d) for d in (1, -1)] + [sibling]

    barrier = pltpu.get_barrier_semaphore()
    for peer in peers:
        pl.semaphore_signal(barrier, inc=1, device_id=peer, device_id_type=MESH)

    loads = []

    def load(src, dst):
        copy = pltpu.make_async_copy(src, dst, local_sems.at[len(loads)])
        copy.start()
        loads.append(copy)
        return copy

    w_load = load(w_hbm, w_ring.at[z])
    g_load = load(g_hbm, g_own)
    pair_loads = [load(gate_in_hbm, gate_in), load(values_hbm, values), load(filters_hbm, filters)]
    gate_load = load(gate_out_hbm.at[x], near_gate.at[0])
    table_loads = [
        load(src, dst)
        for src, dst in (
            (in_hi_h, in_hi), (in_lo_h, in_lo), (ac_hi_h, ac_hi), (ac_lo_h, ac_lo),
            (cos_h, cos), (sin_h, sin), (fourth_h, fourth), (of_hi_h, of_hi), (of_lo_h, of_lo),
        )
    ]
    pl.semaphore_wait(barrier, len(peers))

    copies = []

    def send(src, dst, device):
        k = len(copies)
        copy = pltpu.make_async_remote_copy(
            src_ref=src, dst_ref=dst, send_sem=send_sems.at[k], recv_sem=recv_sems.at[k],
            device_id=device, device_id_type=MESH,
        )
        copy.start()
        copies.append(copy)
        return copy

    waited = [0]

    def flush(count):
        for copy in copies[waited[0] : count]:
            copy.wait_send()
        waited[0] = count

    half_w = w_ring.shape[1] // 2
    half_g = g_ring.shape[1] // 2
    first, second = pl.ds(0, half_w), pl.ds(half_w, half_w)
    top, low = pl.ds(0, half_g), pl.ds(half_g, half_g)

    halves = (first, second)
    ring = {}
    for side in (0, 1):
        for way in (1, -1):
            rows = halves[side if way == 1 else 1 - side]
            ring[way, side] = send(w_hbm.at[rows], w_ring.at[z, rows], at_z(way))
    g_load.wait()
    for part_of in (top, low):
        g_ring[x, part_of, :] = g_own[:, part_of].astype(jnp.float32).T.astype(BF)
    right_top = send(g_ring.at[x, top], g_ring.at[x, top], at_x(1))
    left_low = send(g_ring.at[x, low], g_ring.at[x, low], at_x(-1))
    right_low = send(g_ring.at[x, low], g_ring.at[x, low], at_x(1))
    left_top = send(g_ring.at[x, top], g_ring.at[x, top], at_x(-1))
    shared = [send(g_ring.at[x], g_other.at[0], sibling)]
    w_load.wait()
    for copy in pair_loads:
        copy.wait()
    for i in range(XS):
        product = gate_in[i].astype(jnp.float32) * values[i].astype(jnp.float32)
        stage[0, i] = product.astype(BF)
        stage[1, i] = filters[i].astype(BF)

    w_shared = []

    def step(r):
        for side in (0, 1):
            for way in (1, -1):
                if r == ZS // 2 and side:
                    continue
                ring[way, side].wait_recv()
                if r == ZS // 2 or (r == ZS // 2 - 1 and side):
                    continue
                block = w_ring.at[zmod(-r * way), halves[side if way == 1 else 1 - side]]
                ring[way, side] = send(block, block, at_z(way))
        even, odd = (0, 2, -2, 4)[r - 1], (1, -1, 3, -3)[r - 1]
        e = lax.rem(1 - core + z, 2)
        row = zmod(even + e * (odd - even))
        w_shared.append(send(w_ring.at[row], w_other.at[lax.rem(row // 2 - y + YS, YS)], sibling))

    step(1)
    right_top.wait_recv()
    far_top = send(g_ring.at[xmod(-1), top], g_ring.at[xmod(-1), top], at_x(1))
    left_low.wait_recv()
    far_low = send(g_ring.at[xmod(1), low], g_ring.at[xmod(1), low], at_x(-1))
    step(2)
    step(3)
    product_x = [
        send(stage.at[0, xmod(d)], crossed.at[0, :, x], at_x(d)) for d in range(1, XS)
    ]
    crossed[0, :, x] = stage[0, x]
    product_z = []

    def product_over_z(start, size):
        at = pl.ds(start, size)
        product_z.extend(
            send(crossed.at[0, zmod(d), at], pair_in.at[0, z, at], at_z(d)) for d in range(1, ZS)
        )
        pair_in[0, z, at] = crossed[0, z, at]

    filters_z = [
        send(stage.at[1, :, zmod(d)], crossed.at[1, z], at_z(d)) for d in range(1, ZS)
    ]
    crossed[1, z] = stage[1, :, z]
    filters_x = []

    def filters_over_x():
        for copy in filters_z:
            copy.wait_recv()
        filters_x.extend(
            send(crossed.at[1, :, xmod(d)], pair_in.at[1, :, x], at_x(d)) for d in range(1, XS)
        )
        pair_in[1, :, x] = crossed[1, :, x]

    right_low.wait_recv()
    shared.append(send(g_ring.at[xmod(-1)], g_other.at[1], sibling))
    left_top.wait_recv()
    shared.append(send(g_ring.at[xmod(1)], g_other.at[2], sibling))
    step(4)

    def rows_for(d, of_core):
        return lax.rem(y + d, YS) * 2 + of_core

    for d in range(YS):
        w_mine[d] = w_ring[rows_for(d, core)]
    for copy in w_shared:
        copy.wait_recv()

    offsets = (0, -1, 1, 2)
    parts = []
    passed = []
    gates = []
    deep = w_ring.shape[1]
    wide = (YS * deep, w_ring.shape[2])

    def pass_on(n):
        for side in range(2):
            parts[n][side].wait_recv()
            relay[n, side] = (hold[n, side] + inbox[n, side, 0].astype(jnp.float32)).astype(BF)
            passed.append(send(relay.at[n, side], final.at[n, side], at_y(1 - 2 * side)))

    for n, off in enumerate(offsets):
        if n == 3:
            far_top.wait_recv()
            far_low.wait_recv()
            gates.extend(
                send(gate_out_hbm.at[xmod(d)], near_gate.at[d], at_x(d)) for d in range(1, XS)
            )
            shared.append(send(g_ring.at[xmod(2)], g_other.at[3], sibling))
        shared[n].wait_recv()

        @pl.loop(0, g_ring.shape[2] // CHUNK)
        def _(i, n=n, off=off):
            at = pl.ds(pl.multiple_of(i * CHUNK, CHUNK), CHUNK)
            total = dot(w_mine[...].reshape(wide), g_ring[xmod(off), :, at])
            total = total + dot(w_other[...].reshape(wide), g_other[n, :, at])
            total = total.reshape(YS, deep, CHUNK)
            own[n, :, at] = total[0]
            hold[n, 0, :, at] = total[1, :half_w]
            hold[n, 1, :, at] = total[3, half_w:]
            part[n, 0, 0, :, at] = total[2, :half_w].astype(BF)
            part[n, 0, 1, :, at] = total[1, half_w:].astype(BF)
            part[n, 1, 0, :, at] = total[2, half_w:].astype(BF)
            part[n, 1, 1, :, at] = total[3, :half_w].astype(BF)

        parts.append([send(part.at[n, side], inbox.at[n, side], at_y(1 - 2 * side)) for side in range(2)])

    arrivals = []
    homes = []

    def total_up(n):
        for copy in passed[2 * n : 2 * n + 2]:
            copy.wait_recv()
        d = -offsets[n] % XS
        if d:
            gates[d - 1].wait_recv()
        else:
            gate_load.wait()
        upper = own[n, :half_w] + final[n, 0].astype(jnp.float32) + inbox[n, 1, 1].astype(jnp.float32)
        lower = own[n, half_w:] + final[n, 1].astype(jnp.float32) + inbox[n, 0, 1].astype(jnp.float32)
        back = jnp.concatenate([upper, lower], 0)
        result = back * near_gate[d].astype(jnp.float32)
        gated[n] = result.astype(BF).reshape(gated.shape[1:])
        gated_in[z, n] = gated[n, z]
        if n:
            some = pl.ds(0, 2) if n == 1 else pl.ds(n, 1)
            for d in range(1, ZS):
                arrivals.append(send(gated.at[some, zmod(d)], gated_in.at[z, some], at_z(d)))
        back_bf[n] = back.astype(BF)

    inner = own.shape[2]
    rows = gated_in.shape[0] * gated_in.shape[1] * gated_in.shape[2]
    into, twist, across = (in_hi, in_lo), (cos, sin), (ac_hi, ac_lo)

    def pair_block(i):
        return lambda at: pair_in[i, :, :, :, at].reshape(rows, CHUNK)

    early = len(copies)
    for copy in product_x:
        copy.wait_recv()
    product_over_z(0, XS // 2)
    pass_on(0)
    pass_on(1)
    pass_on(2)
    total_up(0)
    pass_on(3)
    total_up(1)
    total_up(2)
    filters_over_x()
    total_up(3)
    product_over_z(XS // 2, XS // 2)
    for copy in table_loads:
        copy.wait()
    for copy in filters_x:
        copy.wait_recv()
    forward(pair_block(1), into, twist, fourth, across, y_ref, z_ref, spec_f)
    stays = [load(back_bf.at[0], home_out.at[x])]
    flush(early)

    def gated_block(at):
        blocks = []
        for i in range(XS):
            e = lax.rem(i - x + XS, XS)
            blocks.append(gated_in[:, 2 * e - e // 2 - 4 * (e // 3), :, at])
        return jnp.stack(blocks, 1).reshape(rows, CHUNK)

    for copy in arrivals:
        copy.wait_recv()
    forward(
        gated_block,
        into, twist, fourth, across, y_ref, z_ref, spec_g,
    )

    width = gated_in.shape[2]
    lanes = skip_ref.shape[1]
    pick = lax.broadcasted_iota(jnp.int32, (width, lanes), 1) == z * width + lax.broadcasted_iota(
        jnp.int32, (width, lanes), 0
    )
    scale = jnp.sum(jnp.where(pick, skip_ref[pl.ds(x, 1), :], 0.0), axis=1, keepdims=True)
    gone = []
    turns = []

    def mixed_over_x():
        for copy in gone[0]:
            copy.wait_recv()
        turns.extend(
            send(landed.at[0, :, xmod(d)], mixed_out.at[x], at_x(d)) for d in range(1, XS)
        )
        stays.append(load(landed.at[0, :, x], mixed_out.at[x]))

    def filters_over_z(k):
        at = pl.ds((k - 1) * CHUNK, CHUNK)
        for copy in gone[k]:
            copy.wait_recv()
        turns.extend(
            send(landed.at[1, zmod(d), :, :, at], filters_out.at[:, z, :, at], at_z(d))
            for d in range(1, ZS)
        )
        stays.append(load(landed.at[1, z, :, :, at], filters_out.at[:, z, :, at]))

    def leave(which, start, size):
        if start == 0:
            combine(spec_g, (spec_f, spec_p)[which], z_ref)
            columns(z_ref, across, spec_r)
            unfold(spec_r, twist, fourth, u_ref)
        for c in range(start, start + size, CHUNK):
            at = pl.ds(c, CHUNK)
            u = u_ref[:, at]
            out = dot(of_hi[...], u) + dot(of_lo[...], u)
            if which == 0:
                out = out.reshape(ZS * XS, width, CHUNK)
                out = out + scale * gated_block(at).reshape(out.shape).astype(jnp.float32)
            leaving[which, :, :, :, at] = out.astype(BF).reshape(ZS, XS, width, CHUNK)
        at = pl.ds(start, size)
        if which == 0:
            gone.append(
                [send(leaving.at[0, zmod(d)], landed.at[0, z], at_z(d)) for d in range(1, ZS)]
            )
            landed[0, z] = leaving[0, z]
        else:
            gone.append(
                [
                    send(leaving.at[1, :, xmod(d), :, at], landed.at[1, :, x, :, at], at_x(d))
                    for d in range(1, XS)
                ]
            )
            landed[1, :, x, :, at] = leaving[1, :, x, :, at]

    leave(0, 0, inner)
    for copy in product_z:
        copy.wait_recv()
    forward(pair_block(0), into, twist, fourth, across, y_ref, z_ref, spec_p)
    middle = len(copies)
    leave(1, 0, CHUNK)
    leave(1, CHUNK, CHUNK)
    filters_over_z(1)
    filters_over_z(2)
    for n, off in enumerate(offsets):
        if n:
            homes.append(send(back_bf.at[n], home_out.at[x], at_x(off)))
    mixed_over_x()
    flush(middle)
    for copy in stays:
        copy.wait()
    for copy in homes + turns:
        copy.wait_recv()
    flush(len(copies))
    assert len(copies) == send_sems.shape[0]
    assert len(loads) == local_sems.shape[0]


def layer(grad_out, out_weight, gate_in, gate_out, values, filters, skip_scale):
    rows, inner = gate_in.shape
    deep, wide = out_weight.shape
    width = rows // (ZS * XS)
    into, out_of, cos, sin, across, fourth = make_tables(ZS * XS, width, inner)
    tables = (*into, *out_of, cos, sin, *across, fourth)
    spec_rows = cos.shape[0]
    split = (XS, ZS, width, inner)
    count = 128

    def vmem(shape, dtype=BF):
        return pltpu.VMEM(shape, dtype)

    spec = vmem((4, spec_rows, inner // 2), jnp.float32)
    return pl.pallas_call(
        layer_kernel,
        out_shape=[
            jax.ShapeDtypeStruct((XS, deep, inner), BF),
            jax.ShapeDtypeStruct(split, BF),
            jax.ShapeDtypeStruct(split, BF),
        ],
        in_specs=[pl.BlockSpec(memory_space=pl.ANY)] * 6
        + [VMEM]
        + [pl.BlockSpec(memory_space=pl.ANY)] * len(tables),
        out_specs=[pl.BlockSpec(memory_space=pl.ANY)] * 3,
        scratch_shapes=[
            vmem(split),
            vmem(split),
            vmem(split, jnp.float32),
            *[vmem(t.shape, t.dtype) for t in tables],
            vmem((ZS, deep, wide)),
            vmem((YS, deep, wide)),
            vmem((YS, deep, wide)),
            vmem(grad_out.shape),
            vmem((XS,) + grad_out.shape[::-1]),
            vmem((XS,) + grad_out.shape[::-1]),
            vmem((XS, deep, inner), jnp.float32),
            vmem((XS, 2, deep // 2, inner), jnp.float32),
            vmem((XS, 2, 2, deep // 2, inner)),
            vmem((XS, 2, 2, deep // 2, inner)),
            vmem((XS, 2, deep // 2, inner)),
            vmem((XS, 2, deep // 2, inner)),
            vmem((XS, deep, inner)),
            vmem((XS, deep, inner)),
            vmem((XS, ZS, width, inner)),
            vmem((ZS, XS, width, inner)),
            vmem((2,) + split),
            vmem((2, ZS, XS, width, inner)),
            vmem((2, ZS, XS, width, inner)),
            vmem((2 * spec_rows, inner), jnp.float32),
            vmem((4, spec_rows, inner // 2)),
            vmem((2 * spec_rows, inner)),
            spec,
            spec,
            spec,
            spec,
            vmem((2, ZS, XS, width, inner)),
            vmem((2, ZS, XS, width, inner)),
            pltpu.SemaphoreType.DMA((count,)),
            pltpu.SemaphoreType.DMA((count,)),
            pltpu.SemaphoreType.DMA((19,)),
        ],
        compiler_params=pltpu.CompilerParams(
            collective_id=0, has_side_effects=True, vmem_limit_bytes=58 * 1024 * 1024
        ),
        cost_estimate=pl.CostEstimate(flops=10 * 10**9, bytes_accessed=20 * 10**6, transcendentals=0),
    )(
        out_weight,
        grad_out,
        gate_in.reshape(split),
        values.reshape(split),
        gate_out.reshape(XS, deep, inner),
        filters.reshape(split),
        skip_scale.reshape(XS, deep),
        *tables,
    )


def shards(grad_out, out_weight, gate_in, gate_out, values, conv_out, filters, skip_scale):
    rows, inner = gate_in.shape
    home, grad_filters, mixed = layer(
        grad_out, out_weight, gate_in, gate_out, values, filters, skip_scale
    )

    def wide(block):
        return block.reshape(rows, inner).astype(jnp.float32)

    grad_gate_out = (wide(home) * wide(conv_out)).astype(BF)
    grad_gate_in = (wide(mixed) * wide(values)).astype(BF)
    grad_values = (wide(mixed) * wide(gate_in)).astype(BF)
    return (grad_gate_in, grad_values, grad_gate_out, wide(grad_filters))


def solution(mesh):
    placed = (
        P("seq", "ch"),
        P("seq", "ch"),
        P("ch", "seq"),
        P("ch", "seq"),
        P("ch", "seq"),
        P("ch", "seq"),
        P("ch", "seq"),
        P("ch"),
    )
    return jax.shard_map(
        shards,
        mesh=mesh,
        in_specs=placed,
        out_specs=(P("ch", "seq"), P("ch", "seq"), P("ch", "seq"), P("ch", "seq")),
        check_vma=False,
    )
```

```python
import jax
import jax.numpy as jnp
import ml_dtypes
import numpy as np
from jax import lax
from jax.experimental import pallas as pl
from jax.experimental.pallas import tpu as pltpu
from jax.sharding import PartitionSpec as P

OUTER = 64
CHUNK = 256
STEP = 16


def split_pair(table):
    high = table.astype(np.float32).astype(ml_dtypes.bfloat16)
    low = (table - high.astype(np.float64)).astype(np.float32).astype(ml_dtypes.bfloat16)
    return high, low


def make_tables(blocks, width, inner):
    total = OUTER * inner
    half = OUTER // 2 + 1
    k = np.arange(half)
    a = np.arange(blocks)
    b = np.arange(inner)
    first = 2.0 * np.pi * (np.outer(k, a) % OUTER) / OUTER
    eye = np.eye(width)
    k_cos = np.kron(np.cos(first), eye)
    k_sin = np.kron(np.sin(first), eye)
    into = np.concatenate([k_cos, -k_sin], 0)
    weight = np.full((half, 1), 2.0)
    weight[0] = 1.0
    weight[-1] = 1.0
    weight = weight / total
    back_cos = np.kron((weight * np.cos(first)).T, eye)
    back_sin = np.kron((weight * np.sin(first)).T, eye)
    out_of = np.concatenate([back_cos, back_sin], 1)
    turn = 2.0 * np.pi * (np.outer(k, b) % total) / total
    turn = np.repeat(turn, width, axis=0)
    quarter = inner // 4
    c = np.arange(quarter)
    second = 2.0 * np.pi * (np.outer(c, c) % quarter) / quarter
    fourth = 2.0 * np.pi * np.outer(np.arange(4), c) / inner
    fourth = np.concatenate([np.cos(fourth), np.sin(fourth)], 0)
    c, s = np.cos(second), np.sin(second)
    across = np.concatenate([np.concatenate([c, -s], 1), np.concatenate([s, c], 1)], 0)
    return (
        split_pair(into),
        split_pair(out_of),
        np.cos(turn).astype(np.float32),
        np.sin(turn).astype(np.float32),
        split_pair(across),
        fourth.astype(np.float32),
    )


def dot(left, right):
    return jnp.dot(left, right, preferred_element_type=jnp.float32)


def turned(real, imag, cos, sin):
    return real * cos + imag * sin, imag * cos - real * sin


ZS, XS, YS = 8, 4, 4
VMEM = pl.BlockSpec(memory_space=pltpu.VMEM)
MESH = pl.DeviceIdType.MESH
BF = jnp.bfloat16


def four_way(parts):
    (re0, im0), (re1, im1), (re2, im2), (re3, im3) = parts
    sum_re, sum_im, dif_re, dif_im = re0 + re2, im0 + im2, re0 - re2, im0 - im2
    odd_re, odd_im, gap_re, gap_im = re1 + re3, im1 + im3, re1 - re3, im1 - im3
    return (
        (sum_re + odd_re, sum_im + odd_im),
        (dif_re + gap_im, dif_im - gap_re),
        (sum_re - odd_re, sum_im - odd_im),
        (dif_re - gap_im, dif_im + gap_re),
    )


def by_rows(rows, body):
    @pl.loop(0, rows // STEP, unroll=3)
    def _(i):
        body(pl.ds(pl.multiple_of(i * STEP, STEP), STEP), i * STEP)


def turn_fourth(part, fourth, r):
    if r == 0:
        return part
    return turned(*part, fourth[pl.ds(r, 1), :], fourth[pl.ds(4 + r, 1), :])


def forward(block_of, into, twist, fourth, across, y_ref, z_ref, out_ref):
    rows = z_ref.shape[1]
    quarter = z_ref.shape[2] // 2

    for c in range(y_ref.shape[1] // CHUNK):
        at = pl.ds(c * CHUNK, CHUNK)
        block = block_of(at)
        y_ref[:, at] = sum(dot(table[...], block) for table in into)

    def body(at, start):
        far = pl.ds(pl.multiple_of(rows + start, STEP), STEP)
        parts = []
        for q in range(4):
            col = pl.ds(q * quarter, quarter)
            parts.append(turned(y_ref[at, col], y_ref[far, col], twist[0][at, col], twist[1][at, col]))
        for r, part in enumerate(four_way(parts)):
            real, imag = turn_fourth(part, fourth, r)
            z_ref[r, at, :quarter] = real.astype(BF)
            z_ref[r, at, quarter:] = imag.astype(BF)

    by_rows(rows, body)
    columns(z_ref, across, out_ref)


def columns(z_ref, across, out_ref):
    for r in range(4):
        z = z_ref[r]
        out_ref[r] = sum(dot(z, table[...]) for table in across)


def combine(grad_ref, other_ref, z_ref):
    rows = z_ref.shape[1]
    quarter = z_ref.shape[2] // 2

    def body(at, _):
        for r in range(4):
            g_re, g_im = grad_ref[r, at, :quarter], grad_ref[r, at, quarter:]
            o_re, o_im = other_ref[r, at, :quarter], other_ref[r, at, quarter:]
            z_ref[r, at, :quarter] = (g_re * o_re + g_im * o_im).astype(BF)
            z_ref[r, at, quarter:] = (g_re * o_im - g_im * o_re).astype(BF)

    by_rows(rows, body)


def unfold(spec_ref, twist, fourth, u_ref):
    rows = spec_ref.shape[1]
    quarter = spec_ref.shape[2] // 2

    def body(at, start):
        far = pl.ds(pl.multiple_of(rows + start, STEP), STEP)
        parts = [
            turn_fourth((spec_ref[r, at, :quarter], spec_ref[r, at, quarter:]), fourth, r)
            for r in range(4)
        ]
        for q, part in enumerate(four_way(parts)):
            col = pl.ds(q * quarter, quarter)
            real, imag = turned(*part, twist[0][at, col], twist[1][at, col])
            u_ref[at, col] = real.astype(BF)
            u_ref[far, col] = imag.astype(BF)

    by_rows(rows, body)


def layer_kernel(
    w_hbm, g_hbm, gate_in_hbm, values_hbm, gate_out_hbm, filters_hbm, skip_ref,
    in_hi_h, in_lo_h, of_hi_h, of_lo_h, cos_h, sin_h, ac_hi_h, ac_lo_h, fourth_h,
    home_out, filters_out, mixed_out,
    gate_in, values, filters, in_hi, in_lo, of_hi, of_lo, cos, sin, ac_hi, ac_lo, fourth,
    w_ring, w_mine, w_other, g_own, g_ring, g_other, own, hold, part, inbox, relay, final,
    near_gate, back_bf, gated, gated_in, stage, crossed, pair_in,
    y_ref, z_ref, u_ref, spec_r, spec_g, spec_p, spec_f, leaving, landed,
    send_sems, recv_sems, local_sems,
):
    s, h = lax.axis_index("seq"), lax.axis_index("ch")
    z, x = s // XS, s % XS
    y, core = h // 2, h % 2

    def zmod(d):
        return lax.rem(z + d + ZS, ZS)

    def xmod(d):
        return lax.rem(x + d + XS, XS)

    def at_z(d):
        return (zmod(d) * XS + x, h)

    def at_x(d):
        return (z * XS + xmod(d), h)

    def at_y(d):
        return (s, lax.rem(y + d + YS, YS) * 2 + core)

    sibling = (s, y * 2 + 1 - core)
    peers = [at_z(d) for d in range(1, ZS)] + [at_x(d) for d in range(1, XS)]
    peers += [at_y(d) for d in (1, -1)] + [sibling]

    barrier = pltpu.get_barrier_semaphore()
    for peer in peers:
        pl.semaphore_signal(barrier, inc=1, device_id=peer, device_id_type=MESH)

    loads = []

    def load(src, dst):
        copy = pltpu.make_async_copy(src, dst, local_sems.at[len(loads)])
        copy.start()
        loads.append(copy)
        return copy

    w_load = load(w_hbm, w_ring.at[z])
    g_load = load(g_hbm, g_own)
    pair_loads = [load(gate_in_hbm, gate_in), load(values_hbm, values), load(filters_hbm, filters)]
    gate_load = load(gate_out_hbm.at[x], near_gate.at[0])
    table_loads = [
        load(src, dst)
        for src, dst in (
            (in_hi_h, in_hi), (in_lo_h, in_lo), (ac_hi_h, ac_hi), (ac_lo_h, ac_lo),
            (cos_h, cos), (sin_h, sin), (fourth_h, fourth), (of_hi_h, of_hi), (of_lo_h, of_lo),
        )
    ]
    pl.semaphore_wait(barrier, len(peers))

    copies = []

    def send(src, dst, device):
        k = len(copies)
        copy = pltpu.make_async_remote_copy(
            src_ref=src, dst_ref=dst, send_sem=send_sems.at[k], recv_sem=recv_sems.at[k],
            device_id=device, device_id_type=MESH,
        )
        copy.start()
        copies.append(copy)
        return copy

    waited = [0]

    def flush(count):
        for copy in copies[waited[0] : count]:
            copy.wait_send()
        waited[0] = count

    half_w = w_ring.shape[1] // 2
    half_g = g_ring.shape[1] // 2
    first, second = pl.ds(0, half_w), pl.ds(half_w, half_w)
    top, low = pl.ds(0, half_g), pl.ds(half_g, half_g)

    halves = (first, second)
    ring = {}
    for side in (0, 1):
        for way in (1, -1):
            rows = halves[side if way == 1 else 1 - side]
            ring[way, side] = send(w_hbm.at[rows], w_ring.at[z, rows], at_z(way))
    g_load.wait()
    for part_of in (top, low):
        g_ring[x, part_of, :] = g_own[:, part_of].astype(jnp.float32).T.astype(BF)
    right_top = send(g_ring.at[x, top], g_ring.at[x, top], at_x(1))
    left_low = send(g_ring.at[x, low], g_ring.at[x, low], at_x(-1))
    right_low = send(g_ring.at[x, low], g_ring.at[x, low], at_x(1))
    left_top = send(g_ring.at[x, top], g_ring.at[x, top], at_x(-1))
    shared = [send(g_ring.at[x], g_other.at[0], sibling)]
    w_load.wait()
    for copy in pair_loads:
        copy.wait()
    for i in range(XS):
        product = gate_in[i].astype(jnp.float32) * values[i].astype(jnp.float32)
        stage[0, i] = product.astype(BF)
        stage[1, i] = filters[i].astype(BF)

    w_shared = []

    def step(r):
        for side in (0, 1):
            for way in (1, -1):
                if r == ZS // 2 and side:
                    continue
                ring[way, side].wait_recv()
                if r == ZS // 2 or (r == ZS // 2 - 1 and side):
                    continue
                block = w_ring.at[zmod(-r * way), halves[side if way == 1 else 1 - side]]
                ring[way, side] = send(block, block, at_z(way))
        even, odd = (0, 2, -2, 4)[r - 1], (1, -1, 3, -3)[r - 1]
        e = lax.rem(1 - core + z, 2)
        row = zmod(even + e * (odd - even))
        w_shared.append(send(w_ring.at[row], w_other.at[lax.rem(row // 2 - y + YS, YS)], sibling))

    step(1)
    right_top.wait_recv()
    far_top = send(g_ring.at[xmod(-1), top], g_ring.at[xmod(-1), top], at_x(1))
    left_low.wait_recv()
    far_low = send(g_ring.at[xmod(1), low], g_ring.at[xmod(1), low], at_x(-1))
    step(2)
    step(3)
    product_x = [
        send(stage.at[0, xmod(d)], crossed.at[0, :, x], at_x(d)) for d in range(1, XS)
    ]
    crossed[0, :, x] = stage[0, x]
    product_z = []

    def product_over_z(start, size):
        at = pl.ds(start, size)
        product_z.extend(
            send(crossed.at[0, zmod(d), at], pair_in.at[0, z, at], at_z(d)) for d in range(1, ZS)
        )
        pair_in[0, z, at] = crossed[0, z, at]

    filters_z = [
        send(stage.at[1, :, zmod(d)], crossed.at[1, z], at_z(d)) for d in range(1, ZS)
    ]
    crossed[1, z] = stage[1, :, z]
    filters_x = []

    def filters_over_x():
        for copy in filters_z:
            copy.wait_recv()
        filters_x.extend(
            send(crossed.at[1, :, xmod(d)], pair_in.at[1, :, x], at_x(d)) for d in range(1, XS)
        )
        pair_in[1, :, x] = crossed[1, :, x]

    right_low.wait_recv()
    shared.append(send(g_ring.at[xmod(-1)], g_other.at[1], sibling))
    left_top.wait_recv()
    shared.append(send(g_ring.at[xmod(1)], g_other.at[2], sibling))
    step(4)

    def rows_for(d, of_core):
        return lax.rem(y + d, YS) * 2 + of_core

    for d in range(YS):
        w_mine[d] = w_ring[rows_for(d, core)]
    for copy in w_shared:
        copy.wait_recv()

    offsets = (0, -1, 1, 2)
    parts = []
    passed = []
    gates = []
    deep = w_ring.shape[1]
    wide = (YS * deep, w_ring.shape[2])

    def pass_on(n):
        for side in range(2):
            parts[n][side].wait_recv()
            relay[n, side] = (hold[n, side] + inbox[n, side, 0].astype(jnp.float32)).astype(BF)
            passed.append(send(relay.at[n, side], final.at[n, side], at_y(1 - 2 * side)))

    for n, off in enumerate(offsets):
        if n == 3:
            far_top.wait_recv()
            far_low.wait_recv()
            gates.extend(
                send(gate_out_hbm.at[xmod(d)], near_gate.at[d], at_x(d)) for d in range(1, XS)
            )
            shared.append(send(g_ring.at[xmod(2)], g_other.at[3], sibling))
        shared[n].wait_recv()

        @pl.loop(0, g_ring.shape[2] // CHUNK)
        def _(i, n=n, off=off):
            at = pl.ds(pl.multiple_of(i * CHUNK, CHUNK), CHUNK)
            total = dot(w_mine[...].reshape(wide), g_ring[xmod(off), :, at])
            total = total + dot(w_other[...].reshape(wide), g_other[n, :, at])
            total = total.reshape(YS, deep, CHUNK)
            own[n, :, at] = total[0]
            hold[n, 0, :, at] = total[1, :half_w]
            hold[n, 1, :, at] = total[3, half_w:]
            part[n, 0, 0, :, at] = total[2, :half_w].astype(BF)
            part[n, 0, 1, :, at] = total[1, half_w:].astype(BF)
            part[n, 1, 0, :, at] = total[2, half_w:].astype(BF)
            part[n, 1, 1, :, at] = total[3, :half_w].astype(BF)

        parts.append([send(part.at[n, side], inbox.at[n, side], at_y(1 - 2 * side)) for side in range(2)])

    arrivals = []
    homes = []

    def total_up(n):
        for copy in passed[2 * n : 2 * n + 2]:
            copy.wait_recv()
        d = -offsets[n] % XS
        if d:
            gates[d - 1].wait_recv()
        else:
            gate_load.wait()
        upper = own[n, :half_w] + final[n, 0].astype(jnp.float32) + inbox[n, 1, 1].astype(jnp.float32)
        lower = own[n, half_w:] + final[n, 1].astype(jnp.float32) + inbox[n, 0, 1].astype(jnp.float32)
        back = jnp.concatenate([upper, lower], 0)
        result = back * near_gate[d].astype(jnp.float32)
        gated[n] = result.astype(BF).reshape(gated.shape[1:])
        gated_in[z, n] = gated[n, z]
        if n:
            some = pl.ds(0, 2) if n == 1 else pl.ds(n, 1)
            for d in range(1, ZS):
                arrivals.append(send(gated.at[some, zmod(d)], gated_in.at[z, some], at_z(d)))
        back_bf[n] = back.astype(BF)

    inner = own.shape[2]
    rows = gated_in.shape[0] * gated_in.shape[1] * gated_in.shape[2]
    into, twist, across = (in_hi, in_lo), (cos, sin), (ac_hi, ac_lo)

    def pair_block(i):
        return lambda at: pair_in[i, :, :, :, at].reshape(rows, CHUNK)

    early = len(copies)
    for copy in product_x:
        copy.wait_recv()
    product_over_z(0, XS // 2)
    pass_on(0)
    pass_on(1)
    pass_on(2)
    total_up(0)
    pass_on(3)
    total_up(1)
    total_up(2)
    filters_over_x()
    total_up(3)
    product_over_z(XS // 2, XS // 2)
    for copy in table_loads:
        copy.wait()
    for copy in filters_x:
        copy.wait_recv()
    forward(pair_block(1), into, twist, fourth, across, y_ref, z_ref, spec_f)
    stays = [load(back_bf.at[0], home_out.at[x])]
    for n, off in enumerate(offsets):
        if n:
            homes.append(send(back_bf.at[n], home_out.at[x], at_x(off)))
    flush(early)

    def gated_block(at):
        blocks = []
        for i in range(XS):
            e = lax.rem(i - x + XS, XS)
            blocks.append(gated_in[:, 2 * e - e // 2 - 4 * (e // 3), :, at])
        return jnp.stack(blocks, 1).reshape(rows, CHUNK)

    for copy in arrivals:
        copy.wait_recv()
    forward(
        gated_block,
        into, twist, fourth, across, y_ref, z_ref, spec_g,
    )

    width = gated_in.shape[2]
    lanes = skip_ref.shape[1]
    pick = lax.broadcasted_iota(jnp.int32, (width, lanes), 1) == z * width + lax.broadcasted_iota(
        jnp.int32, (width, lanes), 0
    )
    scale = jnp.sum(jnp.where(pick, skip_ref[pl.ds(x, 1), :], 0.0), axis=1, keepdims=True)
    gone = []
    turns = []

    def mixed_over_x():
        for copy in gone[0]:
            copy.wait_recv()
        turns.extend(
            send(landed.at[0, :, xmod(d)], mixed_out.at[x], at_x(d)) for d in range(1, XS)
        )
        stays.append(load(landed.at[0, :, x], mixed_out.at[x]))

    def filters_over_z(k):
        at = pl.ds((k - 1) * CHUNK, CHUNK)
        for copy in gone[k]:
            copy.wait_recv()
        turns.extend(
            send(landed.at[1, zmod(d), :, :, at], filters_out.at[:, z, :, at], at_z(d))
            for d in range(1, ZS)
        )
        stays.append(load(landed.at[1, z, :, :, at], filters_out.at[:, z, :, at]))

    def leave(which, start, size):
        if start == 0:
            combine(spec_g, (spec_f, spec_p)[which], z_ref)
            columns(z_ref, across, spec_r)
            unfold(spec_r, twist, fourth, u_ref)
        for c in range(start, start + size, CHUNK):
            at = pl.ds(c, CHUNK)
            u = u_ref[:, at]
            out = dot(of_hi[...], u) + dot(of_lo[...], u)
            if which == 0:
                out = out.reshape(ZS * XS, width, CHUNK)
                out = out + scale * gated_block(at).reshape(out.shape).astype(jnp.float32)
            leaving[which, :, :, :, at] = out.astype(BF).reshape(ZS, XS, width, CHUNK)
        at = pl.ds(start, size)
        if which == 0:
            gone.append(
                [send(leaving.at[0, zmod(d)], landed.at[0, z], at_z(d)) for d in range(1, ZS)]
            )
            landed[0, z] = leaving[0, z]
        else:
            gone.append(
                [
                    send(leaving.at[1, :, xmod(d), :, at], landed.at[1, :, x, :, at], at_x(d))
                    for d in range(1, XS)
                ]
            )
            landed[1, :, x, :, at] = leaving[1, :, x, :, at]

    leave(0, 0, inner)
    for copy in product_z:
        copy.wait_recv()
    forward(pair_block(0), into, twist, fourth, across, y_ref, z_ref, spec_p)
    middle = len(copies)
    leave(1, 0, CHUNK)
    leave(1, CHUNK, CHUNK)
    filters_over_z(1)
    filters_over_z(2)
    mixed_over_x()
    flush(middle)
    for copy in stays:
        copy.wait()
    for copy in homes + turns:
        copy.wait_recv()
    flush(len(copies))
    assert len(copies) == send_sems.shape[0]
    assert len(loads) == local_sems.shape[0]


def layer(grad_out, out_weight, gate_in, gate_out, values, filters, skip_scale):
    rows, inner = gate_in.shape
    deep, wide = out_weight.shape
    width = rows // (ZS * XS)
    into, out_of, cos, sin, across, fourth = make_tables(ZS * XS, width, inner)
    tables = (*into, *out_of, cos, sin, *across, fourth)
    spec_rows = cos.shape[0]
    split = (XS, ZS, width, inner)
    count = 128

    def vmem(shape, dtype=BF):
        return pltpu.VMEM(shape, dtype)

    spec = vmem((4, spec_rows, inner // 2), jnp.float32)
    return pl.pallas_call(
        layer_kernel,
        out_shape=[
            jax.ShapeDtypeStruct((XS, deep, inner), BF),
            jax.ShapeDtypeStruct(split, BF),
            jax.ShapeDtypeStruct(split, BF),
        ],
        in_specs=[pl.BlockSpec(memory_space=pl.ANY)] * 6
        + [VMEM]
        + [pl.BlockSpec(memory_space=pl.ANY)] * len(tables),
        out_specs=[pl.BlockSpec(memory_space=pl.ANY)] * 3,
        scratch_shapes=[
            vmem(split),
            vmem(split),
            vmem(split, jnp.float32),
            *[vmem(t.shape, t.dtype) for t in tables],
            vmem((ZS, deep, wide)),
            vmem((YS, deep, wide)),
            vmem((YS, deep, wide)),
            vmem(grad_out.shape),
            vmem((XS,) + grad_out.shape[::-1]),
            vmem((XS,) + grad_out.shape[::-1]),
            vmem((XS, deep, inner), jnp.float32),
            vmem((XS, 2, deep // 2, inner), jnp.float32),
            vmem((XS, 2, 2, deep // 2, inner)),
            vmem((XS, 2, 2, deep // 2, inner)),
            vmem((XS, 2, deep // 2, inner)),
            vmem((XS, 2, deep // 2, inner)),
            vmem((XS, deep, inner)),
            vmem((XS, deep, inner)),
            vmem((XS, ZS, width, inner)),
            vmem((ZS, XS, width, inner)),
            vmem((2,) + split),
            vmem((2, ZS, XS, width, inner)),
            vmem((2, ZS, XS, width, inner)),
            vmem((2 * spec_rows, inner), jnp.float32),
            vmem((4, spec_rows, inner // 2)),
            vmem((2 * spec_rows, inner)),
            spec,
            spec,
            spec,
            spec,
            vmem((2, ZS, XS, width, inner)),
            vmem((2, ZS, XS, width, inner)),
            pltpu.SemaphoreType.DMA((count,)),
            pltpu.SemaphoreType.DMA((count,)),
            pltpu.SemaphoreType.DMA((19,)),
        ],
        compiler_params=pltpu.CompilerParams(
            collective_id=0, has_side_effects=True, vmem_limit_bytes=58 * 1024 * 1024
        ),
        cost_estimate=pl.CostEstimate(flops=10 * 10**9, bytes_accessed=20 * 10**6, transcendentals=0),
    )(
        out_weight,
        grad_out,
        gate_in.reshape(split),
        values.reshape(split),
        gate_out.reshape(XS, deep, inner),
        filters.reshape(split),
        skip_scale.reshape(XS, deep),
        *tables,
    )


def finish_kernel(*refs):
    sources, results = refs[:6], refs[6:10]
    held, done, sems = refs[10:16], refs[16:20], refs[20]
    mixed, values, gate_in, home, conv_out, filters = held
    order = (3, 4, 0, 1, 2, 5)
    loads = {n: pltpu.make_async_copy(sources[n], held[n], sems.at[n]) for n in order}
    for n in order:
        loads[n].start()
    stores = []

    def close(n, needs, left, right):
        for need in needs:
            loads[need].wait()

        @pl.loop(0, left.shape[0] // 64)
        def _(i):
            at = pl.ds(pl.multiple_of(i * 64, 64), 64)
            value = left[at, :].astype(jnp.float32)
            if right is not None:
                value = value * right[at, :].astype(jnp.float32)
            done[n][at, :] = value.astype(done[n].dtype)

        stores.append(pltpu.make_async_copy(done[n], results[n], sems.at[6 + n]))
        stores[-1].start()

    close(2, (3, 4), home, conv_out)
    close(0, (0, 1), mixed, values)
    close(1, (2,), mixed, gate_in)
    close(3, (5,), filters, None)
    for store in stores:
        store.wait()


def finish(*arrays):
    shape = arrays[0].shape
    outs = [jax.ShapeDtypeStruct(shape, t) for t in (BF, BF, BF, jnp.float32)]
    hbm = pl.BlockSpec(memory_space=pl.ANY)
    return tuple(
        pl.pallas_call(
            finish_kernel,
            out_shape=outs,
            in_specs=[hbm] * 6,
            out_specs=[hbm] * 4,
            scratch_shapes=[pltpu.VMEM(shape, BF)] * 6
            + [pltpu.VMEM(o.shape, o.dtype) for o in outs]
            + [pltpu.SemaphoreType.DMA((10,))],
            compiler_params=pltpu.CompilerParams(vmem_limit_bytes=62 * 1024 * 1024),
            cost_estimate=pl.CostEstimate(flops=10**6, bytes_accessed=6 * 10**6, transcendentals=0),
        )(*arrays)
    )


def shards(grad_out, out_weight, gate_in, gate_out, values, conv_out, filters, skip_scale):
    rows, inner = gate_in.shape
    home, grad_filters, mixed = layer(
        grad_out, out_weight, gate_in, gate_out, values, filters, skip_scale
    )

    return finish(
        mixed.reshape(rows, inner), values, gate_in, home.reshape(rows, inner), conv_out,
        grad_filters.reshape(rows, inner),
    )


def solution(mesh):
    placed = (
        P("seq", "ch"),
        P("seq", "ch"),
        P("ch", "seq"),
        P("ch", "seq"),
        P("ch", "seq"),
        P("ch", "seq"),
        P("ch", "seq"),
        P("ch"),
    )
    return jax.shard_map(
        shards,
        mesh=mesh,
        in_specs=placed,
        out_specs=(P("ch", "seq"), P("ch", "seq"), P("ch", "seq"), P("ch", "seq")),
        check_vma=False,
    )
```

```python
import jax
import jax.numpy as jnp
import ml_dtypes
import numpy as np
from jax import lax
from jax.experimental import pallas as pl
from jax.experimental.pallas import tpu as pltpu
from jax.sharding import PartitionSpec as P

OUTER = 64
CHUNK = 256
STEP = 16


def split_pair(table):
    high = table.astype(np.float32).astype(ml_dtypes.bfloat16)
    low = (table - high.astype(np.float64)).astype(np.float32).astype(ml_dtypes.bfloat16)
    return high, low


def make_tables(blocks, width, inner):
    total = OUTER * inner
    half = OUTER // 2 + 1
    k = np.arange(half)
    a = np.arange(blocks)
    b = np.arange(inner)
    first = 2.0 * np.pi * (np.outer(k, a) % OUTER) / OUTER
    eye = np.eye(width)
    k_cos = np.kron(np.cos(first), eye)
    k_sin = np.kron(np.sin(first), eye)
    into = np.concatenate([k_cos, -k_sin], 0)
    weight = np.full((half, 1), 2.0)
    weight[0] = 1.0
    weight[-1] = 1.0
    weight = weight / total
    back_cos = np.kron((weight * np.cos(first)).T, eye)
    back_sin = np.kron((weight * np.sin(first)).T, eye)
    out_of = np.concatenate([back_cos, back_sin], 1)
    turn = 2.0 * np.pi * (np.outer(k, b) % total) / total
    turn = np.repeat(turn, width, axis=0)
    quarter = inner // 4
    c = np.arange(quarter)
    second = 2.0 * np.pi * (np.outer(c, c) % quarter) / quarter
    fourth = 2.0 * np.pi * np.outer(np.arange(4), c) / inner
    fourth = np.concatenate([np.cos(fourth), np.sin(fourth)], 0)
    c, s = np.cos(second), np.sin(second)
    across = np.concatenate([np.concatenate([c, -s], 1), np.concatenate([s, c], 1)], 0)
    return (
        split_pair(into),
        split_pair(out_of),
        np.cos(turn).astype(np.float32),
        np.sin(turn).astype(np.float32),
        split_pair(across),
        fourth.astype(np.float32),
    )


def dot(left, right):
    return jnp.dot(left, right, preferred_element_type=jnp.float32)


def turned(real, imag, cos, sin):
    return real * cos + imag * sin, imag * cos - real * sin


ZS, XS, YS = 8, 4, 4
VMEM = pl.BlockSpec(memory_space=pltpu.VMEM)
MESH = pl.DeviceIdType.MESH
BF = jnp.bfloat16


def four_way(parts):
    (re0, im0), (re1, im1), (re2, im2), (re3, im3) = parts
    sum_re, sum_im, dif_re, dif_im = re0 + re2, im0 + im2, re0 - re2, im0 - im2
    odd_re, odd_im, gap_re, gap_im = re1 + re3, im1 + im3, re1 - re3, im1 - im3
    return (
        (sum_re + odd_re, sum_im + odd_im),
        (dif_re + gap_im, dif_im - gap_re),
        (sum_re - odd_re, sum_im - odd_im),
        (dif_re - gap_im, dif_im + gap_re),
    )


def by_rows(rows, body):
    @pl.loop(0, rows // STEP, unroll=3)
    def _(i):
        body(pl.ds(pl.multiple_of(i * STEP, STEP), STEP), i * STEP)


def turn_fourth(part, fourth, r):
    if r == 0:
        return part
    return turned(*part, fourth[pl.ds(r, 1), :], fourth[pl.ds(4 + r, 1), :])


def forward(block_of, into, twist, fourth, across, y_ref, z_ref, out_ref):
    rows = z_ref.shape[1]
    quarter = z_ref.shape[2] // 2

    for c in range(y_ref.shape[1] // CHUNK):
        at = pl.ds(c * CHUNK, CHUNK)
        block = block_of(at)
        y_ref[:, at] = sum(dot(table[...], block) for table in into)

    def body(at, start):
        far = pl.ds(pl.multiple_of(rows + start, STEP), STEP)
        parts = []
        for q in range(4):
            col = pl.ds(q * quarter, quarter)
            parts.append(turned(y_ref[at, col], y_ref[far, col], twist[0][at, col], twist[1][at, col]))
        for r, part in enumerate(four_way(parts)):
            real, imag = turn_fourth(part, fourth, r)
            z_ref[r, at, :quarter] = real.astype(BF)
            z_ref[r, at, quarter:] = imag.astype(BF)

    by_rows(rows, body)
    columns(z_ref, across, out_ref)


def columns(z_ref, across, out_ref):
    for r in range(4):
        z = z_ref[r]
        out_ref[r] = sum(dot(z, table[...]) for table in across)


def combine(grad_ref, other_ref, z_ref):
    rows = z_ref.shape[1]
    quarter = z_ref.shape[2] // 2

    def body(at, _):
        for r in range(4):
            g_re, g_im = grad_ref[r, at, :quarter], grad_ref[r, at, quarter:]
            o_re, o_im = other_ref[r, at, :quarter], other_ref[r, at, quarter:]
            z_ref[r, at, :quarter] = (g_re * o_re + g_im * o_im).astype(BF)
            z_ref[r, at, quarter:] = (g_re * o_im - g_im * o_re).astype(BF)

    by_rows(rows, body)


def unfold(spec_ref, twist, fourth, u_ref):
    rows = spec_ref.shape[1]
    quarter = spec_ref.shape[2] // 2

    def body(at, start):
        far = pl.ds(pl.multiple_of(rows + start, STEP), STEP)
        parts = [
            turn_fourth((spec_ref[r, at, :quarter], spec_ref[r, at, quarter:]), fourth, r)
            for r in range(4)
        ]
        for q, part in enumerate(four_way(parts)):
            col = pl.ds(q * quarter, quarter)
            real, imag = turned(*part, twist[0][at, col], twist[1][at, col])
            u_ref[at, col] = real.astype(BF)
            u_ref[far, col] = imag.astype(BF)

    by_rows(rows, body)


def layer_kernel(
    w_hbm, g_hbm, gate_in_hbm, values_hbm, gate_out_hbm, filters_hbm, skip_ref,
    in_hi_h, in_lo_h, of_hi_h, of_lo_h, cos_h, sin_h, ac_hi_h, ac_lo_h, fourth_h,
    home_out, filters_out, mixed_out,
    gate_in, values, filters, in_hi, in_lo, of_hi, of_lo, cos, sin, ac_hi, ac_lo, fourth,
    w_ring, w_mine, w_other, g_own, g_ring, g_other, own, hold, part, inbox, relay, final,
    near_gate, back_bf, gated, gated_in, stage, crossed, pair_in,
    y_ref, z_ref, u_ref, spec_r, spec_g, spec_p, spec_f, leaving, landed,
    send_sems, recv_sems, local_sems,
):
    s, h = lax.axis_index("seq"), lax.axis_index("ch")
    z, x = s // XS, s % XS
    y, core = h // 2, h % 2

    def zmod(d):
        return lax.rem(z + d + ZS, ZS)

    def xmod(d):
        return lax.rem(x + d + XS, XS)

    def at_z(d):
        return (zmod(d) * XS + x, h)

    def at_x(d):
        return (z * XS + xmod(d), h)

    def at_y(d):
        return (s, lax.rem(y + d + YS, YS) * 2 + core)

    sibling = (s, y * 2 + 1 - core)
    peers = [at_z(d) for d in range(1, ZS)] + [at_x(d) for d in range(1, XS)]
    peers += [at_y(d) for d in (1, -1)] + [sibling]

    barrier = pltpu.get_barrier_semaphore()
    for peer in peers:
        pl.semaphore_signal(barrier, inc=1, device_id=peer, device_id_type=MESH)

    loads = []

    def load(src, dst):
        copy = pltpu.make_async_copy(src, dst, local_sems.at[len(loads)])
        copy.start()
        loads.append(copy)
        return copy

    w_load = load(w_hbm, w_ring.at[z])
    g_load = load(g_hbm, g_own)
    pair_loads = [load(gate_in_hbm, gate_in), load(values_hbm, values), load(filters_hbm, filters)]
    gate_load = load(gate_out_hbm.at[x], near_gate.at[0])
    table_loads = [
        load(src, dst)
        for src, dst in (
            (in_hi_h, in_hi), (in_lo_h, in_lo), (ac_hi_h, ac_hi), (ac_lo_h, ac_lo),
            (cos_h, cos), (sin_h, sin), (fourth_h, fourth), (of_hi_h, of_hi), (of_lo_h, of_lo),
        )
    ]
    pl.semaphore_wait(barrier, len(peers))

    copies = []

    def send(src, dst, device):
        k = len(copies)
        copy = pltpu.make_async_remote_copy(
            src_ref=src, dst_ref=dst, send_sem=send_sems.at[k], recv_sem=recv_sems.at[k],
            device_id=device, device_id_type=MESH,
        )
        copy.start()
        copies.append(copy)
        return copy

    waited = [0]

    def flush(count):
        for copy in copies[waited[0] : count]:
            copy.wait_send()
        waited[0] = count

    half_w = w_ring.shape[1] // 2
    half_g = g_ring.shape[1] // 2
    first, second = pl.ds(0, half_w), pl.ds(half_w, half_w)
    top, low = pl.ds(0, half_g), pl.ds(half_g, half_g)

    halves = (first, second)
    ring = {}
    for side in (0, 1):
        for way in (1, -1):
            rows = halves[side if way == 1 else 1 - side]
            ring[way, side] = send(w_hbm.at[rows], w_ring.at[z, rows], at_z(way))
    g_load.wait()
    for part_of in (top, low):
        g_ring[x, part_of, :] = g_own[:, part_of].astype(jnp.float32).T.astype(BF)
    right_top = send(g_ring.at[x, top], g_ring.at[x, top], at_x(1))
    left_low = send(g_ring.at[x, low], g_ring.at[x, low], at_x(-1))
    right_low = send(g_ring.at[x, low], g_ring.at[x, low], at_x(1))
    left_top = send(g_ring.at[x, top], g_ring.at[x, top], at_x(-1))
    shared = [send(g_ring.at[x], g_other.at[0], sibling)]
    w_load.wait()
    for copy in pair_loads:
        copy.wait()
    for i in range(XS):
        product = gate_in[i].astype(jnp.float32) * values[i].astype(jnp.float32)
        stage[0, i] = product.astype(BF)
        stage[1, i] = filters[i].astype(BF)

    w_shared = []

    def step(r):
        for side in (0, 1):
            for way in (1, -1):
                if r == ZS // 2 and side:
                    continue
                ring[way, side].wait_recv()
                if r == ZS // 2 or (r == ZS // 2 - 1 and side):
                    continue
                block = w_ring.at[zmod(-r * way), halves[side if way == 1 else 1 - side]]
                ring[way, side] = send(block, block, at_z(way))
        even, odd = (0, 2, -2, 4)[r - 1], (1, -1, 3, -3)[r - 1]
        e = lax.rem(1 - core + z, 2)
        row = zmod(even + e * (odd - even))
        w_shared.append(send(w_ring.at[row], w_other.at[lax.rem(row // 2 - y + YS, YS)], sibling))

    step(1)
    right_top.wait_recv()
    far_top = send(g_ring.at[xmod(-1), top], g_ring.at[xmod(-1), top], at_x(1))
    left_low.wait_recv()
    far_low = send(g_ring.at[xmod(1), low], g_ring.at[xmod(1), low], at_x(-1))
    step(2)
    step(3)
    product_x = []
    crossed[0, :, x] = stage[0, x]
    product_z = []

    def product_over_z(start, size):
        at = pl.ds(start, size)
        product_z.extend(
            send(crossed.at[0, zmod(d), at], pair_in.at[0, z, at], at_z(d)) for d in range(1, ZS)
        )
        pair_in[0, z, at] = crossed[0, z, at]

    filters_z = [
        send(stage.at[1, :, zmod(d)], crossed.at[1, z], at_z(d)) for d in range(1, ZS)
    ]
    crossed[1, z] = stage[1, :, z]
    filters_x = []

    def filters_over_x():
        for copy in filters_z:
            copy.wait_recv()
        filters_x.extend(
            send(crossed.at[1, :, xmod(d)], pair_in.at[1, :, x], at_x(d)) for d in range(1, XS)
        )
        pair_in[1, :, x] = crossed[1, :, x]

    right_low.wait_recv()
    shared.append(send(g_ring.at[xmod(-1)], g_other.at[1], sibling))
    left_top.wait_recv()
    shared.append(send(g_ring.at[xmod(1)], g_other.at[2], sibling))
    step(4)

    def rows_for(d, of_core):
        return lax.rem(y + d, YS) * 2 + of_core

    for d in range(YS):
        w_mine[d] = w_ring[rows_for(d, core)]
    for copy in w_shared:
        copy.wait_recv()

    offsets = (0, -1, 1, 2)
    parts = []
    passed = []
    gates = []
    deep = w_ring.shape[1]
    wide = (YS * deep, w_ring.shape[2])

    def pass_on(n):
        for side in range(2):
            parts[n][side].wait_recv()
            relay[n, side] = (hold[n, side] + inbox[n, side, 0].astype(jnp.float32)).astype(BF)
            passed.append(send(relay.at[n, side], final.at[n, side], at_y(1 - 2 * side)))

    for n, off in enumerate(offsets):
        if n == 3:
            far_top.wait_recv()
            far_low.wait_recv()
            gates.extend(
                send(gate_out_hbm.at[xmod(d)], near_gate.at[d], at_x(d)) for d in range(1, XS)
            )
            product_x.extend(
                send(stage.at[0, xmod(d)], crossed.at[0, :, x], at_x(d)) for d in range(1, XS)
            )
            shared.append(send(g_ring.at[xmod(2)], g_other.at[3], sibling))
        shared[n].wait_recv()

        @pl.loop(0, g_ring.shape[2] // CHUNK)
        def _(i, n=n, off=off):
            at = pl.ds(pl.multiple_of(i * CHUNK, CHUNK), CHUNK)
            total = dot(w_mine[...].reshape(wide), g_ring[xmod(off), :, at])
            total = total + dot(w_other[...].reshape(wide), g_other[n, :, at])
            total = total.reshape(YS, deep, CHUNK)
            own[n, :, at] = total[0]
            hold[n, 0, :, at] = total[1, :half_w]
            hold[n, 1, :, at] = total[3, half_w:]
            part[n, 0, 0, :, at] = total[2, :half_w].astype(BF)
            part[n, 0, 1, :, at] = total[1, half_w:].astype(BF)
            part[n, 1, 0, :, at] = total[2, half_w:].astype(BF)
            part[n, 1, 1, :, at] = total[3, :half_w].astype(BF)

        parts.append([send(part.at[n, side], inbox.at[n, side], at_y(1 - 2 * side)) for side in range(2)])

    arrivals = []
    homes = []

    def total_up(n):
        for copy in passed[2 * n : 2 * n + 2]:
            copy.wait_recv()
        d = -offsets[n] % XS
        if d:
            gates[d - 1].wait_recv()
        else:
            gate_load.wait()
        upper = own[n, :half_w] + final[n, 0].astype(jnp.float32) + inbox[n, 1, 1].astype(jnp.float32)
        lower = own[n, half_w:] + final[n, 1].astype(jnp.float32) + inbox[n, 0, 1].astype(jnp.float32)
        back = jnp.concatenate([upper, lower], 0)
        result = back * near_gate[d].astype(jnp.float32)
        gated[n] = result.astype(BF).reshape(gated.shape[1:])
        gated_in[z, n] = gated[n, z]
        if n:
            some = pl.ds(0, 2) if n == 1 else pl.ds(n, 1)
            for d in range(1, ZS):
                arrivals.append(send(gated.at[some, zmod(d)], gated_in.at[z, some], at_z(d)))
        back_bf[n] = back.astype(BF)

    inner = own.shape[2]
    rows = gated_in.shape[0] * gated_in.shape[1] * gated_in.shape[2]
    into, twist, across = (in_hi, in_lo), (cos, sin), (ac_hi, ac_lo)

    def pair_block(i):
        return lambda at: pair_in[i, :, :, :, at].reshape(rows, CHUNK)

    early = len(copies)
    pass_on(0)
    pass_on(1)
    pass_on(2)
    total_up(0)
    pass_on(3)
    total_up(1)
    for copy in product_x:
        copy.wait_recv()
    product_over_z(0, XS // 2)
    total_up(2)
    filters_over_x()
    total_up(3)
    product_over_z(XS // 2, XS // 2)
    for copy in table_loads:
        copy.wait()
    for copy in filters_x:
        copy.wait_recv()
    forward(pair_block(1), into, twist, fourth, across, y_ref, z_ref, spec_f)
    stays = [load(back_bf.at[0], home_out.at[x])]
    for n, off in enumerate(offsets):
        if n:
            homes.append(send(back_bf.at[n], home_out.at[x], at_x(off)))
    flush(early)

    def gated_block(at):
        blocks = []
        for i in range(XS):
            e = lax.rem(i - x + XS, XS)
            blocks.append(gated_in[:, 2 * e - e // 2 - 4 * (e // 3), :, at])
        return jnp.stack(blocks, 1).reshape(rows, CHUNK)

    for copy in arrivals:
        copy.wait_recv()
    forward(
        gated_block,
        into, twist, fourth, across, y_ref, z_ref, spec_g,
    )

    width = gated_in.shape[2]
    lanes = skip_ref.shape[1]
    pick = lax.broadcasted_iota(jnp.int32, (width, lanes), 1) == z * width + lax.broadcasted_iota(
        jnp.int32, (width, lanes), 0
    )
    scale = jnp.sum(jnp.where(pick, skip_ref[pl.ds(x, 1), :], 0.0), axis=1, keepdims=True)
    gone = []
    turns = []

    def mixed_over_x():
        for copy in gone[0]:
            copy.wait_recv()
        turns.extend(
            send(landed.at[0, :, xmod(d)], mixed_out.at[x], at_x(d)) for d in range(1, XS)
        )
        stays.append(load(landed.at[0, :, x], mixed_out.at[x]))

    def filters_over_z(k):
        at = pl.ds((k - 1) * CHUNK, CHUNK)
        for copy in gone[k]:
            copy.wait_recv()
        turns.extend(
            send(landed.at[1, zmod(d), :, :, at], filters_out.at[:, z, :, at], at_z(d))
            for d in range(1, ZS)
        )
        stays.append(load(landed.at[1, z, :, :, at], filters_out.at[:, z, :, at]))

    def leave(which, start, size):
        if start == 0:
            combine(spec_g, (spec_f, spec_p)[which], z_ref)
            columns(z_ref, across, spec_r)
            unfold(spec_r, twist, fourth, u_ref)
        for c in range(start, start + size, CHUNK):
            at = pl.ds(c, CHUNK)
            u = u_ref[:, at]
            out = dot(of_hi[...], u) + dot(of_lo[...], u)
            if which == 0:
                out = out.reshape(ZS * XS, width, CHUNK)
                out = out + scale * gated_block(at).reshape(out.shape).astype(jnp.float32)
            leaving[which, :, :, :, at] = out.astype(BF).reshape(ZS, XS, width, CHUNK)
        at = pl.ds(start, size)
        if which == 0:
            gone.append(
                [send(leaving.at[0, zmod(d)], landed.at[0, z], at_z(d)) for d in range(1, ZS)]
            )
            landed[0, z] = leaving[0, z]
        else:
            gone.append(
                [
                    send(leaving.at[1, :, xmod(d), :, at], landed.at[1, :, x, :, at], at_x(d))
                    for d in range(1, XS)
                ]
            )
            landed[1, :, x, :, at] = leaving[1, :, x, :, at]

    leave(0, 0, inner)
    for copy in product_z:
        copy.wait_recv()
    forward(pair_block(0), into, twist, fourth, across, y_ref, z_ref, spec_p)
    middle = len(copies)
    leave(1, 0, CHUNK)
    leave(1, CHUNK, CHUNK)
    filters_over_z(1)
    filters_over_z(2)
    mixed_over_x()
    flush(middle)
    for copy in stays:
        copy.wait()
    for copy in homes + turns:
        copy.wait_recv()
    flush(len(copies))
    assert len(copies) == send_sems.shape[0]
    assert len(loads) == local_sems.shape[0]


def layer(grad_out, out_weight, gate_in, gate_out, values, filters, skip_scale):
    rows, inner = gate_in.shape
    deep, wide = out_weight.shape
    width = rows // (ZS * XS)
    into, out_of, cos, sin, across, fourth = make_tables(ZS * XS, width, inner)
    tables = (*into, *out_of, cos, sin, *across, fourth)
    spec_rows = cos.shape[0]
    split = (XS, ZS, width, inner)
    count = 128

    def vmem(shape, dtype=BF):
        return pltpu.VMEM(shape, dtype)

    spec = vmem((4, spec_rows, inner // 2), jnp.float32)
    return pl.pallas_call(
        layer_kernel,
        out_shape=[
            jax.ShapeDtypeStruct((XS, deep, inner), BF),
            jax.ShapeDtypeStruct(split, BF),
            jax.ShapeDtypeStruct(split, BF),
        ],
        in_specs=[pl.BlockSpec(memory_space=pl.ANY)] * 6
        + [VMEM]
        + [pl.BlockSpec(memory_space=pl.ANY)] * len(tables),
        out_specs=[pl.BlockSpec(memory_space=pl.ANY)] * 3,
        scratch_shapes=[
            vmem(split),
            vmem(split),
            vmem(split, jnp.float32),
            *[vmem(t.shape, t.dtype) for t in tables],
            vmem((ZS, deep, wide)),
            vmem((YS, deep, wide)),
            vmem((YS, deep, wide)),
            vmem(grad_out.shape),
            vmem((XS,) + grad_out.shape[::-1]),
            vmem((XS,) + grad_out.shape[::-1]),
            vmem((XS, deep, inner), jnp.float32),
            vmem((XS, 2, deep // 2, inner), jnp.float32),
            vmem((XS, 2, 2, deep // 2, inner)),
            vmem((XS, 2, 2, deep // 2, inner)),
            vmem((XS, 2, deep // 2, inner)),
            vmem((XS, 2, deep // 2, inner)),
            vmem((XS, deep, inner)),
            vmem((XS, deep, inner)),
            vmem((XS, ZS, width, inner)),
            vmem((ZS, XS, width, inner)),
            vmem((2,) + split),
            vmem((2, ZS, XS, width, inner)),
            vmem((2, ZS, XS, width, inner)),
            vmem((2 * spec_rows, inner), jnp.float32),
            vmem((4, spec_rows, inner // 2)),
            vmem((2 * spec_rows, inner)),
            spec,
            spec,
            spec,
            spec,
            vmem((2, ZS, XS, width, inner)),
            vmem((2, ZS, XS, width, inner)),
            pltpu.SemaphoreType.DMA((count,)),
            pltpu.SemaphoreType.DMA((count,)),
            pltpu.SemaphoreType.DMA((19,)),
        ],
        compiler_params=pltpu.CompilerParams(
            collective_id=0, has_side_effects=True, vmem_limit_bytes=58 * 1024 * 1024
        ),
        cost_estimate=pl.CostEstimate(flops=10 * 10**9, bytes_accessed=20 * 10**6, transcendentals=0),
    )(
        out_weight,
        grad_out,
        gate_in.reshape(split),
        values.reshape(split),
        gate_out.reshape(XS, deep, inner),
        filters.reshape(split),
        skip_scale.reshape(XS, deep),
        *tables,
    )


def finish_kernel(*refs):
    sources, results = refs[:6], refs[6:10]
    held, done, sems = refs[10:16], refs[16:20], refs[20]
    mixed, values, gate_in, home, conv_out, filters = held
    order = (3, 4, 0, 1, 2, 5)
    loads = {n: pltpu.make_async_copy(sources[n], held[n], sems.at[n]) for n in order}
    for n in order:
        loads[n].start()
    stores = []

    def close(n, needs, left, right):
        for need in needs:
            loads[need].wait()

        @pl.loop(0, left.shape[0] // 64)
        def _(i):
            at = pl.ds(pl.multiple_of(i * 64, 64), 64)
            value = left[at, :].astype(jnp.float32)
            if right is not None:
                value = value * right[at, :].astype(jnp.float32)
            done[n][at, :] = value.astype(done[n].dtype)

        stores.append(pltpu.make_async_copy(done[n], results[n], sems.at[6 + n]))
        stores[-1].start()

    close(2, (3, 4), home, conv_out)
    close(0, (0, 1), mixed, values)
    close(1, (2,), mixed, gate_in)
    close(3, (5,), filters, None)
    for store in stores:
        store.wait()


def finish(*arrays):
    shape = arrays[0].shape
    outs = [jax.ShapeDtypeStruct(shape, t) for t in (BF, BF, BF, jnp.float32)]
    hbm = pl.BlockSpec(memory_space=pl.ANY)
    return tuple(
        pl.pallas_call(
            finish_kernel,
            out_shape=outs,
            in_specs=[hbm] * 6,
            out_specs=[hbm] * 4,
            scratch_shapes=[pltpu.VMEM(shape, BF)] * 6
            + [pltpu.VMEM(o.shape, o.dtype) for o in outs]
            + [pltpu.SemaphoreType.DMA((10,))],
            compiler_params=pltpu.CompilerParams(vmem_limit_bytes=62 * 1024 * 1024),
            cost_estimate=pl.CostEstimate(flops=10**6, bytes_accessed=6 * 10**6, transcendentals=0),
        )(*arrays)
    )


def shards(grad_out, out_weight, gate_in, gate_out, values, conv_out, filters, skip_scale):
    rows, inner = gate_in.shape
    home, grad_filters, mixed = layer(
        grad_out, out_weight, gate_in, gate_out, values, filters, skip_scale
    )

    return finish(
        mixed.reshape(rows, inner), values, gate_in, home.reshape(rows, inner), conv_out,
        grad_filters.reshape(rows, inner),
    )


def solution(mesh):
    placed = (
        P("seq", "ch"),
        P("seq", "ch"),
        P("ch", "seq"),
        P("ch", "seq"),
        P("ch", "seq"),
        P("ch", "seq"),
        P("ch", "seq"),
        P("ch"),
    )
    return jax.shard_map(
        shards,
        mesh=mesh,
        in_specs=placed,
        out_specs=(P("ch", "seq"), P("ch", "seq"), P("ch", "seq"), P("ch", "seq")),
        check_vma=False,
    )
```
